128 devices in a mesh: gx: 8 (over z, core), gy: 4 (over y), gz: 4 (over x).
Axes of the slice: x: 4, y: 4, z: 4, core: 2. Of those that a mesh axis runs over, the one named last changes fastest.
Arguments:
- features: bfloat16 [256, 64, 64, 128], P('gx', 'gy', 'gz'), may hold values from -6 to 6
- occupancy: int32 [32, 8, 8], P('gx', 'gy', 'gz'), may hold values from 0 to 1, as said below
- weight: bfloat16 [3, 3, 3, 128, 128], replicated, may hold values from -0.109375 to 0.109375
- cotangent: bfloat16 [256, 64, 64, 128], P('gx', 'gy', 'gz'), may hold values from -6 to 6
Outputs:
- outputs: bfloat16 [256, 64, 64, 128], P('gx', 'gy', 'gz')
- input_grad: bfloat16 [256, 64, 64, 128], P('gx', 'gy', 'gz')
- weight_grad: float32 [3, 3, 3, 128, 128], replicated
The draws below stay inside these ranges and needn't reach their ends.
Inputs may be any that keep to these rules, and one draw needn't show every extreme that they name: `occupancy`: in every plane of devices that share a gx index, the regions of the 16 devices hold 16, 16, 12, 12, 10, 10, 8, 8, 8, 6, 6, 4, 4, 3, 3 and 2 occupied bricks, in an order drawn from the seed; so each plane holds exactly 128 occupied bricks and some device holds 16. Which bricks of a region are occupied is drawn from the seed.
All inputs are finite; a program needn't handle non-finite values.
Results may differ from the reference program's by a relative error of at most 0.001.
Values may be sent and summed in bfloat16 or wider, within the bound.
No kernel may reach another device: no remote copies, remote signals or barrier semaphores. Data moves between devices by JAX's collectives and lax.ppermute only.
A program may use at most 128 MiB of HBM per device.

```python
import math
import jax
import jax.numpy as jnp
from jax import lax

C = 128
E = 8
BX = 4
BY = 2
BZ = 2
NBX = 32
NBY = 8
NBZ = 8
NX = 256
NY = 64
NZ = 64
OCCUPIED = 1024


def draw_occupancy(key, part):
    key = jax.random.fold_in(key, 11)
    planes = NBX // BX
    count_y = NBY // BY
    count_z = NBZ // BZ
    members = count_y * count_z
    region_slots = BX * BY * BZ
    pattern = jnp.array([16, 16, 12, 12, 10, 10, 8, 8, 8, 6, 6, 4, 4, 3, 3, 2], jnp.int32)
    key_loads, key_slots = jax.random.split(key)
    orders = jax.vmap(lambda sub: jax.random.permutation(sub, members))(jax.random.split(key_loads, planes))
    loads = pattern[orders]
    slot_order = jax.vmap(lambda sub: jax.random.permutation(sub, region_slots))(jax.random.split(key_slots, planes * members))
    slot_order = slot_order.reshape(planes, members, region_slots)
    filled = (slot_order < loads[:, :, None]).astype(jnp.int32)
    filled = filled.reshape(planes, count_y, count_z, BX, BY, BZ)
    return jnp.transpose(filled, (0, 3, 1, 4, 2, 5)).reshape(NBX, NBY, NBZ)


def level_of(own_key, shape, cuts, least, top_value):
    level = 1.0
    for dim, parts in cuts:
        heights = jax.random.uniform(jax.random.fold_in(jax.random.fold_in(own_key, 6), dim), (parts,), jnp.float32, least / len(cuts), top_value / len(cuts))
        level = level * jnp.repeat(jnp.exp(heights), shape[dim] // parts).reshape((-1,) + (1,) * (len(shape) - 1 - dim))
    return level


def noise(key, dims, spread, reach, shards=(), dtype=jnp.bfloat16):
    values = jax.random.normal(key, dims, jnp.float32) * spread
    if len(shards) > 0:
        values = level_of(key, dims, shards, -0.22, 0.18) * values
    return jnp.clip(values, min=-reach, max=reach).astype(dtype)


def setup_inputs(seed: int = 0) -> dict:
    seeds = jax.random.split(jax.random.key(seed), 5)
    return {
        "features": noise(seeds[0], (NX, NY, NZ, C), 1.0, 6.0, ((0, 8), (1, 4), (2, 4))),
        "occupancy": draw_occupancy(jax.random.fold_in(seeds[4], 71), 0),
        "weight": noise(seeds[2], (3, 3, 3, C, C), (27 * C) ** -0.5, 0.109375),
        "cotangent": noise(seeds[3], (NX, NY, NZ, C), 1.0, 6.0, ((0, 8), (1, 4), (2, 4))),
    }


def conv_valid(field, kernel):
    return lax.conv_general_dilated(field, kernel, (1, 1, 1), 'VALID', dimension_numbers=('NDHWC', 'DHWIO', 'NDHWC'), preferred_element_type=jnp.float32)

def flip_kernel(weight):
    return jnp.transpose(weight[::-1, ::-1, ::-1], (0, 1, 2, 4, 3))

def weight_terms(x_rims, g_inner):
    extent_x, extent_y, extent_z = g_inner.shape[1:4]
    channels = g_inner.shape[-1]
    flat_g = g_inner.reshape(-1, channels)
    terms = []
    for tap in range(27):
        along_x, along_y, along_z = (tap // 9, tap // 3 % 3, tap % 3)
        piece = x_rims[:, along_x:along_x + extent_x, along_y:along_y + extent_y, along_z:along_z + extent_z, :].reshape(-1, channels)
        terms.append(lax.dot_general(piece, flat_g, (((0,), (0,)), ((), ())), preferred_element_type=jnp.float32))
    return jnp.stack(terms).reshape(3, 3, 3, channels, channels)

def brick_work(rims, weight, flipped):
    x_rims = rims[:, 0]
    g_rims = rims[:, 1]
    produced = conv_valid(x_rims, weight).astype(jnp.bfloat16)
    gradient = conv_valid(g_rims, flipped).astype(jnp.bfloat16)
    partial_terms = weight_terms(x_rims, g_rims[:, 1:-1, 1:-1, 1:-1])
    return (produced, gradient, partial_terms)

def cut_rims(padded, index, count_y, count_z, edge):
    along_x = index // (count_y * count_z)
    along_y = index // count_z % count_y
    along_z = index % count_z
    zero_index = jnp.int32(0)
    start = (zero_index, (along_x * edge).astype(jnp.int32), (along_y * edge).astype(jnp.int32), (along_z * edge).astype(jnp.int32), zero_index)
    return lax.dynamic_slice(padded, start, (2, edge + 2, edge + 2, edge + 2, padded.shape[-1]))

def to_region(bricks, count_x, count_y, count_z, edge):
    channels = bricks.shape[-1]
    shaped = bricks.reshape(count_x, count_y, count_z, edge, edge, edge, channels)
    return jnp.transpose(shaped, (0, 3, 1, 4, 2, 5, 6)).reshape(count_x * edge, count_y * edge, count_z * edge, channels)

def reference(features, occupancy, weight, cotangent):
    count_x, count_y, count_z = occupancy.shape
    cell_mask = jnp.broadcast_to(occupancy[:, None, :, None, :, None], (count_x, E, count_y, E, count_z, E)).reshape(NX, NY, NZ).astype(jnp.bfloat16)[..., None]
    stacked = jnp.stack([features * cell_mask, cotangent * cell_mask])
    padded = jnp.pad(stacked, ((0, 0), (1, 1), (1, 1), (1, 1), (0, 0)))
    brick_ids = jnp.nonzero(occupancy.reshape(-1), size=OCCUPIED)[0].astype(jnp.int32)
    flipped = flip_kernel(weight)

    def visit(carry, group):
        rims = jax.vmap(lambda index: cut_rims(padded, index, count_y, count_z, E))(group)
        produced, gradient, partial_terms = brick_work(rims, weight, flipped)
        return (carry + partial_terms, (produced, gradient))
    start_total = jnp.zeros((3, 3, 3, C, C), jnp.float32)
    total, (produced, gradient) = lax.scan(visit, start_total, brick_ids.reshape(-1, 8))
    produced = produced.reshape(OCCUPIED, E, E, E, C)
    gradient = gradient.reshape(OCCUPIED, E, E, E, C)
    empty = jnp.zeros((count_x * count_y * count_z, E, E, E, C), jnp.bfloat16)
    outputs = to_region(empty.at[brick_ids].set(produced), count_x, count_y, count_z, E)
    input_grad = to_region(empty.at[brick_ids].set(gradient), count_x, count_y, count_z, E)
    weight_grad = total * (1.0 / math.sqrt(OCCUPIED * E ** 3))
    return (outputs, input_grad, weight_grad)
```

```python
import math

import jax
import jax.numpy as jnp
from jax import lax
from jax.experimental import pallas as pl
from jax.experimental.pallas import tpu as pltpu
from jax.sharding import PartitionSpec as P

SHARE = 8
X, Y, Z, C = 32, 16, 16, 128
E = 8
ROWS = Y * Z
GROUP = 4
TAPS = 9 * C
WIDE = 3 * C
PAD_ROWS = 3584
F32 = jnp.float32
BF16 = jnp.bfloat16
VMEM = pl.BlockSpec(memory_space=pltpu.VMEM)
SMEM = pl.BlockSpec(memory_space=pltpu.SMEM)


def params():
    return pltpu.CompilerParams(vmem_limit_bytes=48 * 1024 * 1024)


def brick_flags(occ_ref, brick):
    low_z = lax.broadcasted_iota(jnp.int32, (E, Z, C), 1) < E
    halves = []
    for j in range(2):
        flag = jnp.where(low_z, occ_ref[brick, j, 0], occ_ref[brick, j, 1])
        halves.append(flag)
    return jnp.concatenate(halves, axis=0) == 1


def prepare_kernel(occ_ref, f_ref, c_ref, s_ref, zlo_ref, zhi_ref, ylo_ref, yhi_ref):
    keep = brick_flags(occ_ref, pl.program_id(0))
    for part, ref in enumerate((f_ref, c_ref)):
        value = jnp.where(keep[None], ref[...].astype(F32), 0.0).astype(BF16)
        s_ref[part] = value
        zlo_ref[part] = value[:, :, 0, :]
        zhi_ref[part] = value[:, :, Z - 1, :]
        ylo_ref[part] = value[:, 0]
        yhi_ref[part] = value[:, Y - 1]


def prepare(occupancy, features, cotangent):
    face = jax.ShapeDtypeStruct((2, X, Z, C), BF16)
    face_spec = pl.BlockSpec((2, E, Z, C), lambda i: (0, i, 0, 0))
    block = pl.BlockSpec((E, Y, Z, C), lambda i: (i, 0, 0, 0))
    return pl.pallas_call(
        prepare_kernel,
        grid=(X // E,),
        in_specs=[SMEM, block, block],
        out_specs=[pl.BlockSpec((2, E, Y, Z, C), lambda i: (0, i, 0, 0, 0))] + [face_spec] * 4,
        out_shape=[jax.ShapeDtypeStruct((2, X, Y, Z, C), BF16)] + [face] * 4,
        compiler_params=params(),
        cost_estimate=pl.CostEstimate(flops=1000000, bytes_accessed=9 << 20, transcendentals=0),
    )(occupancy, features, cotangent)


def put_slab(scratch, slot, center, ylo, yhi, zlo, zhi):
    whole = jnp.concatenate([ylo[None], center, yhi[None]], axis=0)
    scratch[1, slot] = whole
    flat = whole.astype(F32).reshape((Y + 2) * Z, C)
    at = lax.broadcasted_iota(jnp.int32, (Y + 2, Z, C), 1)
    back = pltpu.roll(flat, 1, 0).reshape(Y + 2, Z, C)
    ahead = pltpu.roll(flat, (Y + 2) * Z - 1, 0).reshape(Y + 2, Z, C)
    low = zlo.astype(F32)[: Y + 2, None, :]
    high = zhi.astype(F32)[: Y + 2, None, :]
    scratch[0, slot] = jnp.where(at == 0, low, back).astype(BF16)
    scratch[2, slot] = jnp.where(at == Z - 1, high, ahead).astype(BF16)


def patches(scratch, slots):
    pieces = []
    for ty in range(3):
        for tz in range(3):
            pieces.append(scratch[tz, :slots, ty : ty + Y].reshape(slots * ROWS, C))
    return jnp.concatenate(pieces, axis=1)


def load_own(scratch, first, s_ref, ylo_ref, yhi_ref, zlo_ref, zhi_ref):
    for slot in range(GROUP):
        x = first + slot
        put_slab(scratch, slot, s_ref[0, x], ylo_ref[0, x], yhi_ref[0, x], zlo_ref[0, x], zhi_ref[0, x])


def load_far(scratch, slot, far_ref):
    rims = far_ref[0, Y + 2 :].reshape(-1, C)
    put_slab(scratch, slot, far_ref[0, :Y], far_ref[0, Y], far_ref[0, Y + 1], rims[:24], rims[24:])


def kernel_grad_kernel(s_ref, g_ref, ylo_ref, yhi_ref, zlo_ref, zhi_ref, far_lo, far_hi, o_ref, scratch, total, around):
    zero = jnp.zeros((Y, Z, C), BF16)
    load_far(scratch, 0, far_lo)
    load_far(scratch, 1, far_hi)
    none = jnp.zeros((ROWS, C), BF16)
    first = jnp.concatenate([g_ref[0, 0].reshape(ROWS, C), none], axis=0)
    last = jnp.concatenate([none, g_ref[0, X - 1].reshape(ROWS, C)], axis=0)
    beside = jnp.concatenate([first, jnp.zeros_like(first), last], axis=1)
    contract = (((0,), (0,)), ((), ()))
    total[...] = lax.dot_general(patches(scratch, 2), beside, contract, preferred_element_type=F32)
    around[0] = zero
    around[X + 1] = zero
    around[1 : X + 1] = g_ref[0]

    def step(i, carry):
        x = i * GROUP
        load_own(scratch, x, s_ref, ylo_ref, yhi_ref, zlo_ref, zhi_ref)
        beside = jnp.concatenate(
            [around[pl.ds(x + 2 - tx, GROUP)].reshape(GROUP * ROWS, C) for tx in range(3)], axis=1
        )
        total[...] += lax.dot_general(patches(scratch, GROUP), beside, contract, preferred_element_type=F32)
        return carry

    lax.fori_loop(0, X // GROUP, step, 0)
    scale = 1.0 / math.sqrt(SHARE * 128 * E**3)
    for tx in range(3):
        o_ref[pl.ds(tx * TAPS, TAPS)] = total[:, tx * C : (tx + 1) * C] * scale
    o_ref[pl.ds(3 * TAPS, PAD_ROWS - 3 * TAPS)] = jnp.zeros((PAD_ROWS - 3 * TAPS, C), F32)


def whole_part(shape, part):
    zeros = (0,) * (len(shape) - 1)
    return pl.BlockSpec((1,) + tuple(shape[1:]), lambda i: (part,) + zeros)


def kernel_grad(stacked, ylo, yhi, zlo, zhi, far_lo, far_hi):
    operands = (ylo, yhi, zlo, zhi, far_lo, far_hi)
    return pl.pallas_call(
        kernel_grad_kernel,
        grid=(1,),
        in_specs=[whole_part(stacked.shape, 0), whole_part(stacked.shape, 1)]
        + [whole_part(a.shape, 0) for a in operands],
        out_specs=VMEM,
        out_shape=jax.ShapeDtypeStruct((PAD_ROWS, C), F32),
        scratch_shapes=[
            pltpu.VMEM((3, GROUP, Y + 2, Z, C), BF16),
            pltpu.VMEM((TAPS, WIDE), F32),
            pltpu.VMEM((X + 2, Y, Z, C), BF16),
        ],
        compiler_params=params(),
        cost_estimate=pl.CostEstimate(
            flops=2 * 27 * C * C * X * ROWS, bytes_accessed=8 << 20, transcendentals=0
        ),
    )(stacked, stacked, *operands)


def conv_kernel(
    occ_ref, s_ref, ylo_ref, yhi_ref, zlo_ref, zhi_ref, far_lo, far_hi, w_ref, o_ref, scratch, near, next_
):
    def finish(x, total):
        keep = brick_flags(occ_ref, x // E)
        o_ref[x] = jnp.where(keep, total.reshape(Y, Z, C), 0.0).astype(BF16)

    load_far(scratch, 0, far_lo)
    near[...] = jnp.zeros((ROWS, C), F32)
    next_[...] = jnp.dot(patches(scratch, 1), w_ref[:, :C], preferred_element_type=F32)

    def step(i, carry):
        x = i * GROUP
        load_own(scratch, x, s_ref, ylo_ref, yhi_ref, zlo_ref, zhi_ref)
        made = jnp.dot(patches(scratch, GROUP), w_ref[...], preferred_element_type=F32)

        def term(slot, tx):
            return made[slot * ROWS : (slot + 1) * ROWS, tx * C : (tx + 1) * C]

        before = near[...] + term(0, 2)

        @pl.when(i > 0)
        def _():
            finish(x - 1, before)

        finish(x, next_[...] + term(0, 1) + term(1, 2))
        for slot in range(1, GROUP - 1):
            finish(x + slot, term(slot - 1, 0) + term(slot, 1) + term(slot + 1, 2))
        near[...] = term(GROUP - 2, 0) + term(GROUP - 1, 1)
        next_[...] = term(GROUP - 1, 0)
        return carry

    lax.fori_loop(0, X // GROUP, step, 0)
    load_far(scratch, 0, far_hi)
    finish(X - 1, near[...] + jnp.dot(patches(scratch, 1), w_ref[:, 2 * C :], preferred_element_type=F32))


def conv(part, occupancy, stacked, ylo, yhi, zlo, zhi, far_lo, far_hi, weight):
    operands = (stacked, ylo, yhi, zlo, zhi, far_lo, far_hi)
    return pl.pallas_call(
        conv_kernel,
        grid=(1,),
        in_specs=[SMEM] + [whole_part(a.shape, part) for a in operands] + [VMEM],
        out_specs=VMEM,
        out_shape=jax.ShapeDtypeStruct((X, Y, Z, C), BF16),
        scratch_shapes=[
            pltpu.VMEM((3, GROUP, Y + 2, Z, C), BF16),
            pltpu.VMEM((ROWS, C), F32),
            pltpu.VMEM((ROWS, C), F32),
        ],
        compiler_params=params(),
        cost_estimate=pl.CostEstimate(
            flops=2 * 27 * C * C * X * ROWS, bytes_accessed=6 << 20, transcendentals=0
        ),
    )(occupancy, *operands, weight)


def shift_open(value, axis, step):
    count = lax.axis_size(axis)
    return lax.ppermute(value, axis, [(i, i + step) for i in range(count) if 0 <= i + step < count])


def rotate(value, axis, pairs):
    return lax.ppermute(value, axis, pairs)


def chip_ring(axis, step):
    if axis == "gx":
        return [(2 * z + c, 2 * ((z + step) % 4) + c) for z in range(4) for c in range(2)]
    return [(i, (i + step) % 4) for i in range(4)]


def position(axis):
    place = lax.axis_index(axis)
    return place // 2 if axis == "gx" else place


def piece(value, index, rows):
    return lax.dynamic_slice_in_dim(value, index * rows, rows, axis=0)


def scatter_ring(value, axis):
    rows = value.shape[0] // 4
    me = position(axis)
    own = piece(value, me, rows)
    for step in (1, 3, 2):
        own = own + lax.ppermute(piece(value, (me + step) % 4, rows), axis, chip_ring(axis, step))
    return own


def gather_ring(value, axis):
    rows = value.shape[0]
    me = position(axis)
    whole = jnp.zeros((4 * rows,) + value.shape[1:], value.dtype)
    whole = lax.dynamic_update_slice_in_dim(whole, value, me * rows, axis=0)
    for step in (1, 3, 2):
        came = lax.ppermute(value, axis, chip_ring(axis, step))
        whole = lax.dynamic_update_slice_in_dim(whole, came, (me - step) % 4 * rows, axis=0)
    return whole


def body(features, occupancy, weight, cotangent):
    stacked, zlo, zhi, ylo, yhi = prepare(occupancy, features, cotangent)
    near_zlo = shift_open(zhi, "gz", 1)
    near_zhi = shift_open(zlo, "gz", -1)
    near_ylo = shift_open(yhi, "gy", 1)
    near_yhi = shift_open(ylo, "gy", -1)
    edge_lo = jnp.stack([near_zlo[:, :, 0], near_zhi[:, :, 0]], axis=1)
    edge_hi = jnp.stack([near_zlo[:, :, Y - 1], near_zhi[:, :, Y - 1]], axis=1)
    edge_from_lo = shift_open(edge_hi, "gy", 1)
    edge_from_hi = shift_open(edge_lo, "gy", -1)
    blank = jnp.zeros((2, X, 24 - Y - 2, C), BF16)

    def column(side, own):
        return jnp.concatenate(
            [edge_from_lo[:, side, :, None], own, edge_from_hi[:, side, :, None], blank], axis=2
        )

    col_lo = column(0, near_zlo)
    col_hi = column(1, near_zhi)

    def message(x):
        columns = jnp.concatenate([col_lo[:, x], col_hi[:, x]], axis=1).reshape(2, 3, Z, C)
        return jnp.concatenate([stacked[:, x], near_ylo[:, x, None], near_yhi[:, x, None], columns], axis=1)

    far_lo = shift_open(message(X - 1), "gx", 1)
    far_hi = shift_open(message(0), "gx", -1)
    rims = (near_ylo, near_yhi, col_lo, col_hi, far_lo, far_hi)

    partial = kernel_grad(stacked, *rims)

    def arrange(kernel):
        return jnp.transpose(kernel, (1, 2, 3, 0, 4)).reshape(TAPS, WIDE)

    forward = arrange(weight)
    flipped = arrange(jnp.transpose(weight[::-1, ::-1, ::-1], (0, 1, 2, 4, 3)))

    core = lax.axis_index("gx") % 2
    half = PAD_ROWS // 2
    swap = [(i, i ^ 1) for i in range(8)]
    mine = piece(partial, core, half) + lax.ppermute(piece(partial, 1 - core, half), "gx", swap)
    mine = scatter_ring(mine, "gx")
    mine = scatter_ring(mine, "gy")
    one, three, two = (lax.ppermute(mine, "gz", chip_ring("gz", step)) for step in (1, 3, 2))
    summed = (mine + two) + (one + three)
    whole = gather_ring(summed, "gy")
    whole = gather_ring(whole, "gx")
    other = lax.ppermute(whole, "gx", swap)
    full = jnp.concatenate([jnp.where(core == 0, whole, other), jnp.where(core == 0, other, whole)], axis=0)
    weight_grad = full[: 27 * C].reshape(3, 3, 3, C, C)

    outputs = conv(0, occupancy, stacked, *rims, forward)
    input_grad = conv(1, occupancy, stacked, *rims, flipped)
    return (outputs, input_grad, weight_grad)


def solution(mesh):
    placed = (P("gx", "gy", "gz", None), P("gx", "gy", "gz"), P(), P("gx", "gy", "gz", None))
    return jax.shard_map(
        body,
        mesh=mesh,
        in_specs=placed,
        out_specs=(P("gx", "gy", "gz", None), P("gx", "gy", "gz", None), P()),
        check_vma=False,
    )
```

```python
import math

import jax
import jax.numpy as jnp
from jax import lax
from jax.experimental import pallas as pl
from jax.experimental.pallas import tpu as pltpu
from jax.sharding import PartitionSpec as P

SHARE = 8
X, Y, Z, C = 32, 16, 16, 128
E = 8
ROWS = Y * Z
GROUP = 4
PIECE = 8
TAPS = 9 * C
WIDE = 3 * C
HALF = 14
F32 = jnp.float32
BF16 = jnp.bfloat16
VMEM = pl.BlockSpec(memory_space=pltpu.VMEM)
SMEM = pl.BlockSpec(memory_space=pltpu.SMEM)
ANY = pl.BlockSpec(memory_space=pl.ANY)
DEPTH_FIRST = (((0,), (0,)), ((), ()))


def shape(dims, dtype):
    return jax.ShapeDtypeStruct(dims, dtype)


def params(mebibytes=24):
    return pltpu.CompilerParams(vmem_limit_bytes=mebibytes * 1024 * 1024)


def cost(slabs, moved):
    return pl.CostEstimate(flops=2 * 27 * C * C * slabs * ROWS, bytes_accessed=moved, transcendentals=0)


def whole_part(dims, part):
    zeros = (0,) * (len(dims) - 1)
    return pl.BlockSpec((1,) + tuple(dims[1:]), lambda i: (part,) + zeros)


def slab_part(dims, part, count, at):
    zeros = (0,) * (len(dims) - 2)
    return pl.BlockSpec((1, count) + tuple(dims[2:]), lambda i: (part, at) + zeros)


def brick_flags(occ_ref, brick):
    low_z = lax.broadcasted_iota(jnp.int32, (E, Z, C), 1) < E
    halves = [jnp.where(low_z, occ_ref[brick, j, 0], occ_ref[brick, j, 1]) for j in range(2)]
    return jnp.concatenate(halves, axis=0) == 1


def prepare_kernel(occ_ref, f_ref, c_ref, s_ref, zlo_ref, zhi_ref, ylo_ref, yhi_ref):
    keep = brick_flags(occ_ref, pl.program_id(0))
    for part, ref in enumerate((f_ref, c_ref)):
        value = jnp.where(keep[None], ref[...].astype(F32), 0.0).astype(BF16)
        s_ref[part] = value
        zlo_ref[part] = value[:, :, 0, :]
        zhi_ref[part] = value[:, :, Z - 1, :]
        ylo_ref[part] = value[:, 0]
        yhi_ref[part] = value[:, Y - 1]


def prepare(occupancy, features, cotangent):
    face = shape((2, X, Z, C), BF16)
    face_spec = pl.BlockSpec((2, E, Z, C), lambda i: (0, i, 0, 0))
    block = pl.BlockSpec((E, Y, Z, C), lambda i: (i, 0, 0, 0))
    return pl.pallas_call(
        prepare_kernel,
        grid=(X // E,),
        in_specs=[SMEM, block, block],
        out_specs=[pl.BlockSpec((2, E, Y, Z, C), lambda i: (0, i, 0, 0, 0))] + [face_spec] * 4,
        out_shape=[shape((2, X, Y, Z, C), BF16)] + [face] * 4,
        compiler_params=params(),
        cost_estimate=pl.CostEstimate(flops=1000000, bytes_accessed=9 << 20, transcendentals=0),
    )(occupancy, features, cotangent)


def moved_z(whole, step):
    rows = whole.shape[0] * whole.shape[1]
    flat = whole.reshape(rows, C)
    return pltpu.roll(flat, -step % rows, 0).reshape(whole.shape)


def put_slab(scratch, slot, center, ylo, yhi, zlo, zhi):
    whole = jnp.concatenate([ylo[None], center, yhi[None]], axis=0)
    scratch[1, slot] = whole
    whole = whole.astype(F32)
    at = lax.broadcasted_iota(jnp.int32, (Y + 2, Z, C), 1)
    low = zlo.astype(F32)[: Y + 2, None, :]
    high = zhi.astype(F32)[: Y + 2, None, :]
    scratch[0, slot] = jnp.where(at == 0, low, moved_z(whole, -1)).astype(BF16)
    scratch[2, slot] = jnp.where(at == Z - 1, high, moved_z(whole, 1)).astype(BF16)


def put_own(scratch, slot, center):
    scratch[1, slot, 1 : Y + 1] = center
    whole = center.astype(F32)
    at = lax.broadcasted_iota(jnp.int32, (Y, Z, C), 1)
    scratch[0, slot, 1 : Y + 1] = jnp.where(at == 0, 0.0, moved_z(whole, -1)).astype(BF16)
    scratch[2, slot, 1 : Y + 1] = jnp.where(at == Z - 1, 0.0, moved_z(whole, 1)).astype(BF16)


def patches(scratch, first, slots):
    pieces = []
    for ty in range(3):
        for tz in range(3):
            pieces.append(scratch[tz, first : first + slots, ty : ty + Y].reshape(slots * ROWS, C))
    return jnp.concatenate(pieces, axis=1)


def put_far(scratch, slot, far_ref):
    rims = far_ref[0, Y + 2 :].reshape(-1, C)
    put_slab(scratch, slot, far_ref[0, :Y], far_ref[0, Y], far_ref[0, Y + 1], rims[:24], rims[24:])


def own_grad_kernel(first, groups, more, s_ref, g_ref, *refs):
    scratch, total = refs[-1], refs[-2]
    scratch[:, :, 0:1] = jnp.zeros((3, 2 * GROUP, 1, Z, C), BF16)
    scratch[:, :, Y + 1 :] = jnp.zeros((3, 2 * GROUP, 1, Z, C), BF16)
    none = jnp.zeros((ROWS, C), BF16)
    for i in range(groups):
        x = (first + i) * GROUP
        base = i % 2 * GROUP
        for slot in range(GROUP):
            put_own(scratch, base + slot, s_ref[0, x + slot])
        columns = []
        for tx in range(3):
            rows = []
            start, stop = x + 1 - tx, x + 1 - tx + GROUP
            if start < 0:
                rows.append(none)
            rows.append(g_ref[0, max(start, 0) : min(stop, X)].reshape(-1, C))
            if stop > X:
                rows.append(none)
            columns.append(jnp.concatenate(rows, axis=0))
        made = lax.dot_general(
            patches(scratch, base, GROUP), jnp.concatenate(columns, axis=1), DEPTH_FIRST, preferred_element_type=F32
        )
        if i > 0:
            total[...] += made
        elif more:
            total[...] = refs[0][...] + made
        else:
            total[...] = made


def own_grad(stacked, first, groups, before, tie):
    more = before is not None
    return pl.pallas_call(
        lambda *refs: own_grad_kernel(first, groups, more, *refs),
        grid=(1,),
        in_specs=[whole_part(stacked.shape, 0), whole_part(stacked.shape, 1)] + [VMEM] * more + [ANY],
        out_specs=VMEM,
        out_shape=shape((TAPS, WIDE), F32),
        scratch_shapes=[pltpu.VMEM((3, 2 * GROUP, Y + 2, Z, C), BF16)],
        compiler_params=params(),
        cost_estimate=cost(groups * GROUP, 8 << 20),
    )(stacked, stacked, *([before] if more else []), tie)


def rim_grad_kernel(
    own_ref, gzlo, gzhi, gylo, gyhi, nylo, nyhi, nzlo, nzhi, elo, ehi, far_lo, far_hi, g_first, g_last,
    keep_ref, send_ref, scratch, total,
):
    put_far(scratch, 0, far_lo)
    put_far(scratch, 1, far_hi)
    none = jnp.zeros((ROWS, C), BF16)
    first = jnp.concatenate([g_first[0].reshape(ROWS, C), none], axis=0)
    last = jnp.concatenate([none, g_last[0].reshape(ROWS, C)], axis=0)
    beside = jnp.concatenate([first, jnp.zeros_like(first), last], axis=1)
    total[...] = own_ref[...] + lax.dot_general(
        patches(scratch, 0, 2), beside, DEPTH_FIRST, preferred_element_type=F32
    )
    blank = jnp.zeros((1, Z, C), BF16)
    at = lax.broadcasted_iota(jnp.int32, (X, Z, C), 1)

    def add(row, stride, trio, face_ref):
        padded = jnp.concatenate([blank, face_ref[0], blank], axis=0)
        around = jnp.concatenate([padded[2 - tx : 2 - tx + X].reshape(X * Z, C) for tx in range(3)], axis=1)
        left = jnp.concatenate([a.astype(BF16).reshape(X * Z, C) for a in trio], axis=1)
        made = lax.dot_general(left, around, DEPTH_FIRST, preferred_element_type=F32)
        for k in range(3):
            start = (row + k * stride) * C
            total[start : start + C] += made[k * C : (k + 1) * C]

    for row, near, edges, face in ((0, nylo, elo, gylo), (6, nyhi, ehi, gyhi)):
        whole = near[0].astype(F32)
        low = edges[0, 0].astype(F32)[:, None, :]
        high = edges[0, 1].astype(F32)[:, None, :]
        before = jnp.where(at == 0, low, moved_z(whole, -1))
        after = jnp.where(at == Z - 1, high, moved_z(whole, 1))
        add(row, 1, (before, whole, after), face)
    for row, near, face in ((0, nzlo, gzlo), (2, nzhi, gzhi)):
        whole = near[0].astype(F32)
        before = jnp.where(at == 0, 0.0, moved_z(whole, -1))
        after = jnp.where(at == Z - 1, 0.0, moved_z(whole, 1))
        add(row, 3, (before, whole, after), face)

    scale = 1.0 / math.sqrt(SHARE * 128 * E**3)
    core = lax.axis_index("gx") % 2
    for mine in range(2):

        @pl.when(core == mine)
        def _():
            for tap in range(27):
                tx, row = tap // 9, tap % 9
                ref = keep_ref if tap // HALF == mine else send_ref
                ref[tap % HALF] = total[row * C : (row + 1) * C, tx * C : (tx + 1) * C] * scale
            ref = keep_ref if mine == 1 else send_ref
            ref[HALF - 1] = jnp.zeros((C, C), F32)


def rim_grad(own, stacked, faces, near, edges, far):
    zlo, zhi, ylo, yhi = faces
    nzlo, nzhi, nylo, nyhi = near
    operands = [zlo, zhi, ylo, yhi, nylo, nyhi, nzlo, nzhi, *edges, *far]
    parts = [1, 1, 1, 1] + [0] * 8
    return pl.pallas_call(
        rim_grad_kernel,
        grid=(1,),
        in_specs=[VMEM]
        + [whole_part(a.shape, part) for a, part in zip(operands, parts, strict=True)]
        + [slab_part(stacked.shape, 1, 1, 0), slab_part(stacked.shape, 1, 1, X - 1)],
        out_specs=[VMEM, VMEM],
        out_shape=[shape((HALF, C, C), F32)] * 2,
        scratch_shapes=[pltpu.VMEM((3, 2, Y + 2, Z, C), BF16), pltpu.VMEM((TAPS, WIDE), F32)],
        compiler_params=params(),
        cost_estimate=cost(3, 6 << 20),
    )(own, *operands, stacked, stacked)


def conv_kernel(first, wide_lo, wide_hi, *refs):
    occ_ref, s_ref, ylo_ref, yhi_ref, zlo_ref, zhi_ref = refs[:6]
    lo = refs[6 : 6 + wide_lo]
    hi = refs[6 + wide_lo : 6 + wide_lo + wide_hi]
    w_ref = refs[6 + wide_lo + wide_hi]
    o_ref, token_ref, scratch = refs[-3:]
    token_ref[...] = jnp.zeros_like(token_ref)
    keep = brick_flags(occ_ref, first // E)

    def finish(x, total):
        o_ref[x] = jnp.where(keep, total.reshape(Y, Z, C), 0.0).astype(BF16)

    def put_edge(slot, edge):
        if len(edge) == 1:
            put_far(scratch, slot, edge[0])
        else:
            put_slab(scratch, slot, *(ref[0, 0] for ref in edge))

    ends = 2 * GROUP
    put_edge(ends, lo)
    put_edge(ends + 1, hi)
    next_ = jnp.dot(patches(scratch, ends, 1), w_ref[:, :C], preferred_element_type=F32)
    last = jnp.dot(patches(scratch, ends + 1, 1), w_ref[:, 2 * C :], preferred_element_type=F32)
    near = None
    for i in range(PIECE // GROUP):
        x = i * GROUP
        base = i % 2 * GROUP
        for slot in range(GROUP):
            at = x + slot
            put_slab(scratch, base + slot, s_ref[0, at], ylo_ref[0, at], yhi_ref[0, at], zlo_ref[0, at], zhi_ref[0, at])
        made = jnp.dot(patches(scratch, base, GROUP), w_ref[...], preferred_element_type=F32)

        def term(slot, tx):
            return made[slot * ROWS : (slot + 1) * ROWS, tx * C : (tx + 1) * C]

        if i > 0:
            finish(x - 1, near + term(0, 2))
        finish(x, next_ + term(0, 1) + term(1, 2))
        for slot in range(1, GROUP - 1):
            finish(x + slot, term(slot - 1, 0) + term(slot, 1) + term(slot + 1, 2))
        near = term(GROUP - 2, 0) + term(GROUP - 1, 1)
        next_ = term(GROUP - 1, 0)
    finish(PIECE - 1, near + last)


def conv_piece(part, index, occupancy, field, far, weight, done, tie):
    first = index * PIECE
    operands = [occupancy, *field]
    specs = [SMEM] + [slab_part(a.shape, part, PIECE, index) for a in field]
    widths = []
    for at, message in ((first - 1, far[0]), (first + PIECE, far[1])):
        if 0 <= at < X:
            operands += field
            specs += [slab_part(a.shape, part, 1, at) for a in field]
            widths.append(len(field))
        else:
            operands.append(message)
            specs.append(whole_part(message.shape, part))
            widths.append(1)
    operands += [weight, tie]
    specs += [VMEM, ANY]
    aliases = {}
    if done is not None:
        aliases = {len(operands): 0}
        operands.append(done)
        specs.append(ANY)
    return pl.pallas_call(
        lambda *refs: conv_kernel(first, *widths, *refs),
        grid=(1,),
        in_specs=specs,
        out_specs=[pl.BlockSpec((PIECE, Y, Z, C), lambda i: (index, 0, 0, 0)), VMEM],
        out_shape=[shape((X, Y, Z, C), BF16), shape((8, C), F32)],
        scratch_shapes=[pltpu.VMEM((3, 2 * GROUP + 2, Y + 2, Z, C), BF16)],
        input_output_aliases=aliases,
        compiler_params=params(),
        cost_estimate=cost(PIECE, 2 << 20),
    )(*operands)


def small_kernel(kernel, out_shape, operands, ties=(), specs=None):
    count = len(operands)

    def run(*refs):
        kernel(*refs[:count], *refs[count + len(ties) :])

    return pl.pallas_call(
        run,
        in_specs=(specs or [VMEM] * count) + [ANY] * len(ties),
        out_specs=jax.tree.map(lambda _: VMEM, out_shape),
        out_shape=out_shape,
        compiler_params=params(),
        cost_estimate=pl.CostEstimate(flops=1000, bytes_accessed=1 << 20, transcendentals=0),
    )(*operands, *ties)


def edge_kernel(zlo, zhi, lo, hi):
    for side, ref in enumerate((zlo, zhi)):
        lo[:, side] = ref[:, :, 0, :]
        hi[:, side] = ref[:, :, Y - 1, :]


def message_kernel(s_first, s_last, ylo, yhi, zlo, zhi, elo, ehi, col_lo, col_hi, to_lo, to_hi):
    for side, (near, col) in enumerate(((zlo, col_lo), (zhi, col_hi))):
        own = near[...].astype(F32)
        low = elo[:, side].astype(F32)[:, :, None, :]
        high = ehi[:, side].astype(F32)[:, :, None, :]
        tail = jnp.zeros((2, X, 24 - Y - 2, C), F32)
        col[...] = jnp.concatenate([low, own, high, tail], axis=2).astype(BF16)
    for at, center, to in ((0, s_first, to_lo), (X - 1, s_last, to_hi)):
        to[:, :Y] = center[:, 0]
        to[:, Y] = ylo[:, at]
        to[:, Y + 1] = yhi[:, at]
        rims = jnp.concatenate([col_lo[:, at], col_hi[:, at]], axis=1)
        to[:, Y + 2 :] = rims.reshape(2, 3, Z, C)


def arrange_kernel(w_ref, forward, flipped):
    for tap in range(27):
        tx, row = tap // 9, tap % 9
        forward[row * C : (row + 1) * C, tx * C : (tx + 1) * C] = w_ref[tap]
        flipped[row * C : (row + 1) * C, tx * C : (tx + 1) * C] = w_ref[26 - tap].astype(F32).T.astype(BF16)


def place(axis):
    at = lax.axis_index(axis)
    return at // 2 if axis == "gx" else at


def ring(axis, step):
    if axis == "gx":
        return [(2 * z + c, 2 * ((z + step) % 4) + c) for z in range(4) for c in range(2)]
    return [(i, (i + step) % 4) for i in range(4)]


def deal(axis, terms, ties=()):
    rows = terms[0].shape[0] // 4

    def kernel(*refs):
        me = place(axis)
        for step in range(4):
            at = pl.ds((me + step) % 4 * rows, rows)
            total = refs[0][at]
            for ref in refs[1 : len(terms)]:
                total = total + ref[at]
            refs[len(terms) + step][...] = total

    return small_kernel(kernel, [shape((rows, C), F32)] * 4, terms, ties)


def collect(axis, parts, ties=()):
    rows = parts[0].shape[0]

    def kernel(*refs):
        me = place(axis)
        for step in range(4):
            refs[4][pl.ds((me + 4 - step) % 4 * rows, rows)] = refs[step][...]

    return small_kernel(kernel, shape((4 * rows, C), F32), parts, ties)


def rotate(axis, values):
    return [lax.ppermute(value, axis, ring(axis, step)) for step, value in zip((1, 2, 3), values, strict=True)]


def sum_kernel(a, b, c, d, o):
    o[...] = (a[...] + c[...]) + (b[...] + d[...])


def final_kernel(own, other, o):
    core = lax.axis_index("gx") % 2
    for mine in range(2):

        @pl.when(core == mine)
        def _():
            halves = (own, other) if mine == 0 else (other, own)
            o[: HALF * C] = halves[0][...]
            o[HALF * C :] = halves[1][: 27 * C - HALF * C]


def shift_open(value, axis, step):
    count = lax.axis_size(axis)
    return lax.ppermute(value, axis, [(i, i + step) for i in range(count) if 0 <= i + step < count])


def body(features, occupancy, weight, cotangent):
    stacked, zlo, zhi, ylo, yhi = prepare(occupancy, features, cotangent)
    near_zlo = shift_open(zhi, "gz", 1)
    near_zhi = shift_open(zlo, "gz", -1)
    near_ylo = shift_open(yhi, "gy", 1)
    near_yhi = shift_open(ylo, "gy", -1)
    own = own_grad(stacked, 0, 5, None, zlo)

    edge = shape((2, 2, X, C), BF16)
    edge_lo, edge_hi = small_kernel(edge_kernel, [edge, edge], [near_zlo, near_zhi], [own])
    edges = (shift_open(edge_hi, "gy", 1), shift_open(edge_lo, "gy", -1))
    forward, flipped = small_kernel(
        arrange_kernel, [shape((TAPS, WIDE), BF16)] * 2, [weight.reshape(27, C, C)], [edge_lo]
    )

    column = shape((2, X, 24, C), BF16)
    message = shape((2, Y + 5, Z, C), BF16)
    col_lo, col_hi, to_lo, to_hi = small_kernel(
        message_kernel,
        [column, column, message, message],
        [stacked[:, :1], stacked[:, X - 1 :], near_ylo, near_yhi, near_zlo, near_zhi, *edges],
        [forward],
    )
    far = (shift_open(to_hi, "gx", 1), shift_open(to_lo, "gx", -1))
    own = own_grad(stacked, 5, 3, own, to_lo)
    keep, send = rim_grad(
        own, stacked, (zlo, zhi, ylo, yhi), (near_zlo, near_zhi, near_ylo, near_yhi), edges, far
    )

    field = [stacked, near_ylo, near_yhi, col_lo, col_hi]
    made = [None, None]
    weights = (forward, flipped)
    order = [(part, index) for part in range(2) for index in range(X // PIECE)]

    def convolve(count, tie):
        token = tie
        for _ in range(count):
            part, index = order.pop(0)
            made[part], token = conv_piece(
                part, index, occupancy, field, far, weights[part], made[part], token
            )
        return [token] if count else []

    swap = [(i, i ^ 1) for i in range(8)]
    came = lax.ppermute(send, "gx", swap)
    flat = (HALF * C, C)
    own, *parts = deal("gx", [keep.reshape(flat), came.reshape(flat)])
    came = rotate("gx", parts)
    ties = convolve(3, parts[0])
    own, *parts = deal("gy", [own, *came], ties)
    came = rotate("gy", parts)
    ties = convolve(1, parts[0])
    part_shape = shape(own.shape, F32)
    mine = small_kernel(sum_kernel, part_shape, [own, *came], ties)
    came = rotate("gz", [mine] * 3)
    ties = convolve(1, mine)
    summed = small_kernel(sum_kernel, part_shape, [mine, *came], ties)
    came = rotate("gy", [summed] * 3)
    ties = convolve(1, summed)
    whole = collect("gy", [summed, *came], ties)
    came = rotate("gx", [whole] * 3)
    ties = convolve(1, whole)
    whole = collect("gx", [whole, *came], ties)
    other = lax.ppermute(whole, "gx", swap)
    ties = convolve(1, whole)
    full = small_kernel(final_kernel, shape((27 * C, C), F32), [whole, other], ties)
    return (made[0], made[1], full.reshape(3, 3, 3, C, C))


def solution(mesh):
    placed = (P("gx", "gy", "gz", None), P("gx", "gy", "gz"), P(), P("gx", "gy", "gz", None))
    return jax.shard_map(
        body,
        mesh=mesh,
        in_specs=placed,
        out_specs=(P("gx", "gy", "gz", None), P("gx", "gy", "gz", None), P()),
        check_vma=False,
    )
```

```python
import math

import jax
import jax.numpy as jnp
from jax import lax
from jax.experimental import pallas as pl
from jax.experimental.pallas import tpu as pltpu
from jax.sharding import PartitionSpec as P

SHARE = 8
X, Y, Z, C = 32, 16, 16, 128
E = 8
ROWS = Y * Z
GROUP = 4
PIECE = 8
TAPS = 9 * C
WIDE = 3 * C
HALF = 14
F32 = jnp.float32
BF16 = jnp.bfloat16
VMEM = pl.BlockSpec(memory_space=pltpu.VMEM)
SMEM = pl.BlockSpec(memory_space=pltpu.SMEM)
ANY = pl.BlockSpec(memory_space=pl.ANY)
HBM = pl.BlockSpec(memory_space=pltpu.HBM)
DEPTH_FIRST = (((0,), (0,)), ((), ()))


def shape(dims, dtype):
    return jax.ShapeDtypeStruct(dims, dtype)


def params(mebibytes=24):
    return pltpu.CompilerParams(vmem_limit_bytes=mebibytes * 1024 * 1024)


def cost(slabs, moved):
    return pl.CostEstimate(flops=2 * 27 * C * C * slabs * ROWS, bytes_accessed=moved, transcendentals=0)


def inside(axis, side):
    at = lax.axis_index(axis)
    return at > 0 if side == 0 else at < lax.axis_size(axis) - 1


def held(value, axis, side):
    return jnp.where(inside(axis, side), value, jnp.zeros_like(value))


def brick_flags(occ_ref, brick):
    low_z = lax.broadcasted_iota(jnp.int32, (E, Z, C), 1) < E
    halves = [jnp.where(low_z, occ_ref[brick, j, 0], occ_ref[brick, j, 1]) for j in range(2)]
    return jnp.concatenate(halves, axis=0) == 1


def prepare_kernel(occ_ref, f_ref, c_ref, s_ref, zlo_ref, zhi_ref, ylo_ref, yhi_ref, buffer, arrived):
    bricks = X // E

    def copy(part, brick):
        source = (f_ref, c_ref)[part].at[pl.ds(brick * E, E)]
        return pltpu.make_async_copy(source, buffer.at[part, pl.ds(brick * E, E)], arrived.at[part, brick])

    for brick in range(bricks):
        for part in range(2):
            copy(part, brick).start()
    for brick in range(bricks):
        keep = brick_flags(occ_ref, brick)
        span = slice(brick * E, (brick + 1) * E)
        for part in range(2):
            copy(part, brick).wait()
            value = jnp.where(keep[None], buffer[part, span].astype(F32), 0.0).astype(BF16)
            s_ref[part, span] = value
            zlo_ref[part, span] = value[:, :, 0, :]
            zhi_ref[part, span] = value[:, :, Z - 1, :]
            ylo_ref[part, span] = value[:, 0]
            yhi_ref[part, span] = value[:, Y - 1]


def prepare(occupancy, features, cotangent):
    return pl.pallas_call(
        prepare_kernel,
        in_specs=[SMEM, HBM, HBM],
        out_specs=[VMEM] * 5,
        out_shape=[shape((2, X, Y, Z, C), BF16)] + [shape((2, X, Z, C), BF16)] * 4,
        scratch_shapes=[pltpu.VMEM((2, X, Y, Z, C), BF16), pltpu.SemaphoreType.DMA((2, X // E))],
        compiler_params=params(),
        cost_estimate=pl.CostEstimate(flops=1000000, bytes_accessed=9 << 20, transcendentals=0),
    )(occupancy, features, cotangent)


def moved_z(whole, step):
    rows = whole.shape[0] * whole.shape[1]
    flat = whole.reshape(rows, C)
    return pltpu.roll(flat, -step % rows, 0).reshape(whole.shape)


def put_slab(scratch, slot, center, ylo, yhi, zlo, zhi):
    whole = jnp.concatenate([ylo[None], center, yhi[None]], axis=0)
    scratch[1, slot] = whole
    whole = whole.astype(F32)
    at = lax.broadcasted_iota(jnp.int32, (Y + 2, Z, C), 1)
    low = zlo.astype(F32)[: Y + 2, None, :]
    high = zhi.astype(F32)[: Y + 2, None, :]
    scratch[0, slot] = jnp.where(at == 0, low, moved_z(whole, -1)).astype(BF16)
    scratch[2, slot] = jnp.where(at == Z - 1, high, moved_z(whole, 1)).astype(BF16)


def put_own(scratch, slot, center):
    scratch[1, slot, 1 : Y + 1] = center
    whole = center.astype(F32)
    at = lax.broadcasted_iota(jnp.int32, (Y, Z, C), 1)
    scratch[0, slot, 1 : Y + 1] = jnp.where(at == 0, 0.0, moved_z(whole, -1)).astype(BF16)
    scratch[2, slot, 1 : Y + 1] = jnp.where(at == Z - 1, 0.0, moved_z(whole, 1)).astype(BF16)


def patches(scratch, first, slots):
    pieces = []
    for ty in range(3):
        for tz in range(3):
            pieces.append(scratch[tz, first : first + slots, ty : ty + Y].reshape(slots * ROWS, C))
    return jnp.concatenate(pieces, axis=1)


def put_far(scratch, slot, far_ref, part, side):
    slab = held(far_ref[part], "gx", side)
    rims = slab[Y + 2 :].reshape(-1, C)
    put_slab(scratch, slot, slab[:Y], slab[Y], slab[Y + 1], rims[:24], rims[24:])


def own_grad_kernel(first, groups, more, s_ref, *refs):
    scratch, total = refs[-1], refs[-2]
    scratch[:, :, 0:1] = jnp.zeros((3, 2 * GROUP, 1, Z, C), BF16)
    scratch[:, :, Y + 1 :] = jnp.zeros((3, 2 * GROUP, 1, Z, C), BF16)
    none = jnp.zeros((ROWS, C), BF16)
    for i in range(groups):
        x = (first + i) * GROUP
        base = i % 2 * GROUP
        for slot in range(GROUP):
            put_own(scratch, base + slot, s_ref[0, x + slot])
        columns = []
        for tx in range(3):
            rows = []
            start, stop = x + 1 - tx, x + 1 - tx + GROUP
            if start < 0:
                rows.append(none)
            rows.append(s_ref[1, max(start, 0) : min(stop, X)].reshape(-1, C))
            if stop > X:
                rows.append(none)
            columns.append(jnp.concatenate(rows, axis=0))
        made = lax.dot_general(
            patches(scratch, base, GROUP), jnp.concatenate(columns, axis=1), DEPTH_FIRST, preferred_element_type=F32
        )
        if i > 0:
            total[...] += made
        elif more:
            total[...] = refs[0][...] + made
        else:
            total[...] = made


def own_grad(stacked, first, groups, before, tie):
    more = before is not None
    return pl.pallas_call(
        lambda *refs: own_grad_kernel(first, groups, more, *refs),
        in_specs=[VMEM] * (1 + more) + [ANY],
        out_specs=VMEM,
        out_shape=shape((TAPS, WIDE), F32),
        scratch_shapes=[pltpu.VMEM((3, 2 * GROUP, Y + 2, Z, C), BF16)],
        compiler_params=params(),
        cost_estimate=cost(groups * GROUP, 8 << 20),
    )(stacked, *([before] if more else []), tie)


def rim_grad_kernel(
    own_ref, s_ref, gzlo, gzhi, gylo, gyhi, nzlo, nzhi, nylo, nyhi, elo, ehi, far_lo, far_hi,
    keep_ref, send_ref, scratch, total,
):
    put_far(scratch, 0, far_lo, 0, 0)
    put_far(scratch, 1, far_hi, 0, 1)
    none = jnp.zeros((ROWS, C), BF16)
    first = jnp.concatenate([s_ref[1, 0].reshape(ROWS, C), none], axis=0)
    last = jnp.concatenate([none, s_ref[1, X - 1].reshape(ROWS, C)], axis=0)
    beside = jnp.concatenate([first, jnp.zeros_like(first), last], axis=1)
    total[...] = own_ref[...] + lax.dot_general(
        patches(scratch, 0, 2), beside, DEPTH_FIRST, preferred_element_type=F32
    )
    blank = jnp.zeros((1, Z, C), BF16)
    at = lax.broadcasted_iota(jnp.int32, (X, Z, C), 1)

    def add(row, stride, trio, face_ref):
        padded = jnp.concatenate([blank, face_ref[1], blank], axis=0)
        around = jnp.concatenate([padded[2 - tx : 2 - tx + X].reshape(X * Z, C) for tx in range(3)], axis=1)
        left = jnp.concatenate([a.astype(BF16).reshape(X * Z, C) for a in trio], axis=1)
        made = lax.dot_general(left, around, DEPTH_FIRST, preferred_element_type=F32)
        for k in range(3):
            start = (row + k * stride) * C
            total[start : start + C] += made[k * C : (k + 1) * C]

    for side, row, near, edges, face in ((0, 0, nylo, elo, gylo), (1, 6, nyhi, ehi, gyhi)):
        whole = near[0].astype(F32)
        corners = held(edges[0].astype(F32), "gy", side)
        low = corners[0][:, None, :]
        high = corners[1][:, None, :]
        before = jnp.where(at == 0, low, moved_z(whole, -1))
        after = jnp.where(at == Z - 1, high, moved_z(whole, 1))
        add(row, 1, (before, whole, after), face)
    for side, row, near, face in ((0, 0, nzlo, gzlo), (1, 2, nzhi, gzhi)):
        whole = held(near[0].astype(F32), "gz", side)
        before = jnp.where(at == 0, 0.0, moved_z(whole, -1))
        after = jnp.where(at == Z - 1, 0.0, moved_z(whole, 1))
        add(row, 3, (before, whole, after), face)

    scale = 1.0 / math.sqrt(SHARE * 128 * E**3)
    core = lax.axis_index("gx") % 2
    for mine in range(2):

        @pl.when(core == mine)
        def _():
            for tap in range(27):
                tx, row = tap // 9, tap % 9
                ref = keep_ref if tap // HALF == mine else send_ref
                ref[tap % HALF] = total[row * C : (row + 1) * C, tx * C : (tx + 1) * C] * scale
            ref = keep_ref if mine == 1 else send_ref
            ref[HALF - 1] = jnp.zeros((C, C), F32)


def rim_grad(own, stacked, operands):
    return pl.pallas_call(
        rim_grad_kernel,
        in_specs=[VMEM] * (2 + len(operands)),
        out_specs=[VMEM, VMEM],
        out_shape=[shape((HALF, C, C), F32)] * 2,
        scratch_shapes=[pltpu.VMEM((3, 2, Y + 2, Z, C), BF16), pltpu.VMEM((TAPS, WIDE), F32)],
        compiler_params=params(),
        cost_estimate=cost(3, 6 << 20),
    )(own, stacked, *operands)


def conv_kernel(part, index, occ_ref, s_ref, ylo_ref, yhi_ref, zlo_ref, zhi_ref, w_ref, *refs):
    first = index * PIECE
    starts, ends = index == 0, first + PIECE == X
    refs = list(refs)
    far_lo = refs.pop(0) if starts else None
    far_hi = refs.pop(0) if ends else None
    before = None if starts else refs.pop(0)
    o_ref, carry_ref, scratch, made_ref, left = refs[-5:]
    keep = brick_flags(occ_ref, index)

    def finish(x, total):
        flags = keep if x >= 0 else brick_flags(occ_ref, index - 1)
        made_ref[x + 1] = jnp.where(flags, total.reshape(Y, Z, C), 0.0).astype(BF16)

    def copy(slot, start, stop):
        target = o_ref.at[pl.ds(first - 1 + start, stop - start)]
        return pltpu.make_async_copy(made_ref.at[pl.ds(start, stop - start)], target, left.at[slot])

    if starts:
        put_far(scratch, 2 * GROUP, far_lo, part, 0)
        near = None
        next_ = jnp.dot(patches(scratch, 2 * GROUP, 1), w_ref[:, :C], preferred_element_type=F32)
    else:
        near, next_ = before[0], before[1]
    copies = []
    for i in range(PIECE // GROUP):
        x = i * GROUP
        base = i % 2 * GROUP
        for slot in range(GROUP):
            at = (part, first + x + slot)
            put_slab(scratch, base + slot, s_ref[at], ylo_ref[at], yhi_ref[at], zlo_ref[at], zhi_ref[at])
        made = jnp.dot(patches(scratch, base, GROUP), w_ref[...], preferred_element_type=F32)

        def term(slot, tx):
            return made[slot * ROWS : (slot + 1) * ROWS, tx * C : (tx + 1) * C]

        if near is not None:
            finish(x - 1, near + term(0, 2))
        finish(x, next_ + term(0, 1) + term(1, 2))
        for slot in range(1, GROUP - 1):
            finish(x + slot, term(slot - 1, 0) + term(slot, 1) + term(slot + 1, 2))
        copies.append(copy(i, x + (near is None), x + GROUP))
        copies[-1].start()
        near = term(GROUP - 2, 0) + term(GROUP - 1, 1)
        next_ = term(GROUP - 1, 0)
    if ends:
        put_far(scratch, 2 * GROUP, far_hi, part, 1)
        last = jnp.dot(patches(scratch, 2 * GROUP, 1), w_ref[:, 2 * C :], preferred_element_type=F32)
        finish(PIECE - 1, near + last)
        copies.append(copy(len(copies), PIECE, PIECE + 1))
        copies[-1].start()
    carry_ref[0] = near
    carry_ref[1] = next_
    for made_copy in copies:
        made_copy.wait()


def conv_piece(part, index, occupancy, field, far, weight, before, done, tie):
    operands = [occupancy, *field, weight]
    starts, ends = index == 0, (index + 1) * PIECE == X
    if starts:
        operands.append(far[0])
    if ends:
        operands.append(far[1])
    if not starts:
        operands.append(before)
    specs = [SMEM] + [VMEM] * (len(operands) - 1)
    operands.append(tie)
    specs.append(ANY)
    aliases = {}
    if not starts:
        aliases = {len(operands): 0}
        operands.append(done)
        specs.append(ANY)
    return pl.pallas_call(
        lambda *refs: conv_kernel(part, index, *refs),
        in_specs=specs,
        out_specs=[ANY, VMEM],
        out_shape=[shape((X, Y, Z, C), BF16), shape((2, ROWS, C), F32)],
        scratch_shapes=[
            pltpu.VMEM((3, 2 * GROUP + 1, Y + 2, Z, C), BF16),
            pltpu.VMEM((PIECE + 1, Y, Z, C), BF16),
            pltpu.SemaphoreType.DMA((3,)),
        ],
        input_output_aliases=aliases,
        compiler_params=params(),
        cost_estimate=cost(PIECE, 2 << 20),
    )(*operands)


def small_kernel(kernel, out_shape, operands, ties=(), specs=None):
    count = len(operands)

    def run(*refs):
        kernel(*refs[:count], *refs[count + len(ties) :])

    return pl.pallas_call(
        run,
        in_specs=(specs or [VMEM] * count) + [ANY] * len(ties),
        out_specs=jax.tree.map(lambda _: VMEM, out_shape),
        out_shape=out_shape,
        compiler_params=params(),
        cost_estimate=pl.CostEstimate(flops=1000, bytes_accessed=1 << 20, transcendentals=0),
    )(*operands, *ties)


def edge_kernel(zlo, zhi, lo, hi):
    for side, ref in enumerate((zlo, zhi)):
        lo[:, side] = held(ref[:, :, 0, :], "gz", side)
        hi[:, side] = held(ref[:, :, Y - 1, :], "gz", side)


def message_kernel(s_ref, ylo, yhi, zlo, zhi, elo, ehi, held_ylo, held_yhi, col_lo, col_hi, to_lo, to_hi):
    held_ylo[...] = held(ylo[...], "gy", 0)
    held_yhi[...] = held(yhi[...], "gy", 1)
    tail = jnp.zeros((2, X, 24 - Y - 2, C), F32)
    for side, (near, col) in enumerate(((zlo, col_lo), (zhi, col_hi))):
        own = held(near[...].astype(F32), "gz", side)
        low = held(elo[:, side].astype(F32), "gy", 0)[:, :, None, :]
        high = held(ehi[:, side].astype(F32), "gy", 1)[:, :, None, :]
        col[...] = jnp.concatenate([low, own, high, tail], axis=2).astype(BF16)
    for at, to in ((0, to_lo), (X - 1, to_hi)):
        to[:, :Y] = s_ref[:, at]
        to[:, Y] = held_ylo[:, at]
        to[:, Y + 1] = held_yhi[:, at]
        rims = jnp.concatenate([col_lo[:, at], col_hi[:, at]], axis=1)
        to[:, Y + 2 :] = rims.reshape(2, 3, Z, C)


def arrange_kernel(w_ref, forward, flipped):
    for tap in range(27):
        tx, row = tap // 9, tap % 9
        forward[row * C : (row + 1) * C, tx * C : (tx + 1) * C] = w_ref[tap]
        flipped[row * C : (row + 1) * C, tx * C : (tx + 1) * C] = w_ref[26 - tap].astype(F32).T.astype(BF16)


def place(axis):
    at = lax.axis_index(axis)
    return at // 2 if axis == "gx" else at


def ring(axis, step):
    if axis == "gx":
        return [(2 * z + c, 2 * ((z + step) % 4) + c) for z in range(4) for c in range(2)]
    return [(i, (i + step) % 4) for i in range(4)]


def deal(axis, terms, ties=()):
    rows = terms[0].shape[0] // 4

    def kernel(*refs):
        me = place(axis)
        for step in range(4):
            at = pl.ds((me + step) % 4 * rows, rows)
            total = refs[0][at]
            for ref in refs[1 : len(terms)]:
                total = total + ref[at]
            refs[len(terms) + step][...] = total

    return small_kernel(kernel, [shape((rows, C), F32)] * 4, terms, ties)


def collect(axis, parts, ties=()):
    rows = parts[0].shape[0]

    def kernel(*refs):
        me = place(axis)
        for step in range(4):
            refs[4][pl.ds((me + 4 - step) % 4 * rows, rows)] = refs[step][...]

    return small_kernel(kernel, shape((4 * rows, C), F32), parts, ties)


def rotate(axis, values):
    return [lax.ppermute(value, axis, ring(axis, step)) for step, value in zip((1, 2, 3), values, strict=True)]


def sum_kernel(a, b, c, d, o):
    o[...] = (a[...] + c[...]) + (b[...] + d[...])


def final_kernel(own, other, o):
    core = lax.axis_index("gx") % 2
    for mine in range(2):

        @pl.when(core == mine)
        def _():
            halves = (own, other) if mine == 0 else (other, own)
            o[: HALF * C] = halves[0][...]
            o[HALF * C :] = halves[1][: 27 * C - HALF * C]


def shift(value, axis, step):
    count = lax.axis_size(axis)
    return lax.ppermute(value, axis, [(i, (i + step) % count) for i in range(count)])


def body(features, occupancy, weight, cotangent):
    stacked, zlo, zhi, ylo, yhi = prepare(occupancy, features, cotangent)
    near_zlo = shift(zhi, "gz", 1)
    near_zhi = shift(zlo, "gz", -1)
    near_ylo = shift(yhi, "gy", 1)
    near_yhi = shift(ylo, "gy", -1)
    own = own_grad(stacked, 0, 5, None, zlo)

    edge = shape((2, 2, X, C), BF16)
    edge_lo, edge_hi = small_kernel(edge_kernel, [edge, edge], [near_zlo, near_zhi], [own])
    edges = (shift(edge_hi, "gy", 1), shift(edge_lo, "gy", -1))
    forward, flipped = small_kernel(
        arrange_kernel, [shape((TAPS, WIDE), BF16)] * 2, [weight.reshape(27, C, C)], [edge_lo]
    )

    face = shape((2, X, Z, C), BF16)
    column = shape((2, X, 24, C), BF16)
    message = shape((2, Y + 5, Z, C), BF16)
    held_ylo, held_yhi, col_lo, col_hi, to_lo, to_hi = small_kernel(
        message_kernel,
        [face, face, column, column, message, message],
        [stacked, near_ylo, near_yhi, near_zlo, near_zhi, *edges],
        [forward],
    )
    far = (shift(to_hi, "gx", 1), shift(to_lo, "gx", -1))
    own = own_grad(stacked, 5, 3, own, to_lo)
    rims = [zlo, zhi, ylo, yhi, near_zlo, near_zhi, held_ylo, held_yhi, *edges, *far]
    keep, send = rim_grad(own, stacked, rims)

    field = [stacked, held_ylo, held_yhi, col_lo, col_hi]
    made = [None, None]
    carry = [None, None]
    weights = (forward, flipped)
    order = [(part, index) for part in range(2) for index in range(X // PIECE)]

    def convolve(count, tie):
        token = tie
        for _ in range(count):
            part, index = order.pop(0)
            made[part], carry[part] = conv_piece(
                part, index, occupancy, field, far, weights[part], carry[part], made[part], token
            )
            token = carry[part]
        return [token] if count else []

    swap = [(i, i ^ 1) for i in range(8)]
    came = lax.ppermute(send, "gx", swap)
    flat = (HALF * C, C)
    own, *parts = deal("gx", [keep.reshape(flat), came.reshape(flat)])
    came = rotate("gx", parts)
    ties = convolve(3, parts[0])
    own, *parts = deal("gy", [own, *came], ties)
    came = rotate("gy", parts)
    ties = convolve(1, parts[0])
    part_shape = shape(own.shape, F32)
    mine = small_kernel(sum_kernel, part_shape, [own, *came], ties)
    came = rotate("gz", [mine] * 3)
    ties = convolve(1, mine)
    summed = small_kernel(sum_kernel, part_shape, [mine, *came], ties)
    came = rotate("gy", [summed] * 3)
    ties = convolve(1, summed)
    whole = collect("gy", [summed, *came], ties)
    came = rotate("gx", [whole] * 3)
    ties = convolve(2, whole)
    whole = collect("gx", [whole, *came], ties)
    other = lax.ppermute(whole, "gx", swap)
    ties = convolve(0, whole)
    full = small_kernel(final_kernel, shape((27 * C, C), F32), [whole, other], ties)
    return (made[0], made[1], full.reshape(3, 3, 3, C, C))


def solution(mesh):
    placed = (P("gx", "gy", "gz", None), P("gx", "gy", "gz"), P(), P("gx", "gy", "gz", None))
    return jax.shard_map(
        body,
        mesh=mesh,
        in_specs=placed,
        out_specs=(P("gx", "gy", "gz", None), P("gx", "gy", "gz", None), P()),
        check_vma=False,
    )
```

```python
import math

import jax
import jax.numpy as jnp
from jax import lax
from jax.experimental import pallas as pl
from jax.experimental.pallas import tpu as pltpu
from jax.sharding import PartitionSpec as P

SHARE = 8
X, Y, Z, C = 32, 16, 16, 128
E = 8
ROWS = Y * Z
GROUP = 4
TAPS = 9 * C
WIDE = 3 * C
HALF = 14
F32 = jnp.float32
BF16 = jnp.bfloat16
VMEM = pl.BlockSpec(memory_space=pltpu.VMEM)
SMEM = pl.BlockSpec(memory_space=pltpu.SMEM)
ANY = pl.BlockSpec(memory_space=pl.ANY)
DEPTH_FIRST = (((0,), (0,)), ((), ()))


def shape(dims, dtype):
    return jax.ShapeDtypeStruct(dims, dtype)


def params(mebibytes=24):
    return pltpu.CompilerParams(vmem_limit_bytes=mebibytes * 1024 * 1024)


def cost(slabs, moved):
    return pl.CostEstimate(flops=2 * 27 * C * C * slabs * ROWS, bytes_accessed=moved, transcendentals=0)


def inside(axis, side):
    at = lax.axis_index(axis)
    return at > 0 if side == 0 else at < lax.axis_size(axis) - 1


def held(value, axis, side):
    return jnp.where(inside(axis, side), value, jnp.zeros_like(value))


def brick_flags(occ_ref, brick):
    low_z = lax.broadcasted_iota(jnp.int32, (E, Z, C), 1) < E
    halves = [jnp.where(low_z, occ_ref[brick, j, 0], occ_ref[brick, j, 1]) for j in range(2)]
    return jnp.concatenate(halves, axis=0) == 1


def prepare_kernel(occ_ref, f_ref, c_ref, s_ref, zlo_ref, zhi_ref, ylo_ref, yhi_ref):
    for end in (0, X + 1):
        s_ref[:, end] = jnp.zeros((2, Y, Z, C), BF16)
    for brick in range(X // E):
        keep = brick_flags(occ_ref, brick)
        span = slice(brick * E, (brick + 1) * E)
        for part, ref in enumerate((f_ref, c_ref)):
            value = jnp.where(keep[None], ref[span].astype(F32), 0.0).astype(BF16)
            s_ref[part, brick * E + 1 : (brick + 1) * E + 1] = value
            zlo_ref[part, span] = value[:, :, 0, :]
            zhi_ref[part, span] = value[:, :, Z - 1, :]
            ylo_ref[part, span] = value[:, 0]
            yhi_ref[part, span] = value[:, Y - 1]


def prepare(occupancy, features, cotangent):
    return pl.pallas_call(
        prepare_kernel,
        in_specs=[SMEM, VMEM, VMEM],
        out_specs=[VMEM] * 5,
        out_shape=[shape((2, X + 2, Y, Z, C), BF16)] + [shape((2, X, Z, C), BF16)] * 4,
        compiler_params=params(),
        cost_estimate=pl.CostEstimate(flops=1000000, bytes_accessed=9 << 20, transcendentals=0),
    )(occupancy, features, cotangent)


def moved_z(whole, step):
    rows = whole.shape[0] * whole.shape[1]
    flat = whole.reshape(rows, C)
    return pltpu.roll(flat, -step % rows, 0).reshape(whole.shape)


def put_slab(scratch, slot, center, ylo, yhi, zlo, zhi):
    whole = jnp.concatenate([ylo[None], center, yhi[None]], axis=0)
    scratch[1, slot] = whole
    whole = whole.astype(F32)
    at = lax.broadcasted_iota(jnp.int32, (Y + 2, Z, C), 1)
    low = zlo.astype(F32)[: Y + 2, None, :]
    high = zhi.astype(F32)[: Y + 2, None, :]
    scratch[0, slot] = jnp.where(at == 0, low, moved_z(whole, -1)).astype(BF16)
    scratch[2, slot] = jnp.where(at == Z - 1, high, moved_z(whole, 1)).astype(BF16)


def put_own(scratch, slot, center):
    scratch[1, slot, 1 : Y + 1] = center
    whole = center.astype(F32)
    at = lax.broadcasted_iota(jnp.int32, (Y, Z, C), 1)
    scratch[0, slot, 1 : Y + 1] = jnp.where(at == 0, 0.0, moved_z(whole, -1)).astype(BF16)
    scratch[2, slot, 1 : Y + 1] = jnp.where(at == Z - 1, 0.0, moved_z(whole, 1)).astype(BF16)


def patches(shifted, slots):
    pieces = []
    for ty in range(3):
        for tz in range(3):
            pieces.append(shifted[tz, :slots, ty : ty + Y].reshape(slots * ROWS, C))
    return jnp.concatenate(pieces, axis=1)


def put_far(scratch, slot, far_ref, part, side):
    slab = held(far_ref[part], "gx", side)
    rims = slab[Y + 2 :].reshape(-1, C)
    put_slab(scratch, slot, slab[:Y], slab[Y], slab[Y + 1], rims[:24], rims[24:])


def own_grad_kernel(first, groups, more, s_ref, *refs):
    total, even, odd = refs[-3:]
    for shifted in (even, odd):
        shifted[:, :, 0:1] = jnp.zeros((3, GROUP, 1, Z, C), BF16)
        shifted[:, :, Y + 1 :] = jnp.zeros((3, GROUP, 1, Z, C), BF16)

    def put(shifted, x):
        for slot in range(GROUP):
            put_own(shifted, slot, s_ref[0, x + 1 + slot])

    def product(shifted, x):
        columns = [s_ref[1, pl.ds(x + 2 - tx, GROUP)].reshape(GROUP * ROWS, C) for tx in range(3)]
        beside = jnp.concatenate(columns, axis=1)
        return lax.dot_general(patches(shifted, GROUP), beside, DEPTH_FIRST, preferred_element_type=F32)

    put(even, first)
    total[...] = refs[0][...] if more else jnp.zeros_like(total)

    def trip(i, carry):
        x = first + i * 2 * GROUP
        total[...] += product(even, x)
        put(odd, x + GROUP)
        total[...] += product(odd, x + GROUP)
        put(even, jnp.minimum(x + 2 * GROUP, X - GROUP))
        return carry

    lax.fori_loop(0, groups // 2, trip, 0)


def own_grad(stacked, first, groups, before, tie):
    more = before is not None
    return pl.pallas_call(
        lambda *refs: own_grad_kernel(first, groups, more, *refs),
        in_specs=[VMEM] * (1 + more) + [ANY],
        out_specs=VMEM,
        out_shape=shape((TAPS, WIDE), F32),
        scratch_shapes=[pltpu.VMEM((3, GROUP, Y + 2, Z, C), BF16)] * 2,
        compiler_params=params(),
        cost_estimate=cost(groups * GROUP, 8 << 20),
    )(stacked, *([before] if more else []), tie)


def rim_grad_kernel(
    own_ref, s_ref, gzlo, gzhi, gylo, gyhi, nzlo, nzhi, nylo, nyhi, elo, ehi, far_lo, far_hi,
    keep_ref, send_ref, scratch, total,
):
    put_far(scratch, 0, far_lo, 0, 0)
    put_far(scratch, 1, far_hi, 0, 1)
    none = jnp.zeros((ROWS, C), BF16)
    first = jnp.concatenate([s_ref[1, 1].reshape(ROWS, C), none], axis=0)
    last = jnp.concatenate([none, s_ref[1, X].reshape(ROWS, C)], axis=0)
    beside = jnp.concatenate([first, jnp.zeros_like(first), last], axis=1)
    total[...] = own_ref[...] + lax.dot_general(
        patches(scratch, 2), beside, DEPTH_FIRST, preferred_element_type=F32
    )
    blank = jnp.zeros((1, Z, C), BF16)
    at = lax.broadcasted_iota(jnp.int32, (X, Z, C), 1)

    def add(row, stride, trio, face_ref):
        padded = jnp.concatenate([blank, face_ref[1], blank], axis=0)
        around = jnp.concatenate([padded[2 - tx : 2 - tx + X].reshape(X * Z, C) for tx in range(3)], axis=1)
        left = jnp.concatenate([a.astype(BF16).reshape(X * Z, C) for a in trio], axis=1)
        made = lax.dot_general(left, around, DEPTH_FIRST, preferred_element_type=F32)
        for k in range(3):
            start = (row + k * stride) * C
            total[start : start + C] += made[k * C : (k + 1) * C]

    for side, row, near, edges, face in ((0, 0, nylo, elo, gylo), (1, 6, nyhi, ehi, gyhi)):
        whole = near[0].astype(F32)
        corners = held(edges[0].astype(F32), "gy", side)
        low = corners[0][:, None, :]
        high = corners[1][:, None, :]
        before = jnp.where(at == 0, low, moved_z(whole, -1))
        after = jnp.where(at == Z - 1, high, moved_z(whole, 1))
        add(row, 1, (before, whole, after), face)
    for side, row, near, face in ((0, 0, nzlo, gzlo), (1, 2, nzhi, gzhi)):
        whole = held(near[0].astype(F32), "gz", side)
        before = jnp.where(at == 0, 0.0, moved_z(whole, -1))
        after = jnp.where(at == Z - 1, 0.0, moved_z(whole, 1))
        add(row, 3, (before, whole, after), face)

    scale = 1.0 / math.sqrt(SHARE * 128 * E**3)
    core = lax.axis_index("gx") % 2
    for mine in range(2):

        @pl.when(core == mine)
        def _():
            for tap in range(27):
                tx, row = tap // 9, tap % 9
                ref = keep_ref if tap // HALF == mine else send_ref
                ref[tap % HALF] = total[row * C : (row + 1) * C, tx * C : (tx + 1) * C] * scale
            ref = keep_ref if mine == 1 else send_ref
            ref[HALF - 1] = jnp.zeros((C, C), F32)


def rim_grad(own, stacked, operands):
    return pl.pallas_call(
        rim_grad_kernel,
        in_specs=[VMEM] * (2 + len(operands)),
        out_specs=[VMEM, VMEM],
        out_shape=[shape((HALF, C, C), F32)] * 2,
        scratch_shapes=[pltpu.VMEM((3, 2, Y + 2, Z, C), BF16), pltpu.VMEM((TAPS, WIDE), F32)],
        compiler_params=params(),
        cost_estimate=cost(3, 6 << 20),
    )(own, stacked, *operands)


def conv_kernel(part, first, groups, following, occ_ref, *refs):
    starts, ends = first == 0, first + groups * GROUP == X
    refs = list(refs)
    field = [refs.pop(0) for _ in range(5)]
    w_ref = refs.pop(0)
    far_lo = refs.pop(0) if starts else None
    far_hi = refs.pop(0) if ends else None
    before = None if starts else refs.pop(0)
    whole = groups * GROUP == X
    ready = None if whole else refs.pop(0)
    o_ref, carry_ref, even, odd, edge, made_ref, left = refs[-7:]
    count = groups * GROUP

    def put(shifted, at, x):
        s_ref, ylo_ref, yhi_ref, zlo_ref, zhi_ref = field
        for slot in range(GROUP):
            put_slab(shifted, slot, s_ref[at, x + 1 + slot], *(ref[at, x + slot] for ref in field[1:]))

    def finish(x, total):
        flags = brick_flags(occ_ref, jnp.maximum(x, 0) // E)
        made_ref[x - first + 1] = jnp.where(flags, total.reshape(Y, Z, C), 0.0).astype(BF16)

    def copy(slot, start, size):
        target = o_ref.at[pl.ds(first - 1 + start, size)]
        return pltpu.make_async_copy(made_ref.at[pl.ds(start, size)], target, left.at[slot])

    def group(shifted, x, near, next_):
        made = jnp.dot(patches(shifted, GROUP), w_ref[...], preferred_element_type=F32)

        def term(slot, tx):
            return made[slot * ROWS : (slot + 1) * ROWS, tx * C : (tx + 1) * C]

        if not (isinstance(x, int) and x == 0):
            finish(x - 1, near + term(0, 2))
        finish(x, next_ + term(0, 1) + term(1, 2))
        for slot in range(1, GROUP - 1):
            finish(x + slot, term(slot - 1, 0) + term(slot, 1) + term(slot + 1, 2))
        return term(GROUP - 2, 0) + term(GROUP - 1, 1), term(GROUP - 1, 0)

    if starts:
        put_far(edge, 0, far_lo, part, 0)
        near = jnp.zeros((ROWS, C), F32)
        next_ = jnp.dot(patches(edge, 1), w_ref[:, :C], preferred_element_type=F32)
    else:
        near, next_ = before[0], before[1]
    if whole:
        put(even, part, 0)
        carry_ref[0] = near
        carry_ref[1] = next_

        def trip(i, carry):
            x = i * 2 * GROUP
            near, next_ = group(even, x, carry_ref[0], carry_ref[1])
            put(odd, part, x + GROUP)
            near, next_ = group(odd, x + GROUP, near, next_)
            after = i + 1 == groups // 2
            put(even, jnp.where(after, following[0], part), jnp.where(after, following[1], x + 2 * GROUP))
            carry_ref[0] = near
            carry_ref[1] = next_
            return carry

        lax.fori_loop(0, groups // 2, trip, 0)
        near = carry_ref[0]
        parts = [(1, count - 1)]
    else:
        near, next_ = group(ready, first, near, next_)
        parts = [(1, GROUP - 1) if starts else (0, GROUP), (GROUP, GROUP)]
        copy(0, *parts[0]).start()
        put(odd, part, first + GROUP)
        near, next_ = group(odd, first + GROUP, near, next_)
        if following is not None:
            put(even, *following)
        carry_ref[0] = near
        carry_ref[1] = next_
    copy(len(parts) - 1, *parts[-1]).start()
    if ends:
        put_far(edge, 0, far_hi, part, 1)
        last = jnp.dot(patches(edge, 1), w_ref[:, 2 * C :], preferred_element_type=F32)
        finish(X - 1, near + last)
        parts.append((count, 1))
        copy(len(parts) - 1, *parts[-1]).start()
    for slot, span in enumerate(parts):
        copy(slot, *span).wait()


def conv_piece(part, first, groups, following, occupancy, field, far, weight, before, ready, done, tie):
    operands = [occupancy, *field, weight]
    starts, ends = first == 0, first + groups * GROUP == X
    if starts:
        operands.append(far[0])
    if ends:
        operands.append(far[1])
    if not starts:
        operands.append(before)
    if groups * GROUP < X:
        operands.append(ready)
    aliases = {}
    specs = [SMEM] + [VMEM] * (len(operands) - 1)
    operands.append(tie)
    specs.append(ANY)
    if not starts:
        aliases = {len(operands): 0}
        operands.append(done)
        specs.append(ANY)
    shifted = (3, GROUP, Y + 2, Z, C)
    return pl.pallas_call(
        lambda *refs: conv_kernel(part, first, groups, following, *refs),
        in_specs=specs,
        out_specs=[ANY, VMEM, VMEM],
        out_shape=[shape((X, Y, Z, C), BF16), shape((2, ROWS, C), F32), shape(shifted, BF16)],
        scratch_shapes=[
            pltpu.VMEM(shifted, BF16),
            pltpu.VMEM((3, 1, Y + 2, Z, C), BF16),
            pltpu.VMEM((groups * GROUP + 1, Y, Z, C), BF16),
            pltpu.SemaphoreType.DMA((3,)),
        ],
        input_output_aliases=aliases,
        compiler_params=params(),
        cost_estimate=cost(groups * GROUP, 2 << 20),
    )(*operands)


def small_kernel(kernel, out_shape, operands, ties=(), specs=None):
    count = len(operands)

    def run(*refs):
        kernel(*refs[:count], *refs[count + len(ties) :])

    return pl.pallas_call(
        run,
        in_specs=(specs or [VMEM] * count) + [ANY] * len(ties),
        out_specs=jax.tree.map(lambda _: VMEM, out_shape),
        out_shape=out_shape,
        compiler_params=params(),
        cost_estimate=pl.CostEstimate(flops=1000, bytes_accessed=1 << 20, transcendentals=0),
    )(*operands, *ties)


def edge_kernel(zlo, zhi, lo, hi):
    for side, ref in enumerate((zlo, zhi)):
        lo[:, side] = held(ref[:, :, 0, :], "gz", side)
        hi[:, side] = held(ref[:, :, Y - 1, :], "gz", side)


def message_kernel(s_ref, ylo, yhi, zlo, zhi, elo, ehi, held_ylo, held_yhi, col_lo, col_hi, to_lo, to_hi):
    held_ylo[...] = held(ylo[...], "gy", 0)
    held_yhi[...] = held(yhi[...], "gy", 1)
    tail = jnp.zeros((2, X, 24 - Y - 2, C), F32)
    for side, (near, col) in enumerate(((zlo, col_lo), (zhi, col_hi))):
        own = held(near[...].astype(F32), "gz", side)
        low = held(elo[:, side].astype(F32), "gy", 0)[:, :, None, :]
        high = held(ehi[:, side].astype(F32), "gy", 1)[:, :, None, :]
        col[...] = jnp.concatenate([low, own, high, tail], axis=2).astype(BF16)
    for at, to in ((0, to_lo), (X - 1, to_hi)):
        to[:, :Y] = s_ref[:, at + 1]
        to[:, Y] = held_ylo[:, at]
        to[:, Y + 1] = held_yhi[:, at]
        rims = jnp.concatenate([col_lo[:, at], col_hi[:, at]], axis=1)
        to[:, Y + 2 :] = rims.reshape(2, 3, Z, C)


def arrange_kernel(w_ref, forward, flipped):
    for tap in range(27):
        tx, row = tap // 9, tap % 9
        forward[row * C : (row + 1) * C, tx * C : (tx + 1) * C] = w_ref[tap]
        flipped[row * C : (row + 1) * C, tx * C : (tx + 1) * C] = w_ref[26 - tap].astype(F32).T.astype(BF16)


def place(axis):
    at = lax.axis_index(axis)
    return at // 2 if axis == "gx" else at


def ring(axis, step):
    if axis == "gx":
        return [(2 * z + c, 2 * ((z + step) % 4) + c) for z in range(4) for c in range(2)]
    return [(i, (i + step) % 4) for i in range(4)]


def deal(axis, terms, ties=()):
    rows = terms[0].shape[0] // 4

    def kernel(*refs):
        me = place(axis)
        for step in range(4):
            at = pl.ds((me + step) % 4 * rows, rows)
            total = refs[0][at]
            for ref in refs[1 : len(terms)]:
                total = total + ref[at]
            refs[len(terms) + step][...] = total

    return small_kernel(kernel, [shape((rows, C), F32)] * 4, terms, ties)


def collect(axis, parts, ties=()):
    rows = parts[0].shape[0]

    def kernel(*refs):
        me = place(axis)
        for step in range(4):
            refs[4][pl.ds((me + 4 - step) % 4 * rows, rows)] = refs[step][...]

    return small_kernel(kernel, shape((4 * rows, C), F32), parts, ties)


def rotate(axis, values):
    return [lax.ppermute(value, axis, ring(axis, step)) for step, value in zip((1, 2, 3), values, strict=True)]


def sum_kernel(a, b, c, d, o):
    o[...] = (a[...] + c[...]) + (b[...] + d[...])


def final_kernel(own, other, o):
    core = lax.axis_index("gx") % 2
    for mine in range(2):

        @pl.when(core == mine)
        def _():
            halves = (own, other) if mine == 0 else (other, own)
            o[: HALF * C] = halves[0][...]
            o[HALF * C :] = halves[1][: 27 * C - HALF * C]


def shift(value, axis, step):
    count = lax.axis_size(axis)
    return lax.ppermute(value, axis, [(i, (i + step) % count) for i in range(count)])


def body(features, occupancy, weight, cotangent):
    stacked, zlo, zhi, ylo, yhi = prepare(occupancy, features, cotangent)
    near_zlo = shift(zhi, "gz", 1)
    near_zhi = shift(zlo, "gz", -1)
    near_ylo = shift(yhi, "gy", 1)
    near_yhi = shift(ylo, "gy", -1)
    own = own_grad(stacked, 0, 4, None, zlo)

    edge = shape((2, 2, X, C), BF16)
    edge_lo, edge_hi = small_kernel(edge_kernel, [edge, edge], [near_zlo, near_zhi], [own])
    edges = (shift(edge_hi, "gy", 1), shift(edge_lo, "gy", -1))
    forward, flipped = small_kernel(
        arrange_kernel, [shape((TAPS, WIDE), BF16)] * 2, [weight.reshape(27, C, C)], [edge_lo]
    )

    face = shape((2, X, Z, C), BF16)
    column = shape((2, X, 24, C), BF16)
    message = shape((2, Y + 5, Z, C), BF16)
    held_ylo, held_yhi, col_lo, col_hi, to_lo, to_hi = small_kernel(
        message_kernel,
        [face, face, column, column, message, message],
        [stacked, near_ylo, near_yhi, near_zlo, near_zhi, *edges],
        [forward],
    )
    far = (shift(to_hi, "gx", 1), shift(to_lo, "gx", -1))
    own = own_grad(stacked, X // 2, 4, own, to_lo)
    rims = [zlo, zhi, ylo, yhi, near_zlo, near_zhi, held_ylo, held_yhi, *edges, *far]
    keep, send = rim_grad(own, stacked, rims)

    field = [stacked, held_ylo, held_yhi, col_lo, col_hi]
    made = [None, None]
    weights = (forward, flipped)
    step = 2 * GROUP
    order = [(0, 0, X // GROUP)] + [(1, at, 2) for at in range(0, X, step)]
    state = {"carry": None, "ready": None}

    def convolve(tie):
        part, first, groups = order.pop(0)
        following = order[0][:2] if order else None
        made[part], state["carry"], state["ready"] = conv_piece(
            part, first, groups, following, occupancy, field, far, weights[part],
            state["carry"], state["ready"], made[part], tie,
        )
        return [state["carry"]]

    swap = [(i, i ^ 1) for i in range(8)]
    came = lax.ppermute(send, "gx", swap)
    flat = (HALF * C, C)
    own, *parts = deal("gx", [keep.reshape(flat), came.reshape(flat)])
    came = rotate("gx", parts)
    ties = convolve(parts[0])
    own, *parts = deal("gy", [own, *came], ties)
    came = rotate("gy", parts)
    ties = convolve(parts[0])
    part_shape = shape(own.shape, F32)
    mine = small_kernel(sum_kernel, part_shape, [own, *came], ties)
    came = rotate("gz", [mine] * 3)
    ties = convolve(mine)
    summed = small_kernel(sum_kernel, part_shape, [mine, *came], ties)
    came = rotate("gy", [summed] * 3)
    ties = convolve(summed)
    whole = collect("gy", [summed, *came], ties)
    came = rotate("gx", [whole] * 3)
    ties = convolve(whole)
    whole = collect("gx", [whole, *came], ties)
    other = lax.ppermute(whole, "gx", swap)
    full = small_kernel(final_kernel, shape((27 * C, C), F32), [whole, other])
    return (made[0], made[1], full.reshape(3, 3, 3, C, C))


def solution(mesh):
    placed = (P("gx", "gy", "gz", None), P("gx", "gy", "gz"), P(), P("gx", "gy", "gz", None))
    return jax.shard_map(
        body,
        mesh=mesh,
        in_specs=placed,
        out_specs=(P("gx", "gy", "gz", None), P("gx", "gy", "gz", None), P()),
        check_vma=False,
    )
```

```python
import math

import jax
import jax.numpy as jnp
from jax import lax
from jax.experimental import pallas as pl
from jax.experimental.pallas import tpu as pltpu
from jax.sharding import PartitionSpec as P

SHARE = 8
X, Y, Z, C = 32, 16, 16, 128
E = 8
ROWS = Y * Z
GROUP = 4
SPAN = 8
TAPS = 9 * C
WIDE = 3 * C
HALF = 14
F32 = jnp.float32
BF16 = jnp.bfloat16
VMEM = pl.BlockSpec(memory_space=pltpu.VMEM)
SMEM = pl.BlockSpec(memory_space=pltpu.SMEM)
ANY = pl.BlockSpec(memory_space=pl.ANY)
DEPTH_FIRST = (((0,), (0,)), ((), ()))


def shape(dims, dtype):
    return jax.ShapeDtypeStruct(dims, dtype)


def params(mebibytes=24):
    return pltpu.CompilerParams(vmem_limit_bytes=mebibytes * 1024 * 1024)


def cost(slabs, moved):
    return pl.CostEstimate(flops=2 * 27 * C * C * slabs * ROWS, bytes_accessed=moved, transcendentals=0)


def inside(axis, side):
    at = lax.axis_index(axis)
    return at > 0 if side == 0 else at < lax.axis_size(axis) - 1


def held(value, axis, side):
    return jnp.where(inside(axis, side), value, jnp.zeros_like(value))


def brick_flags(occ_ref, brick):
    low_z = lax.broadcasted_iota(jnp.int32, (E, Z, C), 1) < E
    halves = [jnp.where(low_z, occ_ref[brick, j, 0], occ_ref[brick, j, 1]) for j in range(2)]
    return jnp.concatenate(halves, axis=0) == 1


def prepare_kernel(occ_ref, f_ref, c_ref, s_ref, zlo_ref, zhi_ref, ylo_ref, yhi_ref):
    for end in (0, X + 1):
        s_ref[:, end] = jnp.zeros((2, Y, Z, C), BF16)
    for brick in range(X // E):
        keep = brick_flags(occ_ref, brick)
        span = slice(brick * E, (brick + 1) * E)
        for part, ref in enumerate((f_ref, c_ref)):
            value = jnp.where(keep[None], ref[span].astype(F32), 0.0).astype(BF16)
            s_ref[part, brick * E + 1 : (brick + 1) * E + 1] = value
            zlo_ref[part, span] = value[:, :, 0, :]
            zhi_ref[part, span] = value[:, :, Z - 1, :]
            ylo_ref[part, span] = value[:, 0]
            yhi_ref[part, span] = value[:, Y - 1]


def prepare(occupancy, features, cotangent):
    return pl.pallas_call(
        prepare_kernel,
        in_specs=[SMEM, VMEM, VMEM],
        out_specs=[VMEM] * 5,
        out_shape=[shape((2, X + 2, Y, Z, C), BF16)] + [shape((2, X, Z, C), BF16)] * 4,
        compiler_params=params(),
        cost_estimate=pl.CostEstimate(flops=1000000, bytes_accessed=9 << 20, transcendentals=0),
    )(occupancy, features, cotangent)


def moved_z(whole, step):
    rows = whole.shape[0] * whole.shape[1]
    flat = whole.reshape(rows, C)
    return pltpu.roll(flat, -step % rows, 0).reshape(whole.shape)


def put_slab(scratch, slot, center, ylo, yhi, zlo, zhi):
    whole = jnp.concatenate([ylo[None], center, yhi[None]], axis=0)
    scratch[1, slot] = whole
    whole = whole.astype(F32)
    at = lax.broadcasted_iota(jnp.int32, (Y + 2, Z, C), 1)
    low = zlo.astype(F32)[: Y + 2, None, :]
    high = zhi.astype(F32)[: Y + 2, None, :]
    scratch[0, slot] = jnp.where(at == 0, low, moved_z(whole, -1)).astype(BF16)
    scratch[2, slot] = jnp.where(at == Z - 1, high, moved_z(whole, 1)).astype(BF16)


def put_own(scratch, slot, center):
    scratch[1, slot, 1 : Y + 1] = center
    whole = center.astype(F32)
    at = lax.broadcasted_iota(jnp.int32, (Y, Z, C), 1)
    scratch[0, slot, 1 : Y + 1] = jnp.where(at == 0, 0.0, moved_z(whole, -1)).astype(BF16)
    scratch[2, slot, 1 : Y + 1] = jnp.where(at == Z - 1, 0.0, moved_z(whole, 1)).astype(BF16)


def patches(shifted, slots):
    pieces = []
    for ty in range(3):
        for tz in range(3):
            pieces.append(shifted[tz, :slots, ty : ty + Y].reshape(slots * ROWS, C))
    return jnp.concatenate(pieces, axis=1)


def put_far(scratch, slot, far_ref, part, side):
    slab = held(far_ref[part], "gx", side)
    rims = slab[Y + 2 :].reshape(-1, C)
    put_slab(scratch, slot, slab[:Y], slab[Y], slab[Y + 1], rims[:24], rims[24:])


def own_grad_kernel(first, more, s_ref, *refs):
    total, even, odd = refs[-3:]
    for shifted in (even, odd):
        shifted[:, :, 0:1] = jnp.zeros((3, SPAN, 1, Z, C), BF16)
        shifted[:, :, Y + 1 :] = jnp.zeros((3, SPAN, 1, Z, C), BF16)

    def put(shifted, x):
        for slot in range(SPAN):
            put_own(shifted, slot, s_ref[0, x + 1 + slot])

    def product(shifted, x):
        columns = [s_ref[1, x + 2 - tx : x + 2 - tx + SPAN].reshape(SPAN * ROWS, C) for tx in range(3)]
        beside = jnp.concatenate(columns, axis=1)
        return lax.dot_general(patches(shifted, SPAN), beside, DEPTH_FIRST, preferred_element_type=F32)

    put(even, first)
    made = product(even, first)
    put(odd, first + SPAN)
    total[...] = refs[0][...] + made if more else made
    total[...] += product(odd, first + SPAN)


def own_grad(stacked, first, before, tie):
    more = before is not None
    return pl.pallas_call(
        lambda *refs: own_grad_kernel(first, more, *refs),
        in_specs=[VMEM] * (1 + more) + [ANY],
        out_specs=VMEM,
        out_shape=shape((TAPS, WIDE), F32),
        scratch_shapes=[pltpu.VMEM((3, SPAN, Y + 2, Z, C), BF16)] * 2,
        compiler_params=params(),
        cost_estimate=cost(2 * SPAN, 8 << 20),
    )(stacked, *([before] if more else []), tie)


def rim_grad_kernel(
    own_ref, s_ref, gzlo, gzhi, gylo, gyhi, nzlo, nzhi, nylo, nyhi, elo, ehi, far_lo, far_hi,
    keep_ref, send_ref, scratch, total,
):
    put_far(scratch, 0, far_lo, 0, 0)
    put_far(scratch, 1, far_hi, 0, 1)
    none = jnp.zeros((ROWS, C), BF16)
    first = jnp.concatenate([s_ref[1, 1].reshape(ROWS, C), none], axis=0)
    last = jnp.concatenate([none, s_ref[1, X].reshape(ROWS, C)], axis=0)
    beside = jnp.concatenate([first, jnp.zeros_like(first), last], axis=1)
    total[...] = own_ref[...] + lax.dot_general(
        patches(scratch, 2), beside, DEPTH_FIRST, preferred_element_type=F32
    )
    blank = jnp.zeros((1, Z, C), BF16)
    at = lax.broadcasted_iota(jnp.int32, (X, Z, C), 1)

    def add(row, stride, trio, face_ref):
        padded = jnp.concatenate([blank, face_ref[1], blank], axis=0)
        around = jnp.concatenate([padded[2 - tx : 2 - tx + X].reshape(X * Z, C) for tx in range(3)], axis=1)
        left = jnp.concatenate([a.astype(BF16).reshape(X * Z, C) for a in trio], axis=1)
        made = lax.dot_general(left, around, DEPTH_FIRST, preferred_element_type=F32)
        for k in range(3):
            start = (row + k * stride) * C
            total[start : start + C] += made[k * C : (k + 1) * C]

    for side, row, near, edges, face in ((0, 0, nylo, elo, gylo), (1, 6, nyhi, ehi, gyhi)):
        whole = near[0].astype(F32)
        corners = held(edges[0].astype(F32), "gy", side)
        low = corners[0][:, None, :]
        high = corners[1][:, None, :]
        before = jnp.where(at == 0, low, moved_z(whole, -1))
        after = jnp.where(at == Z - 1, high, moved_z(whole, 1))
        add(row, 1, (before, whole, after), face)
    for side, row, near, face in ((0, 0, nzlo, gzlo), (1, 2, nzhi, gzhi)):
        whole = held(near[0].astype(F32), "gz", side)
        before = jnp.where(at == 0, 0.0, moved_z(whole, -1))
        after = jnp.where(at == Z - 1, 0.0, moved_z(whole, 1))
        add(row, 3, (before, whole, after), face)

    scale = 1.0 / math.sqrt(SHARE * 128 * E**3)
    core = lax.axis_index("gx") % 2
    for mine in range(2):

        @pl.when(core == mine)
        def _():
            for tap in range(27):
                tx, row = tap // 9, tap % 9
                ref = keep_ref if tap // HALF == mine else send_ref
                ref[tap % HALF] = total[row * C : (row + 1) * C, tx * C : (tx + 1) * C] * scale
            ref = keep_ref if mine == 1 else send_ref
            ref[HALF - 1] = jnp.zeros((C, C), F32)


def rim_grad(own, stacked, operands):
    return pl.pallas_call(
        rim_grad_kernel,
        in_specs=[VMEM] * (2 + len(operands)),
        out_specs=[VMEM, VMEM],
        out_shape=[shape((HALF, C, C), F32)] * 2,
        scratch_shapes=[pltpu.VMEM((3, 2, Y + 2, Z, C), BF16), pltpu.VMEM((TAPS, WIDE), F32)],
        compiler_params=params(),
        cost_estimate=cost(3, 6 << 20),
    )(own, stacked, *operands)


def conv_kernel(part, first, groups, following, occ_ref, *refs):
    starts, ends = first == 0, first + groups * GROUP == X
    refs = list(refs)
    field = [refs.pop(0) for _ in range(5)]
    w_ref = refs.pop(0)
    far_lo = refs.pop(0) if starts else None
    far_hi = refs.pop(0) if ends else None
    before = None if starts else refs.pop(0)
    ready = None if starts and part == 0 else refs.pop(0)
    o_ref, carry_ref, even, odd, edge, made_ref, left = refs[-7:]
    count = groups * GROUP

    def put(shifted, at, x):
        s_ref, ylo_ref, yhi_ref, zlo_ref, zhi_ref = field
        for slot in range(GROUP):
            put_slab(shifted, slot, s_ref[at, x + 1 + slot], *(ref[at, x + slot] for ref in field[1:]))

    def finish(x, total):
        flags = brick_flags(occ_ref, jnp.maximum(x, 0) // E)
        made_ref[x - first + 1] = jnp.where(flags, total.reshape(Y, Z, C), 0.0).astype(BF16)

    def copy(x, size, sem):
        source = made_ref.at[pl.ds(x - first, size)]
        return pltpu.make_async_copy(source, o_ref.at[pl.ds(x - 1, size)], left.at[sem])

    def group(shifted, x, sem, near, next_, opens):
        made = jnp.dot(patches(shifted, GROUP), w_ref[...], preferred_element_type=F32)

        def term(slot, tx):
            return made[slot * ROWS : (slot + 1) * ROWS, tx * C : (tx + 1) * C]

        if opens is not True:
            finish(x - 1, near + term(0, 2))
        finish(x, next_ + term(0, 1) + term(1, 2))
        for slot in range(1, GROUP - 1):
            finish(x + slot, term(slot - 1, 0) + term(slot, 1) + term(slot + 1, 2))
        if opens is None:
            pl.when(sem == 0)(lambda: copy(x + 1, GROUP - 1, sem).start())
            pl.when(sem > 0)(lambda: copy(x, GROUP, sem).start())
        elif opens:
            copy(x + 1, GROUP - 1, sem).start()
        else:
            copy(x, GROUP, sem).start()
        return term(GROUP - 2, 0) + term(GROUP - 1, 1), term(GROUP - 1, 0)

    if starts:
        put_far(edge, 0, far_lo, part, 0)
        near = jnp.zeros((ROWS, C), F32)
        next_ = jnp.dot(patches(edge, 1), w_ref[:, :C], preferred_element_type=F32)
    else:
        near, next_ = before[0], before[1]
    if groups > 2:
        if ready is None:
            put(even, part, 0)
        else:
            even[...] = ready[...]
        carry_ref[0] = near
        carry_ref[1] = next_

        def trip(i, carry):
            x = first + i * 2 * GROUP
            near, next_ = group(even, x, 2 * i, carry_ref[0], carry_ref[1], None if starts else False)
            put(odd, part, x + GROUP)
            near, next_ = group(odd, x + GROUP, 2 * i + 1, near, next_, False)
            after = i + 1 == groups // 2
            at, then = following or (part, X - GROUP)
            put(even, jnp.where(after, at, part), jnp.where(after, then, x + 2 * GROUP))
            carry_ref[0] = near
            carry_ref[1] = next_
            return carry

        lax.fori_loop(0, groups // 2, trip, 0)
        near = carry_ref[0]
    else:
        near, next_ = group(ready, first, 0, near, next_, starts)
        if groups == 2:
            put(odd, part, first + GROUP)
            near, next_ = group(odd, first + GROUP, 1, near, next_, False)
        put(even, *following)
        carry_ref[0] = near
        carry_ref[1] = next_
    if ends:
        put_far(edge, 0, far_hi, part, 1)
        last = jnp.dot(patches(edge, 1), w_ref[:, 2 * C :], preferred_element_type=F32)
        finish(X - 1, near + last)
        copy(X, 1, groups).start()
    for sem in range(groups):
        x = first + sem * GROUP
        if starts and sem == 0:
            copy(x + 1, GROUP - 1, sem).wait()
        else:
            copy(x, GROUP, sem).wait()
    if ends:
        copy(X, 1, groups).wait()


def conv_piece(part, first, groups, following, occupancy, field, far, weight, before, ready, done, tie):
    operands = [occupancy, *field, weight]
    starts, ends = first == 0, first + groups * GROUP == X
    if starts:
        operands.append(far[0])
    if ends:
        operands.append(far[1])
    if not starts:
        operands.append(before)
    if ready is not None:
        operands.append(ready)
    aliases = {}
    specs = [SMEM] + [VMEM] * (len(operands) - 1)
    operands.append(tie)
    specs.append(ANY)
    if not starts:
        aliases = {len(operands): 0}
        operands.append(done)
        specs.append(ANY)
    shifted = (3, GROUP, Y + 2, Z, C)
    more = following is not None
    buffers = [shape((2, ROWS, C), F32), shape(shifted, BF16)]
    small = shape((8, C), F32)

    scratch = [
        pltpu.VMEM(shifted, BF16),
        pltpu.VMEM((3, 1, Y + 2, Z, C), BF16),
        pltpu.VMEM((groups * GROUP + 1, Y, Z, C), BF16),
        pltpu.SemaphoreType.DMA((groups + 1,)),
    ]
    if not more:
        scratch = [pltpu.VMEM(b.shape, b.dtype) for b in buffers] + scratch

    def plain(*refs):
        conv_kernel(part, first, groups, following, *refs)

    def final(*refs):
        refs[-7][...] = jnp.zeros((8, C), F32)
        conv_kernel(part, first, groups, following, *refs[:-7], *refs[-6:])

    return pl.pallas_call(
        plain if more else final,
        in_specs=specs,
        out_specs=[ANY] + [VMEM] * (2 if more else 1),
        out_shape=[shape((X, Y, Z, C), BF16)] + (buffers if more else [small]),
        scratch_shapes=scratch,
        input_output_aliases=aliases,
        compiler_params=params(),
        cost_estimate=cost(groups * GROUP, 2 << 20),
    )(*operands)


def small_kernel(kernel, out_shape, operands, ties=(), specs=None):
    count = len(operands)

    def run(*refs):
        kernel(*refs[:count], *refs[count + len(ties) :])

    return pl.pallas_call(
        run,
        in_specs=(specs or [VMEM] * count) + [ANY] * len(ties),
        out_specs=jax.tree.map(lambda _: VMEM, out_shape),
        out_shape=out_shape,
        compiler_params=params(),
        cost_estimate=pl.CostEstimate(flops=1000, bytes_accessed=1 << 20, transcendentals=0),
    )(*operands, *ties)


def edge_kernel(zlo, zhi, lo, hi):
    for side, ref in enumerate((zlo, zhi)):
        lo[:, side] = held(ref[:, :, 0, :], "gz", side)
        hi[:, side] = held(ref[:, :, Y - 1, :], "gz", side)


def message_kernel(s_ref, ylo, yhi, zlo, zhi, elo, ehi, held_ylo, held_yhi, col_lo, col_hi, to_lo, to_hi):
    held_ylo[...] = held(ylo[...], "gy", 0)
    held_yhi[...] = held(yhi[...], "gy", 1)
    tail = jnp.zeros((2, X, 24 - Y - 2, C), F32)
    for side, (near, col) in enumerate(((zlo, col_lo), (zhi, col_hi))):
        own = held(near[...].astype(F32), "gz", side)
        low = held(elo[:, side].astype(F32), "gy", 0)[:, :, None, :]
        high = held(ehi[:, side].astype(F32), "gy", 1)[:, :, None, :]
        col[...] = jnp.concatenate([low, own, high, tail], axis=2).astype(BF16)
    for at, to in ((0, to_lo), (X - 1, to_hi)):
        to[:, :Y] = s_ref[:, at + 1]
        to[:, Y] = held_ylo[:, at]
        to[:, Y + 1] = held_yhi[:, at]
        rims = jnp.concatenate([col_lo[:, at], col_hi[:, at]], axis=1)
        to[:, Y + 2 :] = rims.reshape(2, 3, Z, C)


def arrange_kernel(w_ref, forward, flipped):
    for tap in range(27):
        tx, row = tap // 9, tap % 9
        forward[row * C : (row + 1) * C, tx * C : (tx + 1) * C] = w_ref[tap]
        flipped[row * C : (row + 1) * C, tx * C : (tx + 1) * C] = w_ref[26 - tap].astype(F32).T.astype(BF16)


def place(axis):
    at = lax.axis_index(axis)
    return at // 2 if axis == "gx" else at


def pairs(axis, step):
    if axis == "gx":
        return [(2 * z + c, 2 * (z ^ step) + c) for z in range(4) for c in range(2)]
    return [(i, i ^ step) for i in range(4)]


def deal(axis, terms, ties=()):
    rows = terms[0].shape[0] // 4

    def kernel(*refs):
        me = place(axis)
        for step in range(4):
            at = pl.ds((me ^ step) * rows, rows)
            total = refs[0][at]
            for ref in refs[1 : len(terms)]:
                total = total + ref[at]
            refs[len(terms) + step][...] = total

    return small_kernel(kernel, [shape((rows, C), F32)] * 4, terms, ties)


def collect(axis, parts, ties=()):
    rows = parts[0].shape[0]

    def kernel(*refs):
        me = place(axis)
        for step in range(4):
            refs[4][pl.ds((me ^ step) * rows, rows)] = refs[step][...]

    return small_kernel(kernel, shape((4 * rows, C), F32), parts, ties)


def exchange(axis, values):
    return [lax.ppermute(value, axis, pairs(axis, step)) for step, value in zip((1, 2, 3), values, strict=True)]


def sum_kernel(a, b, c, d, o):
    o[...] = (a[...] + c[...]) + (b[...] + d[...])


def write_half(source, target, left, half):
    rows = (HALF if half == 0 else 27 - HALF) * C
    copy = pltpu.make_async_copy(source.at[pl.ds(0, rows)], target.at[pl.ds(half * HALF * C, rows)], left)
    copy.start()
    copy.wait()


def write(source, mine, target):
    def kernel(*refs):
        o_ref, left = refs[-2:]
        core = lax.axis_index("gx") % 2
        half = core if mine else 1 - core
        for side in range(2):
            pl.when(half == side)(lambda side=side: write_half(refs[0], o_ref, left, side))

    operands = [source] + ([] if target is None else [target])
    return pl.pallas_call(
        kernel,
        in_specs=[VMEM, ANY][: len(operands)],
        out_specs=ANY,
        out_shape=shape((27 * C, C), F32),
        scratch_shapes=[pltpu.SemaphoreType.DMA],
        input_output_aliases={} if target is None else {1: 0},
        compiler_params=params(),
        cost_estimate=pl.CostEstimate(flops=1000, bytes_accessed=1 << 20, transcendentals=0),
    )(*operands)


def shift(value, axis, step):
    count = lax.axis_size(axis)
    return lax.ppermute(value, axis, [(i, (i + step) % count) for i in range(count)])


def body(features, occupancy, weight, cotangent):
    stacked, zlo, zhi, ylo, yhi = prepare(occupancy, features, cotangent)
    near_zlo = shift(zhi, "gz", 1)
    near_zhi = shift(zlo, "gz", -1)
    near_ylo = shift(yhi, "gy", 1)
    near_yhi = shift(ylo, "gy", -1)
    own = own_grad(stacked, 0, None, zlo)

    edge = shape((2, 2, X, C), BF16)
    edge_lo, edge_hi = small_kernel(edge_kernel, [edge, edge], [near_zlo, near_zhi], [own])
    edges = (shift(edge_hi, "gy", 1), shift(edge_lo, "gy", -1))
    forward, flipped = small_kernel(
        arrange_kernel, [shape((TAPS, WIDE), BF16)] * 2, [weight.reshape(27, C, C)], [edge_lo]
    )

    face = shape((2, X, Z, C), BF16)
    column = shape((2, X, 24, C), BF16)
    message = shape((2, Y + 5, Z, C), BF16)
    held_ylo, held_yhi, col_lo, col_hi, to_lo, to_hi = small_kernel(
        message_kernel,
        [face, face, column, column, message, message],
        [stacked, near_ylo, near_yhi, near_zlo, near_zhi, *edges],
        [forward],
    )
    far = (shift(to_hi, "gx", 1), shift(to_lo, "gx", -1))
    own = own_grad(stacked, X // 2, own, to_lo)
    rims = [zlo, zhi, ylo, yhi, near_zlo, near_zhi, held_ylo, held_yhi, *edges, *far]
    keep, send = rim_grad(own, stacked, rims)

    field = [stacked, held_ylo, held_yhi, col_lo, col_hi]
    made = [None, None]
    weights = (forward, flipped)
    order = [(0, 0, 6), (0, 24, 2), (1, 0, 1), (1, 4, 1), (1, 8, 6)]
    state = {"carry": None, "ready": None}

    def convolve(tie):
        part, first, groups = order.pop(0)
        following = order[0][:2] if order else None
        made[part], *rest = conv_piece(
            part, first, groups, following, occupancy, field, far, weights[part],
            state["carry"], state["ready"], made[part], tie,
        )
        if order:
            state["carry"], state["ready"] = rest
        return rest[:1]

    swap = [(i, i ^ 1) for i in range(8)]
    came = lax.ppermute(send, "gx", swap)
    flat = (HALF * C, C)
    own, *parts = deal("gx", [keep.reshape(flat), came.reshape(flat)])
    came = exchange("gx", parts)
    ties = convolve(parts[0])
    own, *parts = deal("gy", [own, *came], ties)
    came = exchange("gy", parts)
    ties = convolve(parts[0])
    part_shape = shape(own.shape, F32)
    mine = small_kernel(sum_kernel, part_shape, [own, *came], ties)
    came = exchange("gz", [mine] * 3)
    ties = convolve(mine)
    summed = small_kernel(sum_kernel, part_shape, [mine, *came], ties)
    came = exchange("gy", [summed] * 3)
    ties = convolve(summed)
    whole = collect("gy", [summed, *came], ties)
    came = exchange("gx", [whole] * 3)
    ties = convolve(whole)
    whole = collect("gx", [whole, *came], ties)
    other = lax.ppermute(whole, "gx", swap)
    full = write(other, False, write(whole, True, None))
    return (made[0], made[1], full.reshape(3, 3, 3, C, C))


def solution(mesh):
    placed = (P("gx", "gy", "gz", None), P("gx", "gy", "gz"), P(), P("gx", "gy", "gz", None))
    return jax.shard_map(
        body,
        mesh=mesh,
        in_specs=placed,
        out_specs=(P("gx", "gy", "gz", None), P("gx", "gy", "gz", None), P()),
        check_vma=False,
    )
```

```python
import math

import jax
import jax.numpy as jnp
from jax import lax
from jax.experimental import pallas as pl
from jax.experimental.pallas import tpu as pltpu
from jax.sharding import PartitionSpec as P

SHARE = 8
X, Y, Z, C = 32, 16, 16, 128
E = 8
ROWS = Y * Z
GROUP = 4
SPAN = 8
TAPS = 9 * C
WIDE = 3 * C
HALF = 14
F32 = jnp.float32
BF16 = jnp.bfloat16
VMEM = pl.BlockSpec(memory_space=pltpu.VMEM)
SMEM = pl.BlockSpec(memory_space=pltpu.SMEM)
ANY = pl.BlockSpec(memory_space=pl.ANY)
DEPTH_FIRST = (((0,), (0,)), ((), ()))


def shape(dims, dtype):
    return jax.ShapeDtypeStruct(dims, dtype)


def params(mebibytes=24):
    return pltpu.CompilerParams(vmem_limit_bytes=mebibytes * 1024 * 1024)


def cost(slabs, moved):
    return pl.CostEstimate(flops=2 * 27 * C * C * slabs * ROWS, bytes_accessed=moved, transcendentals=0)


def inside(axis, side):
    at = lax.axis_index(axis)
    return at > 0 if side == 0 else at < lax.axis_size(axis) - 1


def held(value, axis, side):
    return jnp.where(inside(axis, side), value, jnp.zeros_like(value))


def brick_flags(occ_ref, brick):
    low_z = lax.broadcasted_iota(jnp.int32, (E, Z, C), 1) < E
    halves = [jnp.where(low_z, occ_ref[j, 0, brick], occ_ref[j, 1, brick]) for j in range(2)]
    return jnp.concatenate(halves, axis=0) == 1


def mask_slabs(part, source, mask_ref, s_ref, faces):
    zlo_ref, zhi_ref, ylo_ref, yhi_ref = faces
    for end in (0, X + 1):
        s_ref[end] = jnp.zeros((Y, Z, C), BF16)
    for brick in range(X // E):
        span = slice(brick * E, (brick + 1) * E)
        keep = mask_ref[brick].astype(F32) > 0.0
        value = jnp.where(keep[None], source[span].astype(F32), 0.0).astype(BF16)
        s_ref[brick * E + 1 : (brick + 1) * E + 1] = value
        zlo_ref[part, span] = value[:, :, 0, :]
        zhi_ref[part, span] = value[:, :, Z - 1, :]
        ylo_ref[part, span] = value[:, 0]
        yhi_ref[part, span] = value[:, Y - 1]


def prepare_x_kernel(occ_ref, f_ref, s_ref, mask_ref, *faces):
    for brick in range(X // E):
        mask_ref[brick] = jnp.where(brick_flags(occ_ref, brick), 1.0, 0.0).astype(BF16)
    mask_slabs(0, f_ref, mask_ref, s_ref, faces)


def prepare_g_kernel(c_ref, mask_ref, *refs):
    given, s_ref, faces = refs[:4], refs[4], refs[5:]
    for face, ref in zip(faces, given, strict=True):
        face[0] = ref[0]
    mask_slabs(1, c_ref, mask_ref, s_ref, faces)


def prepare(occupancy, features, cotangent):
    slabs = shape((X + 2, Y, Z, C), BF16)
    mask = shape((X // E, Y, Z, C), BF16)
    own_cost = pl.CostEstimate(flops=1000000, bytes_accessed=5 << 20, transcendentals=0)
    fields, mask, *given = pl.pallas_call(
        prepare_x_kernel,
        in_specs=[SMEM, VMEM],
        out_specs=[VMEM] * 6,
        out_shape=[slabs, mask] + [shape((1, X, Z, C), BF16)] * 4,
        compiler_params=params(),
        cost_estimate=own_cost,
    )(jnp.transpose(occupancy, (1, 2, 0)), features)
    cotangents, *faces = pl.pallas_call(
        prepare_g_kernel,
        in_specs=[VMEM] * 6,
        out_specs=[VMEM] * 5,
        out_shape=[slabs] + [shape((2, X, Z, C), BF16)] * 4,
        compiler_params=params(),
        cost_estimate=own_cost,
    )(cotangent, mask, *given)
    return (fields, cotangents), mask, faces


def moved_z(whole, step):
    rows = whole.shape[0] * whole.shape[1]
    flat = whole.reshape(rows, C)
    return pltpu.roll(flat, -step % rows, 0).reshape(whole.shape)


def put_slab(scratch, slot, center, ylo, yhi, zlo, zhi):
    whole = jnp.concatenate([ylo[None], center, yhi[None]], axis=0)
    scratch[1, slot] = whole
    whole = whole.astype(F32)
    at = lax.broadcasted_iota(jnp.int32, (Y + 2, Z, C), 1)
    low = zlo.astype(F32)[: Y + 2, None, :]
    high = zhi.astype(F32)[: Y + 2, None, :]
    scratch[0, slot] = jnp.where(at == 0, low, moved_z(whole, -1)).astype(BF16)
    scratch[2, slot] = jnp.where(at == Z - 1, high, moved_z(whole, 1)).astype(BF16)


def put_own(scratch, slot, center):
    scratch[1, slot, 1 : Y + 1] = center
    whole = center.astype(F32)
    at = lax.broadcasted_iota(jnp.int32, (Y, Z, C), 1)
    scratch[0, slot, 1 : Y + 1] = jnp.where(at == 0, 0.0, moved_z(whole, -1)).astype(BF16)
    scratch[2, slot, 1 : Y + 1] = jnp.where(at == Z - 1, 0.0, moved_z(whole, 1)).astype(BF16)


def patches(shifted, slots):
    pieces = []
    for ty in range(3):
        for tz in range(3):
            pieces.append(shifted[tz, :slots, ty : ty + Y].reshape(slots * ROWS, C))
    return jnp.concatenate(pieces, axis=1)


def put_far(scratch, slot, far_ref, part, side):
    slab = held(far_ref[part], "gx", side)
    rims = slab[Y + 2 :].reshape(-1, C)
    put_slab(scratch, slot, slab[:Y], slab[Y], slab[Y + 1], rims[:24], rims[24:])


def own_grad_kernel(first, more, x_ref, g_ref, *refs):
    total, even, odd = refs[-3:]
    for shifted in (even, odd):
        shifted[:, :, 0:1] = jnp.zeros((3, SPAN, 1, Z, C), BF16)
        shifted[:, :, Y + 1 :] = jnp.zeros((3, SPAN, 1, Z, C), BF16)

    def put(shifted, x):
        for slot in range(SPAN):
            put_own(shifted, slot, x_ref[x + 1 + slot])

    def product(shifted, x):
        columns = [g_ref[x + 2 - tx : x + 2 - tx + SPAN].reshape(SPAN * ROWS, C) for tx in range(3)]
        beside = jnp.concatenate(columns, axis=1)
        return lax.dot_general(patches(shifted, SPAN), beside, DEPTH_FIRST, preferred_element_type=F32)

    put(even, first)
    made = product(even, first)
    put(odd, first + SPAN)
    total[...] = refs[0][...] + made if more else made
    total[...] += product(odd, first + SPAN)


def own_grad(slabs, first, before, tie):
    more = before is not None
    return pl.pallas_call(
        lambda *refs: own_grad_kernel(first, more, *refs),
        in_specs=[VMEM] * (2 + more) + [ANY],
        out_specs=VMEM,
        out_shape=shape((TAPS, WIDE), F32),
        scratch_shapes=[pltpu.VMEM((3, SPAN, Y + 2, Z, C), BF16)] * 2,
        compiler_params=params(),
        cost_estimate=cost(2 * SPAN, 8 << 20),
    )(*slabs, *([before] if more else []), tie)


def add_rim(total, row, stride, trio, face_ref):
    blank = jnp.zeros((1, Z, C), BF16)
    padded = jnp.concatenate([blank, face_ref[1], blank], axis=0)
    around = jnp.concatenate([padded[2 - tx : 2 - tx + X].reshape(X * Z, C) for tx in range(3)], axis=1)
    left = jnp.concatenate([a.astype(BF16).reshape(X * Z, C) for a in trio], axis=1)
    made = lax.dot_general(left, around, DEPTH_FIRST, preferred_element_type=F32)
    for k in range(3):
        start = (row + k * stride) * C
        total[start : start + C] += made[k * C : (k + 1) * C]


def z_rim_kernel(own_ref, gzlo, gzhi, nzlo, nzhi, total):
    total[...] = own_ref[...]
    at = lax.broadcasted_iota(jnp.int32, (X, Z, C), 1)
    for side, row, near, face in ((0, 0, nzlo, gzlo), (1, 2, nzhi, gzhi)):
        whole = held(near[0].astype(F32), "gz", side)
        before = jnp.where(at == 0, 0.0, moved_z(whole, -1))
        after = jnp.where(at == Z - 1, 0.0, moved_z(whole, 1))
        add_rim(total, row, 3, (before, whole, after), face)


def rim_grad_kernel(
    own_ref, g_ref, gylo, gyhi, nylo, nyhi, elo, ehi, far_lo, far_hi, keep_ref, send_ref, scratch, total
):
    total[...] = own_ref[...]
    for side, far, plane, tx in ((0, far_lo, 1, 0), (1, far_hi, X, 2)):
        put_far(scratch.at[:, side : side + 1], 0, far, 0, side)
        left = patches(scratch.at[:, side : side + 1], 1)
        beside = g_ref[plane].reshape(ROWS, C)
        total[:, tx * C : (tx + 1) * C] += lax.dot_general(
            left, beside, DEPTH_FIRST, preferred_element_type=F32
        )
    at = lax.broadcasted_iota(jnp.int32, (X, Z, C), 1)
    for side, row, near, edges, face in ((0, 0, nylo, elo, gylo), (1, 6, nyhi, ehi, gyhi)):
        whole = near[0].astype(F32)
        corners = held(edges[0].astype(F32), "gy", side)
        low = corners[0][:, None, :]
        high = corners[1][:, None, :]
        before = jnp.where(at == 0, low, moved_z(whole, -1))
        after = jnp.where(at == Z - 1, high, moved_z(whole, 1))
        add_rim(total, row, 1, (before, whole, after), face)

    scale = 1.0 / math.sqrt(SHARE * 128 * E**3)
    core = lax.axis_index("gx") % 2
    for mine in range(2):

        @pl.when(core == mine)
        def _():
            for tap in range(27):
                tx, row = tap // 9, tap % 9
                ref = keep_ref if tap // HALF == mine else send_ref
                ref[tap % HALF] = total[row * C : (row + 1) * C, tx * C : (tx + 1) * C] * scale
            ref = keep_ref if mine == 1 else send_ref
            ref[HALF - 1] = jnp.zeros((C, C), F32)


def rim_grad(own, cotangents, operands):
    return pl.pallas_call(
        rim_grad_kernel,
        in_specs=[VMEM] * (2 + len(operands)),
        out_specs=[VMEM, VMEM],
        out_shape=[shape((HALF, C, C), F32)] * 2,
        scratch_shapes=[pltpu.VMEM((3, 2, Y + 2, Z, C), BF16), pltpu.VMEM((TAPS, WIDE), F32)],
        compiler_params=params(),
        cost_estimate=cost(3, 6 << 20),
    )(own, cotangents, *operands)


def conv_kernel(part, first, groups, following, mask_ref, *refs):
    starts, ends = first == 0, first + groups * GROUP == X
    refs = list(refs)
    slabs = [refs.pop(0) for _ in range(2)]
    rims = [refs.pop(0) for _ in range(4)]
    w_ref = refs.pop(0)
    far_lo = refs.pop(0) if starts else None
    far_hi = refs.pop(0) if ends else None
    before = None if starts else refs.pop(0)
    ready = None if starts and part == 0 else refs.pop(0)
    o_ref, carry_ref, even, odd, edge, made_ref, left = refs[-7:]
    count = groups * GROUP

    def put(shifted, at, x):
        for slot in range(GROUP):
            put_slab(shifted, slot, slabs[at][x + 1 + slot], *(ref[at, x + slot] for ref in rims))

    def finish(x, total):
        keep = mask_ref[jnp.maximum(x, 0) // E].astype(F32) > 0.0
        made_ref[x - first + 1] = jnp.where(keep, total.reshape(Y, Z, C), 0.0).astype(BF16)

    def copy(x, size, sem):
        source = made_ref.at[pl.ds(x - first, size)]
        return pltpu.make_async_copy(source, o_ref.at[pl.ds(x - 1, size)], left.at[sem])

    def group(shifted, x, sem, near, next_, opens):
        made = jnp.dot(patches(shifted, GROUP), w_ref[...], preferred_element_type=F32)

        def term(slot, tx):
            return made[slot * ROWS : (slot + 1) * ROWS, tx * C : (tx + 1) * C]

        if opens is not True:
            finish(x - 1, near + term(0, 2))
        finish(x, next_ + term(0, 1) + term(1, 2))
        for slot in range(1, GROUP - 1):
            finish(x + slot, term(slot - 1, 0) + term(slot, 1) + term(slot + 1, 2))
        if opens is None:
            pl.when(sem == 0)(lambda: copy(x + 1, GROUP - 1, sem).start())
            pl.when(sem > 0)(lambda: copy(x, GROUP, sem).start())
        elif opens:
            copy(x + 1, GROUP - 1, sem).start()
        else:
            copy(x, GROUP, sem).start()
        return term(GROUP - 2, 0) + term(GROUP - 1, 1), term(GROUP - 1, 0)

    if starts:
        put_far(edge, 0, far_lo, part, 0)
        near = jnp.zeros((ROWS, C), F32)
        next_ = jnp.dot(patches(edge, 1), w_ref[:, :C], preferred_element_type=F32)
    else:
        near, next_ = before[0], before[1]
    if groups > 2:
        if ready is None:
            put(even, part, 0)
        else:
            even[...] = ready[...]
        carry_ref[0] = near
        carry_ref[1] = next_

        def trip(i, carry):
            x = first + i * 2 * GROUP
            near, next_ = group(even, x, 2 * i, carry_ref[0], carry_ref[1], None if starts else False)
            put(odd, part, x + GROUP)
            near, next_ = group(odd, x + GROUP, 2 * i + 1, near, next_, False)
            after = i + 1 == groups // 2
            then = following[1] if following is not None else X - GROUP
            put(even, part, jnp.where(after, then, x + 2 * GROUP))
            carry_ref[0] = near
            carry_ref[1] = next_
            return carry

        lax.fori_loop(0, groups // 2, trip, 0)
        near = carry_ref[0]
    else:
        if ready is None:
            ready = odd
            put(odd, part, first)
        near, next_ = group(ready, first, 0, near, next_, starts)
        put(even, *following)
        carry_ref[0] = near
        carry_ref[1] = next_
    if ends:
        put_far(edge, 0, far_hi, part, 1)
        last = jnp.dot(patches(edge, 1), w_ref[:, 2 * C :], preferred_element_type=F32)
        finish(X - 1, near + last)
        copy(X, 1, groups).start()
    for sem in range(groups):
        x = first + sem * GROUP
        if starts and sem == 0:
            copy(x + 1, GROUP - 1, sem).wait()
        else:
            copy(x, GROUP, sem).wait()
    if ends:
        copy(X, 1, groups).wait()


def conv_piece(part, first, groups, following, mask, field, far, weight, before, ready, done, tie):
    operands = [mask, *field, weight]
    starts, ends = first == 0, first + groups * GROUP == X
    if starts:
        operands.append(far[0])
    if ends:
        operands.append(far[1])
    if not starts:
        operands.append(before)
    if ready is not None:
        operands.append(ready)
    aliases = {}
    specs = [VMEM] * len(operands)
    operands.append(tie)
    specs.append(ANY)
    if not starts:
        aliases = {len(operands): 0}
        operands.append(done)
        specs.append(ANY)
    shifted = (3, GROUP, Y + 2, Z, C)
    more = following is not None
    buffers = [shape((2, ROWS, C), F32), shape(shifted, BF16)]
    small = shape((8, C), F32)

    scratch = [
        pltpu.VMEM(shifted, BF16),
        pltpu.VMEM((3, 1, Y + 2, Z, C), BF16),
        pltpu.VMEM((groups * GROUP + 1, Y, Z, C), BF16),
        pltpu.SemaphoreType.DMA((groups + 1,)),
    ]
    if not more:
        scratch = [pltpu.VMEM(b.shape, b.dtype) for b in buffers] + scratch

    def plain(*refs):
        conv_kernel(part, first, groups, following, *refs)

    def final(*refs):
        refs[-7][...] = jnp.zeros((8, C), F32)
        conv_kernel(part, first, groups, following, *refs[:-7], *refs[-6:])

    return pl.pallas_call(
        plain if more else final,
        in_specs=specs,
        out_specs=[ANY] + [VMEM] * (2 if more else 1),
        out_shape=[shape((X, Y, Z, C), BF16)] + (buffers if more else [small]),
        scratch_shapes=scratch,
        input_output_aliases=aliases,
        compiler_params=params(),
        cost_estimate=cost(groups * GROUP, 2 << 20),
    )(*operands)


def small_kernel(kernel, out_shape, operands, ties=(), specs=None):
    count = len(operands)

    def run(*refs):
        kernel(*refs[:count], *refs[count + len(ties) :])

    return pl.pallas_call(
        run,
        in_specs=(specs or [VMEM] * count) + [ANY] * len(ties),
        out_specs=jax.tree.map(lambda _: VMEM, out_shape),
        out_shape=out_shape,
        compiler_params=params(),
        cost_estimate=pl.CostEstimate(flops=1000, bytes_accessed=1 << 20, transcendentals=0),
    )(*operands, *ties)


def edge_kernel(zlo, zhi, lo, hi):
    for side, ref in enumerate((zlo, zhi)):
        lo[:, side] = held(ref[:, :, 0, :], "gz", side)
        hi[:, side] = held(ref[:, :, Y - 1, :], "gz", side)


def message_kernel(x_ref, g_ref, ylo, yhi, zlo, zhi, elo, ehi, held_ylo, held_yhi, col_lo, col_hi, to_lo, to_hi):
    held_ylo[...] = held(ylo[...], "gy", 0)
    held_yhi[...] = held(yhi[...], "gy", 1)
    tail = jnp.zeros((2, X, 24 - Y - 2, C), F32)
    for side, (near, col) in enumerate(((zlo, col_lo), (zhi, col_hi))):
        own = held(near[...].astype(F32), "gz", side)
        low = held(elo[:, side].astype(F32), "gy", 0)[:, :, None, :]
        high = held(ehi[:, side].astype(F32), "gy", 1)[:, :, None, :]
        col[...] = jnp.concatenate([low, own, high, tail], axis=2).astype(BF16)
    for at, to in ((0, to_lo), (X - 1, to_hi)):
        to[0, :Y] = x_ref[at + 1]
        to[1, :Y] = g_ref[at + 1]
        to[:, Y] = held_ylo[:, at]
        to[:, Y + 1] = held_yhi[:, at]
        rims = jnp.concatenate([col_lo[:, at], col_hi[:, at]], axis=1)
        to[:, Y + 2 :] = rims.reshape(2, 3, Z, C)


def arrange_kernel(w_ref, forward, flipped):
    for tap in range(27):
        tx, row = tap // 9, tap % 9
        forward[row * C : (row + 1) * C, tx * C : (tx + 1) * C] = w_ref[tap]
        flipped[row * C : (row + 1) * C, tx * C : (tx + 1) * C] = w_ref[26 - tap].astype(F32).T.astype(BF16)


def place(axis):
    at = lax.axis_index(axis)
    return at // 2 if axis == "gx" else at


def pairs(axis, step):
    if axis == "gx":
        return [(2 * z + c, 2 * (z ^ step) + c) for z in range(4) for c in range(2)]
    return [(i, i ^ step) for i in range(4)]


def deal(axis, terms, ties=()):
    rows = terms[0].shape[0] // 4

    def kernel(*refs):
        me = place(axis)
        for step in range(4):
            at = pl.ds((me ^ step) * rows, rows)
            total = refs[0][at]
            for ref in refs[1 : len(terms)]:
                total = total + ref[at]
            refs[len(terms) + step][...] = total

    return small_kernel(kernel, [shape((rows, C), F32)] * 4, terms, ties)


def collect(axis, parts, ties=()):
    rows = parts[0].shape[0]

    def kernel(*refs):
        me = place(axis)
        for step in range(4):
            refs[4][pl.ds((me ^ step) * rows, rows)] = refs[step][...]

    return small_kernel(kernel, shape((4 * rows, C), F32), parts, ties)


def exchange(axis, values):
    return [lax.ppermute(value, axis, pairs(axis, step)) for step, value in zip((1, 2, 3), values, strict=True)]


def sum_kernel(a, b, c, d, o):
    o[...] = (a[...] + c[...]) + (b[...] + d[...])


def write(sources, mine, target, tie):
    arrays = [a for a, _ in sources]
    rows = HALF * C // 4
    short = 27 * C - 2 * HALF * C + rows
    count = sum(len(steps) for _, steps in sources)

    def kernel(*refs):
        o_ref, left = refs[-2:]
        core = lax.axis_index("gx") % 2
        half = core if mine else 1 - core
        me = place("gx")
        for act in ("start", "wait"):
            sem = 0
            for ref, (_, steps) in zip(refs, sources, strict=False):
                for at, step in enumerate(steps):
                    chunk = half * 4 + (me ^ step)

                    def move(size, ref=ref, at=at, chunk=chunk, sem=sem):
                        target = o_ref.at[pl.ds(chunk * rows, size)]
                        copy = pltpu.make_async_copy(ref.at[pl.ds(at * rows, size)], target, left.at[sem])
                        getattr(copy, act)()

                    pl.when(chunk < 7)(lambda move=move: move(rows))
                    pl.when(chunk == 7)(lambda move=move: move(short))
                    sem += 1

    operands = arrays + [tie] + ([] if target is None else [target])
    return pl.pallas_call(
        kernel,
        in_specs=[VMEM] * len(arrays) + [ANY] * (len(operands) - len(arrays)),
        out_specs=ANY,
        out_shape=shape((27 * C, C), F32),
        scratch_shapes=[pltpu.SemaphoreType.DMA((count,))],
        input_output_aliases={} if target is None else {len(operands) - 1: 0},
        compiler_params=params(),
        cost_estimate=pl.CostEstimate(flops=1000, bytes_accessed=1 << 20, transcendentals=0),
    )(*operands)


def join_kernel(a, b, c, o):
    rows = a.shape[0]
    for k, ref in enumerate((a, b, c)):
        o[k * rows : (k + 1) * rows] = ref[...]


def shift(value, axis, step):
    count = lax.axis_size(axis)
    return lax.ppermute(value, axis, [(i, (i + step) % count) for i in range(count)])


def body(features, occupancy, weight, cotangent):
    slabs, mask, faces = prepare(occupancy, features, cotangent)
    zlo, zhi, ylo, yhi = faces
    near_zlo = shift(zhi, "gz", 1)
    near_zhi = shift(zlo, "gz", -1)
    near_ylo = shift(yhi, "gy", 1)
    near_yhi = shift(ylo, "gy", -1)
    own = own_grad(slabs, 0, None, zlo)

    edge = shape((2, 2, X, C), BF16)
    edge_lo, edge_hi = small_kernel(edge_kernel, [edge, edge], [near_zlo, near_zhi], [own])
    edges = (shift(edge_hi, "gy", 1), shift(edge_lo, "gy", -1))
    forward, flipped = small_kernel(
        arrange_kernel, [shape((TAPS, WIDE), BF16)] * 2, [weight.reshape(27, C, C)], [edge_lo]
    )
    own = small_kernel(
        z_rim_kernel, shape((TAPS, WIDE), F32), [own, zlo, zhi, near_zlo, near_zhi], [edge_lo]
    )

    face = shape((2, X, Z, C), BF16)
    column = shape((2, X, 24, C), BF16)
    message = shape((2, Y + 5, Z, C), BF16)
    held_ylo, held_yhi, col_lo, col_hi, to_lo, to_hi = small_kernel(
        message_kernel,
        [face, face, column, column, message, message],
        [*slabs, near_ylo, near_yhi, near_zlo, near_zhi, *edges],
        [forward, own],
    )
    far = (shift(to_hi, "gx", 1), shift(to_lo, "gx", -1))
    own = own_grad(slabs, X // 2, own, to_lo)
    keep, send = rim_grad(own, slabs[1], [ylo, yhi, held_ylo, held_yhi, *edges, *far])

    field = [*slabs, held_ylo, held_yhi, col_lo, col_hi]
    made = [None, None]
    weights = (forward, flipped)
    order = [(0, 0, 1), (0, 4, 6), (0, 28, 1), (1, 0, 1), (1, 4, 1), (1, 8, 6)]
    state = {"carry": None, "ready": None}

    def convolve(tie):
        part, first, groups = order.pop(0)
        following = order[0][:2] if order else None
        made[part], *rest = conv_piece(
            part, first, groups, following, mask, field, far, weights[part],
            state["carry"], state["ready"], made[part], tie,
        )
        if order:
            state["carry"], state["ready"] = rest
        return rest[:1]

    swap = [(i, i ^ 1) for i in range(8)]
    came = lax.ppermute(send, "gx", swap)
    ties = convolve(send)
    flat = (HALF * C, C)
    own, *parts = deal("gx", [keep.reshape(flat), came.reshape(flat)], ties)
    came = exchange("gx", parts)
    ties = convolve(parts[0])
    own, *parts = deal("gy", [own, *came], ties)
    came = exchange("gy", parts)
    ties = convolve(parts[0])
    part_shape = shape(own.shape, F32)
    mine = small_kernel(sum_kernel, part_shape, [own, *came], ties)
    came = exchange("gz", [mine] * 3)
    ties = convolve(mine)
    summed = small_kernel(sum_kernel, part_shape, [mine, *came], ties)
    came = exchange("gy", [summed] * 3)
    ties = convolve(summed)
    chunk = collect("gy", [summed, *came], ties)
    came = exchange("gx", [chunk] * 3)
    beside = lax.ppermute(chunk, "gx", swap)
    (tie,) = convolve(chunk)
    joined = small_kernel(join_kernel, shape((3 * chunk.shape[0], C), F32), came, [tie])
    others = lax.ppermute(joined, "gx", swap)
    full = write([(chunk, (0,)), (joined, (1, 2, 3))], True, None, joined)
    full = write([(beside, (0,))], False, full, joined)
    full = write([(others, (1, 2, 3))], False, full, joined)
    return (made[0], made[1], full.reshape(3, 3, 3, C, C))


def solution(mesh):
    placed = (P("gx", "gy", "gz", None), P("gx", "gy", "gz"), P(), P("gx", "gy", "gz", None))
    return jax.shard_map(
        body,
        mesh=mesh,
        in_specs=placed,
        out_specs=(P("gx", "gy", "gz", None), P("gx", "gy", "gz", None), P()),
        check_vma=False,
    )
```

```python
import math

import jax
import jax.numpy as jnp
from jax import lax
from jax.experimental import pallas as pl
from jax.experimental.pallas import tpu as pltpu
from jax.sharding import PartitionSpec as P

SHARE = 8
X, Y, Z, C = 32, 16, 16, 128
E = 8
ROWS = Y * Z
GROUP = 4
SPAN = 8
TAPS = 9 * C
WIDE = 3 * C
HALF = 14
F32 = jnp.float32
BF16 = jnp.bfloat16
VMEM = pl.BlockSpec(memory_space=pltpu.VMEM)
SMEM = pl.BlockSpec(memory_space=pltpu.SMEM)
ANY = pl.BlockSpec(memory_space=pl.ANY)
DEPTH_FIRST = (((0,), (0,)), ((), ()))


def shape(dims, dtype):
    return jax.ShapeDtypeStruct(dims, dtype)


def params(mebibytes=24):
    return pltpu.CompilerParams(vmem_limit_bytes=mebibytes * 1024 * 1024)


def cost(slabs, moved):
    return pl.CostEstimate(flops=2 * 27 * C * C * slabs * ROWS, bytes_accessed=moved, transcendentals=0)


def inside(axis, side):
    at = lax.axis_index(axis)
    return at > 0 if side == 0 else at < lax.axis_size(axis) - 1


def held(value, axis, side):
    return jnp.where(inside(axis, side), value, jnp.zeros_like(value))


def brick_flags(occ_ref, brick):
    low_z = lax.broadcasted_iota(jnp.int32, (E, Z, C), 1) < E
    halves = [jnp.where(low_z, occ_ref[j, 0, brick], occ_ref[j, 1, brick]) for j in range(2)]
    return jnp.concatenate(halves, axis=0) == 1


def mask_slabs(part, source, mask_ref, s_ref, faces):
    zlo_ref, zhi_ref, ylo_ref, yhi_ref = faces
    for end in (0, X + 1):
        s_ref[end] = jnp.zeros((Y, Z, C), BF16)

    def one(brick, carry):
        span = pl.ds(brick * E, E)
        keep = mask_ref[brick].astype(F32) > 0.0
        value = jnp.where(keep[None], source[span].astype(F32), 0.0).astype(BF16)
        s_ref[pl.ds(brick * E + 1, E)] = value
        zlo_ref[part, span] = value[:, :, 0, :]
        zhi_ref[part, span] = value[:, :, Z - 1, :]
        ylo_ref[part, span] = value[:, 0]
        yhi_ref[part, span] = value[:, Y - 1]
        return carry

    lax.fori_loop(0, X // E, one, 0)


def mask_kernel(occ_ref, mask_ref):
    for brick in range(X // E):
        mask_ref[brick] = jnp.where(brick_flags(occ_ref, brick), 1.0, 0.0).astype(BF16)


def prepare_x_kernel(f_ref, mask_ref, s_ref, *faces):
    mask_slabs(0, f_ref, mask_ref, s_ref, faces)


def prepare_g_kernel(c_ref, mask_ref, *refs):
    given, s_ref, faces = refs[:4], refs[4], refs[5:]
    for face, ref in zip(faces, given, strict=True):
        face[0] = ref[0]
    mask_slabs(1, c_ref, mask_ref, s_ref, faces)


def prepare(occupancy, features, cotangent):
    slabs = shape((X + 2, Y, Z, C), BF16)
    own_cost = pl.CostEstimate(flops=1000000, bytes_accessed=5 << 20, transcendentals=0)
    mask = small_kernel(
        mask_kernel, shape((X // E, Y, Z, C), BF16), [jnp.transpose(occupancy, (1, 2, 0))], specs=[SMEM]
    )
    fields, *given = pl.pallas_call(
        prepare_x_kernel,
        in_specs=[VMEM] * 2,
        out_specs=[VMEM] * 5,
        out_shape=[slabs] + [shape((1, X, Z, C), BF16)] * 4,
        compiler_params=params(),
        cost_estimate=own_cost,
    )(features, mask)
    cotangents, *faces = pl.pallas_call(
        prepare_g_kernel,
        in_specs=[VMEM] * 6,
        out_specs=[VMEM] * 5,
        out_shape=[slabs] + [shape((2, X, Z, C), BF16)] * 4,
        compiler_params=params(),
        cost_estimate=own_cost,
    )(cotangent, mask, *given)
    return (fields, cotangents), mask, faces


def moved_z(whole, step):
    rows = whole.shape[0] * whole.shape[1]
    flat = whole.reshape(rows, C)
    return pltpu.roll(flat, -step % rows, 0).reshape(whole.shape)


def put_slab(scratch, slot, center, ylo, yhi, zlo, zhi):
    whole = jnp.concatenate([ylo[None], center, yhi[None]], axis=0)
    scratch[1, slot] = whole
    whole = whole.astype(F32)
    at = lax.broadcasted_iota(jnp.int32, (Y + 2, Z, C), 1)
    low = zlo.astype(F32)[: Y + 2, None, :]
    high = zhi.astype(F32)[: Y + 2, None, :]
    scratch[0, slot] = jnp.where(at == 0, low, moved_z(whole, -1)).astype(BF16)
    scratch[2, slot] = jnp.where(at == Z - 1, high, moved_z(whole, 1)).astype(BF16)


def put_own(scratch, slot, center):
    scratch[1, slot, 1 : Y + 1] = center
    whole = center.astype(F32)
    at = lax.broadcasted_iota(jnp.int32, (Y, Z, C), 1)
    scratch[0, slot, 1 : Y + 1] = jnp.where(at == 0, 0.0, moved_z(whole, -1)).astype(BF16)
    scratch[2, slot, 1 : Y + 1] = jnp.where(at == Z - 1, 0.0, moved_z(whole, 1)).astype(BF16)


def patches(shifted, slots):
    pieces = []
    for ty in range(3):
        for tz in range(3):
            pieces.append(shifted[tz, :slots, ty : ty + Y].reshape(slots * ROWS, C))
    return jnp.concatenate(pieces, axis=1)


def put_far(scratch, slot, far_ref, part, side):
    slab = held(far_ref[part], "gx", side)
    rims = slab[Y + 2 :].reshape(-1, C)
    put_slab(scratch, slot, slab[:Y], slab[Y], slab[Y + 1], rims[:24], rims[24:])


def own_grad_kernel(first, more, x_ref, g_ref, *refs):
    total, even, odd = refs[-3:]
    for shifted in (even, odd):
        shifted[:, :, 0:1] = jnp.zeros((3, SPAN, 1, Z, C), BF16)
        shifted[:, :, Y + 1 :] = jnp.zeros((3, SPAN, 1, Z, C), BF16)

    def put(shifted, x):
        for slot in range(SPAN):
            put_own(shifted, slot, x_ref[x + 1 + slot])

    def product(shifted, x):
        columns = [g_ref[x + 2 - tx : x + 2 - tx + SPAN].reshape(SPAN * ROWS, C) for tx in range(3)]
        beside = jnp.concatenate(columns, axis=1)
        return lax.dot_general(patches(shifted, SPAN), beside, DEPTH_FIRST, preferred_element_type=F32)

    put(even, first)
    made = product(even, first)
    put(odd, first + SPAN)
    total[...] = refs[0][...] + made if more else made
    total[...] += product(odd, first + SPAN)


def own_grad(slabs, first, before, tie):
    more = before is not None
    return pl.pallas_call(
        lambda *refs: own_grad_kernel(first, more, *refs),
        in_specs=[VMEM] * (2 + more) + [ANY],
        out_specs=VMEM,
        out_shape=shape((TAPS, WIDE), F32),
        scratch_shapes=[pltpu.VMEM((3, SPAN, Y + 2, Z, C), BF16)] * 2,
        compiler_params=params(),
        cost_estimate=cost(2 * SPAN, 8 << 20),
    )(*slabs, *([before] if more else []), tie)


def add_rim(total, row, stride, trio, face_ref):
    blank = jnp.zeros((1, Z, C), BF16)
    padded = jnp.concatenate([blank, face_ref[1], blank], axis=0)
    around = jnp.concatenate([padded[2 - tx : 2 - tx + X].reshape(X * Z, C) for tx in range(3)], axis=1)
    left = jnp.concatenate([a.astype(BF16).reshape(X * Z, C) for a in trio], axis=1)
    made = lax.dot_general(left, around, DEPTH_FIRST, preferred_element_type=F32)
    for k in range(3):
        start = (row + k * stride) * C
        total[start : start + C] += made[k * C : (k + 1) * C]


def z_rim_kernel(own_ref, gzlo, gzhi, nzlo, nzhi, total):
    total[...] = own_ref[...]
    at = lax.broadcasted_iota(jnp.int32, (X, Z, C), 1)
    for side, row, near, face in ((0, 0, nzlo, gzlo), (1, 2, nzhi, gzhi)):
        whole = held(near[0].astype(F32), "gz", side)
        before = jnp.where(at == 0, 0.0, moved_z(whole, -1))
        after = jnp.where(at == Z - 1, 0.0, moved_z(whole, 1))
        add_rim(total, row, 3, (before, whole, after), face)


def rim_grad_kernel(
    own_ref, g_ref, gylo, gyhi, nylo, nyhi, elo, ehi, far_lo, far_hi, keep_ref, send_ref, scratch, total
):
    total[...] = own_ref[...]
    for side, far, plane, tx in ((0, far_lo, 1, 0), (1, far_hi, X, 2)):
        put_far(scratch.at[:, side : side + 1], 0, far, 0, side)
        left = patches(scratch.at[:, side : side + 1], 1)
        beside = g_ref[plane].reshape(ROWS, C)
        total[:, tx * C : (tx + 1) * C] += lax.dot_general(
            left, beside, DEPTH_FIRST, preferred_element_type=F32
        )
    at = lax.broadcasted_iota(jnp.int32, (X, Z, C), 1)
    for side, row, near, edges, face in ((0, 0, nylo, elo, gylo), (1, 6, nyhi, ehi, gyhi)):
        whole = near[0].astype(F32)
        corners = held(edges[0].astype(F32), "gy", side)
        low = corners[0][:, None, :]
        high = corners[1][:, None, :]
        before = jnp.where(at == 0, low, moved_z(whole, -1))
        after = jnp.where(at == Z - 1, high, moved_z(whole, 1))
        add_rim(total, row, 1, (before, whole, after), face)

    scale = 1.0 / math.sqrt(SHARE * 128 * E**3)
    core = lax.axis_index("gx") % 2
    for mine in range(2):

        @pl.when(core == mine)
        def _():
            for tap in range(27):
                tx, row = tap // 9, tap % 9
                ref = keep_ref if tap // HALF == mine else send_ref
                ref[tap % HALF] = total[row * C : (row + 1) * C, tx * C : (tx + 1) * C] * scale
            ref = keep_ref if mine == 1 else send_ref
            ref[HALF - 1] = jnp.zeros((C, C), F32)


def rim_grad(own, cotangents, operands):
    return pl.pallas_call(
        rim_grad_kernel,
        in_specs=[VMEM] * (2 + len(operands)),
        out_specs=[VMEM, VMEM],
        out_shape=[shape((HALF, C, C), F32)] * 2,
        scratch_shapes=[pltpu.VMEM((3, 2, Y + 2, Z, C), BF16), pltpu.VMEM((TAPS, WIDE), F32)],
        compiler_params=params(),
        cost_estimate=cost(3, 6 << 20),
    )(own, cotangents, *operands)


def conv_kernel(part, first, groups, following, mask_ref, *refs):
    starts, ends = first == 0, first + groups * GROUP == X
    refs = list(refs)
    slabs = [refs.pop(0) for _ in range(2)]
    rims = [refs.pop(0) for _ in range(4)]
    w_ref = refs.pop(0)
    far_lo = refs.pop(0) if starts else None
    far_hi = refs.pop(0) if ends else None
    before = None if starts else refs.pop(0)
    late_in = None if starts else refs.pop(0)
    ready = None if starts and part == 0 else refs.pop(0)
    late = None if ends else refs.pop(-5)
    o_ref, carry_ref, even, odd, edge, made_ref, left = refs[-7:]
    count = groups * GROUP
    own_copies = groups if ends else groups - 1
    late_copy = None
    if not starts:
        late_copy = pltpu.make_async_copy(late_in, o_ref.at[pl.ds(first - GROUP - 1, GROUP)], left.at[groups + 1])
        late_copy.start()

    def put(shifted, at, x):
        for slot in range(GROUP):
            put_slab(shifted, slot, slabs[at][x + 1 + slot], *(ref[at, x + slot] for ref in rims))

    def finish(x, total):
        keep = mask_ref[jnp.maximum(x, 0) // E].astype(F32) > 0.0
        made_ref[x - first + 1] = jnp.where(keep, total.reshape(Y, Z, C), 0.0).astype(BF16)

    def copy(x, size, sem):
        source = made_ref.at[pl.ds(x - first, size)]
        return pltpu.make_async_copy(source, o_ref.at[pl.ds(x - 1, size)], left.at[sem])

    def group(shifted, x, sem, near, next_, opens):
        made = jnp.dot(patches(shifted, GROUP), w_ref[...], preferred_element_type=F32)

        def term(slot, tx):
            return made[slot * ROWS : (slot + 1) * ROWS, tx * C : (tx + 1) * C]

        if opens is not True:
            finish(x - 1, near + term(0, 2))
        finish(x, next_ + term(0, 1) + term(1, 2))
        for slot in range(1, GROUP - 1):
            finish(x + slot, term(slot - 1, 0) + term(slot, 1) + term(slot + 1, 2))
        if opens:
            copy(x + 1, GROUP - 1, sem).start()
        elif ends:
            copy(x, GROUP, sem).start()
        else:
            pl.when(sem < own_copies)(lambda: copy(x, GROUP, sem).start())
        return term(GROUP - 2, 0) + term(GROUP - 1, 1), term(GROUP - 1, 0)

    if starts:
        put_far(edge, 0, far_lo, part, 0)
        near = jnp.zeros((ROWS, C), F32)
        next_ = jnp.dot(patches(edge, 1), w_ref[:, :C], preferred_element_type=F32)
    else:
        near, next_ = before[0], before[1]
    if groups > 2:
        even[...] = ready[...]
        carry_ref[0] = near
        carry_ref[1] = next_

        def trip(i, carry):
            x = first + i * 2 * GROUP
            near, next_ = group(even, x, 2 * i, carry_ref[0], carry_ref[1], False)
            put(odd, part, x + GROUP)
            near, next_ = group(odd, x + GROUP, 2 * i + 1, near, next_, False)
            after = i + 1 == groups // 2
            then = following[1] if following is not None else X - GROUP
            put(even, part, jnp.where(after, then, x + 2 * GROUP))
            carry_ref[0] = near
            carry_ref[1] = next_
            return carry

        lax.fori_loop(0, groups // 2, trip, 0)
        near = carry_ref[0]
    else:
        if ready is None:
            ready = even
            put(even, part, first)
        near, next_ = group(ready, first, 0, near, next_, starts)
        put(odd, part, first + GROUP)
        near, next_ = group(odd, first + GROUP, 1, near, next_, False)
        put(even, *following)
        carry_ref[0] = near
        carry_ref[1] = next_
    if ends:
        put_far(edge, 0, far_hi, part, 1)
        last = jnp.dot(patches(edge, 1), w_ref[:, 2 * C :], preferred_element_type=F32)
        finish(X - 1, near + last)
        copy(X, 1, groups).start()
    if late is not None:
        late[...] = made_ref[count - GROUP : count]
    for sem in range(own_copies):
        x = first + sem * GROUP
        if starts and sem == 0:
            copy(x + 1, GROUP - 1, sem).wait()
        else:
            copy(x, GROUP, sem).wait()
    if ends:
        copy(X, 1, groups).wait()
    if late_copy is not None:
        late_copy.wait()


def conv_piece(part, first, groups, following, mask, field, far, weight, state, done, tie):
    operands = [mask, *field, weight]
    starts, ends = first == 0, first + groups * GROUP == X
    if starts:
        operands.append(far[0])
    if ends:
        operands.append(far[1])
    if not starts:
        operands += [state["carry"], state["late"]]
    if "ready" in state:
        operands.append(state["ready"])
    aliases = {}
    specs = [VMEM] * len(operands)
    operands.append(tie)
    specs.append(ANY)
    if not starts:
        aliases = {len(operands): 0}
        operands.append(done)
        specs.append(ANY)
    shifted = (3, GROUP, Y + 2, Z, C)
    more = following is not None
    buffers = [shape((2, ROWS, C), F32), shape(shifted, BF16)]
    kept = buffers + ([] if ends else [shape((GROUP, Y, Z, C), BF16)])
    scratch = [
        pltpu.VMEM(shifted, BF16),
        pltpu.VMEM((3, 1, Y + 2, Z, C), BF16),
        pltpu.VMEM((groups * GROUP + 1, Y, Z, C), BF16),
        pltpu.SemaphoreType.DMA((groups + 2,)),
    ]
    if not more:
        scratch = [pltpu.VMEM(b.shape, b.dtype) for b in buffers] + scratch
        kept = [shape((8, C), F32)]

    def plain(*refs):
        conv_kernel(part, first, groups, following, *refs)

    def final(*refs):
        refs[-7][...] = jnp.zeros((8, C), F32)
        conv_kernel(part, first, groups, following, *refs[:-7], *refs[-6:])

    made, *kept = pl.pallas_call(
        plain if more else final,
        in_specs=specs,
        out_specs=[ANY] + [VMEM] * len(kept),
        out_shape=[shape((X, Y, Z, C), BF16)] + kept,
        scratch_shapes=scratch,
        input_output_aliases=aliases,
        compiler_params=params(),
        cost_estimate=cost(groups * GROUP, 2 << 20),
    )(*operands)
    return made, dict(zip(("carry", "ready", "late"), kept, strict=False))


def small_kernel(kernel, out_shape, operands, ties=(), specs=None):
    count = len(operands)

    def run(*refs):
        kernel(*refs[:count], *refs[count + len(ties) :])

    return pl.pallas_call(
        run,
        in_specs=(specs or [VMEM] * count) + [ANY] * len(ties),
        out_specs=jax.tree.map(lambda _: VMEM, out_shape),
        out_shape=out_shape,
        compiler_params=params(),
        cost_estimate=pl.CostEstimate(flops=1000, bytes_accessed=1 << 20, transcendentals=0),
    )(*operands, *ties)


def edge_kernel(zlo, zhi, lo, hi):
    for side, ref in enumerate((zlo, zhi)):
        lo[:, side] = held(ref[:, :, 0, :], "gz", side)
        hi[:, side] = held(ref[:, :, Y - 1, :], "gz", side)


def message_kernel(x_ref, g_ref, ylo, yhi, zlo, zhi, elo, ehi, held_ylo, held_yhi, col_lo, col_hi, to_lo, to_hi):
    held_ylo[...] = held(ylo[...], "gy", 0)
    held_yhi[...] = held(yhi[...], "gy", 1)
    tail = jnp.zeros((2, X, 24 - Y - 2, C), F32)
    for side, (near, col) in enumerate(((zlo, col_lo), (zhi, col_hi))):
        own = held(near[...].astype(F32), "gz", side)
        low = held(elo[:, side].astype(F32), "gy", 0)[:, :, None, :]
        high = held(ehi[:, side].astype(F32), "gy", 1)[:, :, None, :]
        col[...] = jnp.concatenate([low, own, high, tail], axis=2).astype(BF16)
    for at, to in ((0, to_lo), (X - 1, to_hi)):
        to[0, :Y] = x_ref[at + 1]
        to[1, :Y] = g_ref[at + 1]
        to[:, Y] = held_ylo[:, at]
        to[:, Y + 1] = held_yhi[:, at]
        rims = jnp.concatenate([col_lo[:, at], col_hi[:, at]], axis=1)
        to[:, Y + 2 :] = rims.reshape(2, 3, Z, C)


def arrange_kernel(w_ref, forward, flipped):
    for tap in range(27):
        tx, row = tap // 9, tap % 9
        forward[row * C : (row + 1) * C, tx * C : (tx + 1) * C] = w_ref[tap]
        flipped[row * C : (row + 1) * C, tx * C : (tx + 1) * C] = w_ref[26 - tap].astype(F32).T.astype(BF16)


def places():
    at = lax.axis_index("gx")
    core, z, y = at % 2, at // 2, lax.axis_index("gy")
    return core, z * (1 - core) + y * core, y * (1 - core) + z * core


def pairs(turn, step):
    found = []
    for z in range(4):
        for core in range(2):
            for y in range(4):
                along_z = (turn == 1) == (core == 0)
                partner = (z ^ step, y) if along_z else (z, y ^ step)
                found.append(((2 * z + core) * 4 + y, (2 * partner[0] + core) * 4 + partner[1]))
    return found


def exchange(turn, values):
    steps = zip((1, 2, 3), values, strict=True)
    if turn == 3:
        return [lax.ppermute(value, "gz", [(i, i ^ step) for i in range(4)]) for step, value in steps]
    return [lax.ppermute(value, ("gx", "gy"), pairs(turn, step)) for step, value in steps]


def deal(turn, terms, ties=()):
    rows = terms[0].shape[0] // 4

    def kernel(*refs):
        me = places()[turn]
        for step in range(4):
            at = pl.ds((me ^ step) * rows, rows)
            total = refs[0][at]
            for ref in refs[1 : len(terms)]:
                total = total + ref[at]
            refs[len(terms) + step][...] = total

    return small_kernel(kernel, [shape((rows, C), F32)] * 4, terms, ties)


def collect(turn, parts, ties=()):
    rows = parts[0].shape[0]

    def kernel(*refs):
        me = places()[turn]
        for step in range(4):
            refs[4][pl.ds((me ^ step) * rows, rows)] = refs[step][...]

    return small_kernel(kernel, shape((4 * rows, C), F32), parts, ties)


def sum_kernel(a, b, c, d, o):
    o[...] = (a[...] + c[...]) + (b[...] + d[...])


def write(sources, mine, target, tie):
    arrays = [a for a, _ in sources]
    rows = HALF * C // 4
    short = 27 * C - 2 * HALF * C + rows
    count = sum(len(steps) for _, steps in sources)

    def kernel(*refs):
        o_ref, left = refs[-2:]
        at = lax.axis_index("gx")
        half = at % 2 if mine else 1 - at % 2
        me = at // 2 * (1 - half) + lax.axis_index("gy") * half
        for act in ("start", "wait"):
            sem = 0
            for ref, (_, steps) in zip(refs, sources, strict=False):
                for at, step in enumerate(steps):
                    chunk = half * 4 + (me ^ step)

                    def move(size, ref=ref, at=at, chunk=chunk, sem=sem):
                        target = o_ref.at[pl.ds(chunk * rows, size)]
                        copy = pltpu.make_async_copy(ref.at[pl.ds(at * rows, size)], target, left.at[sem])
                        getattr(copy, act)()

                    pl.when(chunk < 7)(lambda move=move: move(rows))
                    pl.when(chunk == 7)(lambda move=move: move(short))
                    sem += 1

    operands = arrays + [tie] + ([] if target is None else [target])
    return pl.pallas_call(
        kernel,
        in_specs=[VMEM] * len(arrays) + [ANY] * (len(operands) - len(arrays)),
        out_specs=ANY,
        out_shape=shape((27 * C, C), F32),
        scratch_shapes=[pltpu.SemaphoreType.DMA((count,))],
        input_output_aliases={} if target is None else {len(operands) - 1: 0},
        compiler_params=params(),
        cost_estimate=pl.CostEstimate(flops=1000, bytes_accessed=1 << 20, transcendentals=0),
    )(*operands)


def join_kernel(a, b, c, o):
    rows = a.shape[0]
    for k, ref in enumerate((a, b, c)):
        o[k * rows : (k + 1) * rows] = ref[...]


def shift(value, axis, step):
    count = lax.axis_size(axis)
    return lax.ppermute(value, axis, [(i, (i + step) % count) for i in range(count)])


def body(features, occupancy, weight, cotangent):
    slabs, mask, faces = prepare(occupancy, features, cotangent)
    zlo, zhi, ylo, yhi = faces
    near_zlo = shift(zhi, "gz", 1)
    near_zhi = shift(zlo, "gz", -1)
    near_ylo = shift(yhi, "gy", 1)
    near_yhi = shift(ylo, "gy", -1)
    own = own_grad(slabs, 0, None, zlo)

    edge = shape((2, 2, X, C), BF16)
    edge_lo, edge_hi = small_kernel(edge_kernel, [edge, edge], [near_zlo, near_zhi], [own])
    edges = (shift(edge_hi, "gy", 1), shift(edge_lo, "gy", -1))
    forward, flipped = small_kernel(
        arrange_kernel, [shape((TAPS, WIDE), BF16)] * 2, [weight.reshape(27, C, C)], [edge_lo]
    )
    own = small_kernel(
        z_rim_kernel, shape((TAPS, WIDE), F32), [own, zlo, zhi, near_zlo, near_zhi], [edge_lo]
    )

    face = shape((2, X, Z, C), BF16)
    column = shape((2, X, 24, C), BF16)
    message = shape((2, Y + 5, Z, C), BF16)
    held_ylo, held_yhi, col_lo, col_hi, to_lo, to_hi = small_kernel(
        message_kernel,
        [face, face, column, column, message, message],
        [*slabs, near_ylo, near_yhi, near_zlo, near_zhi, *edges],
        [forward, own],
    )
    far = (shift(to_hi, "gx", 1), shift(to_lo, "gx", -1))
    own = own_grad(slabs, X // 2, own, to_lo)
    keep, send = rim_grad(own, slabs[1], [ylo, yhi, held_ylo, held_yhi, *edges, *far])

    field = [*slabs, held_ylo, held_yhi, col_lo, col_hi]
    made = [None, None]
    weights = (forward, flipped)
    order = [(0, 0, 2), (0, 8, 4), (0, 24, 2), (1, 0, 2), (1, 8, 2), (1, 16, 4)]
    state = {}

    def convolve(tie):
        part, first, groups = order.pop(0)
        following = order[0][:2] if order else None
        made[part], kept = conv_piece(
            part, first, groups, following, mask, field, far, weights[part], state, made[part], tie
        )
        state.update(kept)
        return [kept["carry"]]

    swap = [(i, i ^ 1) for i in range(8)]
    came = lax.ppermute(send, "gx", swap)
    ties = convolve(send)
    flat = (HALF * C, C)
    own, *parts = deal(1, [keep.reshape(flat), came.reshape(flat)], ties)
    came = exchange(1, parts)
    ties = convolve(parts[0])
    own, *parts = deal(2, [own, *came], ties)
    came = exchange(2, parts)
    ties = convolve(parts[0])
    part_shape = shape(own.shape, F32)
    mine = small_kernel(sum_kernel, part_shape, [own, *came], ties)
    came = exchange(3, [mine] * 3)
    ties = convolve(mine)
    summed = small_kernel(sum_kernel, part_shape, [mine, *came], ties)
    came = exchange(2, [summed] * 3)
    ties = convolve(summed)
    chunk = collect(2, [summed, *came], ties)
    came = exchange(1, [chunk] * 3)
    beside = lax.ppermute(chunk, "gx", swap)
    ties = convolve(chunk)
    joined = small_kernel(join_kernel, shape((3 * chunk.shape[0], C), F32), came, [beside, *ties])
    others = lax.ppermute(joined, "gx", swap)
    full = write([(chunk, (0,)), (joined, (1, 2, 3))], True, None, joined)
    full = write([(beside, (0,))], False, full, joined)
    full = write([(others, (1, 2, 3))], False, full, joined)
    return (made[0], made[1], full.reshape(3, 3, 3, C, C))


def solution(mesh):
    placed = (P("gx", "gy", "gz", None), P("gx", "gy", "gz"), P(), P("gx", "gy", "gz", None))
    return jax.shard_map(
        body,
        mesh=mesh,
        in_specs=placed,
        out_specs=(P("gx", "gy", "gz", None), P("gx", "gy", "gz", None), P()),
        check_vma=False,
    )
```

```python
import math

import jax
import jax.numpy as jnp
from jax import lax
from jax.experimental import pallas as pl
from jax.experimental.pallas import tpu as pltpu
from jax.sharding import PartitionSpec as P

SHARE = 8
X, Y, Z, C = 32, 16, 16, 128
E = 8
ROWS = Y * Z
GROUP = 4
SPAN = 8
TAPS = 9 * C
WIDE = 3 * C
HALF = 14
F32 = jnp.float32
BF16 = jnp.bfloat16
VMEM = pl.BlockSpec(memory_space=pltpu.VMEM)
SMEM = pl.BlockSpec(memory_space=pltpu.SMEM)
ANY = pl.BlockSpec(memory_space=pl.ANY)
DEPTH_FIRST = (((0,), (0,)), ((), ()))


def shape(dims, dtype):
    return jax.ShapeDtypeStruct(dims, dtype)


def params(mebibytes=24):
    return pltpu.CompilerParams(vmem_limit_bytes=mebibytes * 1024 * 1024)


def cost(slabs, moved):
    return pl.CostEstimate(flops=2 * 27 * C * C * slabs * ROWS, bytes_accessed=moved, transcendentals=0)


def inside(axis, side):
    at = lax.axis_index(axis)
    return at > 0 if side == 0 else at < lax.axis_size(axis) - 1


def held(value, axis, side):
    return jnp.where(inside(axis, side), value, jnp.zeros_like(value))


def brick_flags(occ_ref, brick):
    low_z = lax.broadcasted_iota(jnp.int32, (E, Z, C), 1) < E
    halves = [jnp.where(low_z, occ_ref[j, 0, brick], occ_ref[j, 1, brick]) for j in range(2)]
    return jnp.concatenate(halves, axis=0) == 1


def mask_slabs(part, source, mask_ref, s_ref, faces):
    zlo_ref, zhi_ref, ylo_ref, yhi_ref = faces
    for end in (0, X + 1):
        s_ref[end] = jnp.zeros((Y, Z, C), BF16)

    def one(brick, carry):
        span = pl.ds(brick * E, E)
        keep = mask_ref[brick].astype(F32) > 0.0
        value = jnp.where(keep[None], source[span].astype(F32), 0.0).astype(BF16)
        s_ref[pl.ds(brick * E + 1, E)] = value
        zlo_ref[part, span] = value[:, :, 0, :]
        zhi_ref[part, span] = value[:, :, Z - 1, :]
        ylo_ref[part, span] = value[:, 0]
        yhi_ref[part, span] = value[:, Y - 1]
        return carry

    lax.fori_loop(0, X // E, one, 0)


def mask_kernel(occ_ref, mask_ref):
    for brick in range(X // E):
        mask_ref[brick] = jnp.where(brick_flags(occ_ref, brick), 1.0, 0.0).astype(BF16)


def prepare_x_kernel(f_ref, mask_ref, s_ref, *faces):
    mask_slabs(0, f_ref, mask_ref, s_ref, faces)


def prepare_g_kernel(c_ref, mask_ref, *refs):
    given, s_ref, faces = refs[:4], refs[4], refs[5:]
    for face, ref in zip(faces, given, strict=True):
        face[0] = ref[0]
    mask_slabs(1, c_ref, mask_ref, s_ref, faces)


def prepare(occupancy, features, cotangent):
    slabs = shape((X + 2, Y, Z, C), BF16)
    own_cost = pl.CostEstimate(flops=1000000, bytes_accessed=5 << 20, transcendentals=0)
    mask = small_kernel(
        mask_kernel, shape((X // E, Y, Z, C), BF16), [jnp.transpose(occupancy, (1, 2, 0))], specs=[SMEM],
        moved=16 << 20,
    )
    fields, *given = pl.pallas_call(
        prepare_x_kernel,
        in_specs=[VMEM] * 2,
        out_specs=[VMEM] * 5,
        out_shape=[slabs] + [shape((1, X, Z, C), BF16)] * 4,
        compiler_params=params(),
        cost_estimate=own_cost,
    )(features, mask)
    cotangents, *faces = pl.pallas_call(
        prepare_g_kernel,
        in_specs=[VMEM] * 6,
        out_specs=[VMEM] * 5,
        out_shape=[slabs] + [shape((2, X, Z, C), BF16)] * 4,
        compiler_params=params(),
        cost_estimate=own_cost,
    )(cotangent, mask, *given)
    return (fields, cotangents), mask, faces


def moved_z(whole, step):
    rows = whole.shape[0] * whole.shape[1]
    flat = whole.reshape(rows, C)
    return pltpu.roll(flat, -step % rows, 0).reshape(whole.shape)


def put_slab(scratch, slot, center, ylo, yhi, zlo, zhi):
    whole = jnp.concatenate([ylo[None], center, yhi[None]], axis=0)
    scratch[1, slot] = whole
    whole = whole.astype(F32)
    at = lax.broadcasted_iota(jnp.int32, (Y + 2, Z, C), 1)
    low = zlo.astype(F32)[: Y + 2, None, :]
    high = zhi.astype(F32)[: Y + 2, None, :]
    scratch[0, slot] = jnp.where(at == 0, low, moved_z(whole, -1)).astype(BF16)
    scratch[2, slot] = jnp.where(at == Z - 1, high, moved_z(whole, 1)).astype(BF16)


def put_own(scratch, slot, center):
    scratch[1, slot, 1 : Y + 1] = center
    whole = center.astype(F32)
    at = lax.broadcasted_iota(jnp.int32, (Y, Z, C), 1)
    scratch[0, slot, 1 : Y + 1] = jnp.where(at == 0, 0.0, moved_z(whole, -1)).astype(BF16)
    scratch[2, slot, 1 : Y + 1] = jnp.where(at == Z - 1, 0.0, moved_z(whole, 1)).astype(BF16)


def patches(shifted, slots):
    pieces = []
    for ty in range(3):
        for tz in range(3):
            pieces.append(shifted[tz, :slots, ty : ty + Y].reshape(slots * ROWS, C))
    return jnp.concatenate(pieces, axis=1)


def put_far(scratch, slot, far_ref, part, side):
    slab = held(far_ref[part], "gx", side)
    rims = slab[Y + 2 :].reshape(-1, C)
    put_slab(scratch, slot, slab[:Y], slab[Y], slab[Y + 1], rims[:24], rims[24:])


def own_grad_kernel(first, more, x_ref, g_ref, *refs):
    total, even, odd = refs[-3:]
    for shifted in (even, odd):
        shifted[:, :, 0:1] = jnp.zeros((3, SPAN, 1, Z, C), BF16)
        shifted[:, :, Y + 1 :] = jnp.zeros((3, SPAN, 1, Z, C), BF16)

    def put(shifted, x):
        for slot in range(SPAN):
            put_own(shifted, slot, x_ref[x + 1 + slot])

    def product(shifted, x):
        columns = [g_ref[x + 2 - tx : x + 2 - tx + SPAN].reshape(SPAN * ROWS, C) for tx in range(3)]
        beside = jnp.concatenate(columns, axis=1)
        return lax.dot_general(patches(shifted, SPAN), beside, DEPTH_FIRST, preferred_element_type=F32)

    put(even, first)
    made = product(even, first)
    put(odd, first + SPAN)
    total[...] = refs[0][...] + made if more else made
    total[...] += product(odd, first + SPAN)


def own_grad(slabs, first, before, tie):
    more = before is not None
    return pl.pallas_call(
        lambda *refs: own_grad_kernel(first, more, *refs),
        in_specs=[VMEM] * (2 + more) + [ANY],
        out_specs=VMEM,
        out_shape=shape((TAPS, WIDE), F32),
        scratch_shapes=[pltpu.VMEM((3, SPAN, Y + 2, Z, C), BF16)] * 2,
        compiler_params=params(),
        cost_estimate=cost(2 * SPAN, 8 << 20),
    )(*slabs, *([before] if more else []), tie)


def add_rim(total, row, stride, trio, face_ref):
    blank = jnp.zeros((1, Z, C), BF16)
    padded = jnp.concatenate([blank, face_ref[1], blank], axis=0)
    around = jnp.concatenate([padded[2 - tx : 2 - tx + X].reshape(X * Z, C) for tx in range(3)], axis=1)
    left = jnp.concatenate([a.astype(BF16).reshape(X * Z, C) for a in trio], axis=1)
    made = lax.dot_general(left, around, DEPTH_FIRST, preferred_element_type=F32)
    for k in range(3):
        start = (row + k * stride) * C
        total[start : start + C] += made[k * C : (k + 1) * C]


def z_rim_kernel(own_ref, gzlo, gzhi, nzlo, nzhi, total):
    total[...] = own_ref[...]
    at = lax.broadcasted_iota(jnp.int32, (X, Z, C), 1)
    for side, row, near, face in ((0, 0, nzlo, gzlo), (1, 2, nzhi, gzhi)):
        whole = held(near[0].astype(F32), "gz", side)
        before = jnp.where(at == 0, 0.0, moved_z(whole, -1))
        after = jnp.where(at == Z - 1, 0.0, moved_z(whole, 1))
        add_rim(total, row, 3, (before, whole, after), face)


def rim_grad_kernel(
    own_ref, g_ref, gylo, gyhi, nylo, nyhi, elo, ehi, far_lo, far_hi, keep_ref, send_ref, scratch, total
):
    total[...] = own_ref[...]
    for side, far, plane, tx in ((0, far_lo, 1, 0), (1, far_hi, X, 2)):
        put_far(scratch.at[:, side : side + 1], 0, far, 0, side)
        left = patches(scratch.at[:, side : side + 1], 1)
        beside = g_ref[plane].reshape(ROWS, C)
        total[:, tx * C : (tx + 1) * C] += lax.dot_general(
            left, beside, DEPTH_FIRST, preferred_element_type=F32
        )
    at = lax.broadcasted_iota(jnp.int32, (X, Z, C), 1)
    for side, row, near, edges, face in ((0, 0, nylo, elo, gylo), (1, 6, nyhi, ehi, gyhi)):
        whole = near[0].astype(F32)
        corners = held(edges[0].astype(F32), "gy", side)
        low = corners[0][:, None, :]
        high = corners[1][:, None, :]
        before = jnp.where(at == 0, low, moved_z(whole, -1))
        after = jnp.where(at == Z - 1, high, moved_z(whole, 1))
        add_rim(total, row, 1, (before, whole, after), face)

    scale = 1.0 / math.sqrt(SHARE * 128 * E**3)
    core = lax.axis_index("gx") % 2
    for mine in range(2):

        @pl.when(core == mine)
        def _():
            for tap in range(27):
                tx, row = tap // 9, tap % 9
                ref = keep_ref if tap // HALF == mine else send_ref
                ref[tap % HALF] = total[row * C : (row + 1) * C, tx * C : (tx + 1) * C] * scale
            ref = keep_ref if mine == 1 else send_ref
            ref[HALF - 1] = jnp.zeros((C, C), F32)


def rim_grad(own, cotangents, operands):
    return pl.pallas_call(
        rim_grad_kernel,
        in_specs=[VMEM] * (2 + len(operands)),
        out_specs=[VMEM, VMEM],
        out_shape=[shape((HALF, C, C), F32)] * 2,
        scratch_shapes=[pltpu.VMEM((3, 2, Y + 2, Z, C), BF16), pltpu.VMEM((TAPS, WIDE), F32)],
        compiler_params=params(),
        cost_estimate=cost(3, 6 << 20),
    )(own, cotangents, *operands)


def conv_kernel(part, first, groups, following, mask_ref, *refs):
    starts, ends = first == 0, first + groups * GROUP == X
    refs = list(refs)
    slabs = [refs.pop(0) for _ in range(2)]
    rims = [refs.pop(0) for _ in range(4)]
    w_ref = refs.pop(0)
    far_lo = refs.pop(0) if starts else None
    far_hi = refs.pop(0) if ends else None
    before = None if starts else refs.pop(0)
    late_in = None if starts else refs.pop(0)
    ready = None if starts and part == 0 else refs.pop(0)
    late = None if ends else refs.pop(-5)
    o_ref, carry_ref, even, odd, edge, made_ref, left = refs[-7:]
    count = groups * GROUP
    own_copies = groups if ends else groups - 1
    late_copy = None
    if not starts:
        late_copy = pltpu.make_async_copy(late_in, o_ref.at[pl.ds(first - GROUP - 1, GROUP)], left.at[groups + 1])
        late_copy.start()

    def put(shifted, at, x):
        for slot in range(GROUP):
            put_slab(shifted, slot, slabs[at][x + 1 + slot], *(ref[at, x + slot] for ref in rims))

    def finish(x, total):
        keep = mask_ref[jnp.maximum(x, 0) // E].astype(F32) > 0.0
        made_ref[x - first + 1] = jnp.where(keep, total.reshape(Y, Z, C), 0.0).astype(BF16)

    def copy(x, size, sem):
        source = made_ref.at[pl.ds(x - first, size)]
        return pltpu.make_async_copy(source, o_ref.at[pl.ds(x - 1, size)], left.at[sem])

    def group(shifted, x, sem, near, next_, opens):
        made = jnp.dot(patches(shifted, GROUP), w_ref[...], preferred_element_type=F32)

        def term(slot, tx):
            return made[slot * ROWS : (slot + 1) * ROWS, tx * C : (tx + 1) * C]

        if opens is not True:
            finish(x - 1, near + term(0, 2))
        finish(x, next_ + term(0, 1) + term(1, 2))
        for slot in range(1, GROUP - 1):
            finish(x + slot, term(slot - 1, 0) + term(slot, 1) + term(slot + 1, 2))
        if opens is None:
            pl.when(sem == 0)(lambda: copy(x + 1, GROUP - 1, sem).start())
            pl.when(sem > 0)(lambda: copy(x, GROUP, sem).start())
        elif opens:
            copy(x + 1, GROUP - 1, sem).start()
        elif ends:
            copy(x, GROUP, sem).start()
        else:
            pl.when(sem < own_copies)(lambda: copy(x, GROUP, sem).start())
        return term(GROUP - 2, 0) + term(GROUP - 1, 1), term(GROUP - 1, 0)

    if starts:
        put_far(edge, 0, far_lo, part, 0)
        near = jnp.zeros((ROWS, C), F32)
        next_ = jnp.dot(patches(edge, 1), w_ref[:, :C], preferred_element_type=F32)
    else:
        near, next_ = before[0], before[1]
    if groups > 2:
        if ready is None:
            put(even, part, 0)
        else:
            even[...] = ready[...]
        carry_ref[0] = near
        carry_ref[1] = next_

        def trip(i, carry):
            x = first + i * 2 * GROUP
            near, next_ = group(even, x, 2 * i, carry_ref[0], carry_ref[1], None if starts else False)
            put(odd, part, x + GROUP)
            near, next_ = group(odd, x + GROUP, 2 * i + 1, near, next_, False)
            after = i + 1 == groups // 2
            then = following[1] if following is not None else X - GROUP
            put(even, part, jnp.where(after, then, x + 2 * GROUP))
            carry_ref[0] = near
            carry_ref[1] = next_
            return carry

        lax.fori_loop(0, groups // 2, trip, 0)
        near = carry_ref[0]
    else:
        if ready is None:
            ready = even
            put(even, part, first)
        near, next_ = group(ready, first, 0, near, next_, starts)
        put(odd, part, first + GROUP)
        near, next_ = group(odd, first + GROUP, 1, near, next_, False)
        put(even, *following)
        carry_ref[0] = near
        carry_ref[1] = next_
    if ends:
        put_far(edge, 0, far_hi, part, 1)
        last = jnp.dot(patches(edge, 1), w_ref[:, 2 * C :], preferred_element_type=F32)
        finish(X - 1, near + last)
        copy(X, 1, groups).start()
    if late is not None:
        late[...] = made_ref[count - GROUP : count]
    for sem in range(own_copies):
        x = first + sem * GROUP
        if starts and sem == 0:
            copy(x + 1, GROUP - 1, sem).wait()
        else:
            copy(x, GROUP, sem).wait()
    if ends:
        copy(X, 1, groups).wait()
    if late_copy is not None:
        late_copy.wait()


def conv_piece(part, first, groups, following, mask, field, far, weight, state, done, tie):
    operands = [mask, *field, weight]
    starts, ends = first == 0, first + groups * GROUP == X
    if starts:
        operands.append(far[0])
    if ends:
        operands.append(far[1])
    if not starts:
        operands += [state["carry"], state["late"]]
    if "ready" in state:
        operands.append(state["ready"])
    aliases = {}
    specs = [VMEM] * len(operands)
    operands.append(tie)
    specs.append(ANY)
    if not starts:
        aliases = {len(operands): 0}
        operands.append(done)
        specs.append(ANY)
    shifted = (3, GROUP, Y + 2, Z, C)
    more = following is not None
    buffers = [shape((2, ROWS, C), F32), shape(shifted, BF16)]
    kept = buffers + ([] if ends else [shape((GROUP, Y, Z, C), BF16)])
    scratch = [
        pltpu.VMEM(shifted, BF16),
        pltpu.VMEM((3, 1, Y + 2, Z, C), BF16),
        pltpu.VMEM((groups * GROUP + 1, Y, Z, C), BF16),
        pltpu.SemaphoreType.DMA((groups + 2,)),
    ]
    if not more:
        scratch = [pltpu.VMEM(b.shape, b.dtype) for b in buffers] + scratch
        kept = [shape((8, C), F32)]

    def plain(*refs):
        conv_kernel(part, first, groups, following, *refs)

    def final(*refs):
        refs[-7][...] = jnp.zeros((8, C), F32)
        conv_kernel(part, first, groups, following, *refs[:-7], *refs[-6:])

    made, *kept = pl.pallas_call(
        plain if more else final,
        in_specs=specs,
        out_specs=[ANY] + [VMEM] * len(kept),
        out_shape=[shape((X, Y, Z, C), BF16)] + kept,
        scratch_shapes=scratch,
        input_output_aliases=aliases,
        compiler_params=params(),
        cost_estimate=cost(groups * GROUP, 2 << 20),
    )(*operands)
    return made, dict(zip(("carry", "ready", "late"), kept, strict=False))


def small_kernel(kernel, out_shape, operands, ties=(), specs=None, moved=1 << 20):
    count = len(operands)

    def run(*refs):
        kernel(*refs[:count], *refs[count + len(ties) :])

    return pl.pallas_call(
        run,
        in_specs=(specs or [VMEM] * count) + [ANY] * len(ties),
        out_specs=jax.tree.map(lambda _: VMEM, out_shape),
        out_shape=out_shape,
        compiler_params=params(),
        cost_estimate=pl.CostEstimate(flops=1000, bytes_accessed=moved, transcendentals=0),
    )(*operands, *ties)


def edge_kernel(zlo, zhi, lo, hi):
    for side, ref in enumerate((zlo, zhi)):
        lo[:, side] = held(ref[:, :, 0, :], "gz", side)
        hi[:, side] = held(ref[:, :, Y - 1, :], "gz", side)


def message_kernel(x_ref, g_ref, ylo, yhi, zlo, zhi, elo, ehi, held_ylo, held_yhi, col_lo, col_hi, to_lo, to_hi):
    held_ylo[...] = held(ylo[...], "gy", 0)
    held_yhi[...] = held(yhi[...], "gy", 1)
    tail = jnp.zeros((2, X, 24 - Y - 2, C), F32)
    for side, (near, col) in enumerate(((zlo, col_lo), (zhi, col_hi))):
        own = held(near[...].astype(F32), "gz", side)
        low = held(elo[:, side].astype(F32), "gy", 0)[:, :, None, :]
        high = held(ehi[:, side].astype(F32), "gy", 1)[:, :, None, :]
        col[...] = jnp.concatenate([low, own, high, tail], axis=2).astype(BF16)
    for at, to in ((0, to_lo), (X - 1, to_hi)):
        to[0, :Y] = x_ref[at + 1]
        to[1, :Y] = g_ref[at + 1]
        to[:, Y] = held_ylo[:, at]
        to[:, Y + 1] = held_yhi[:, at]
        rims = jnp.concatenate([col_lo[:, at], col_hi[:, at]], axis=1)
        to[:, Y + 2 :] = rims.reshape(2, 3, Z, C)


def arrange_kernel(w_ref, forward, flipped):
    for tap in range(27):
        tx, row = tap // 9, tap % 9
        forward[row * C : (row + 1) * C, tx * C : (tx + 1) * C] = w_ref[tap]
        flipped[row * C : (row + 1) * C, tx * C : (tx + 1) * C] = w_ref[26 - tap].astype(F32).T.astype(BF16)


ORDER = ("zyx", "yxz")


def first_place(core):
    return lax.axis_index("gx") // 2 * (1 - core) + lax.axis_index("gy") * core


def pairs(turn, step):
    found = []
    for z in range(4):
        for core in range(2):
            for y in range(4):
                for x in range(4):
                    at = {"z": z, "y": y, "x": x}
                    to = dict(at)
                    to[ORDER[core][turn]] ^= step
                    found.append(tuple(((2 * p["z"] + core) * 4 + p["y"]) * 4 + p["x"] for p in (at, to)))
    return found


def exchange(turn, values):
    steps = zip((1, 2, 3), values, strict=True)
    return [lax.ppermute(value, ("gx", "gy", "gz"), pairs(turn, step)) for step, value in steps]


def deal(terms, ties):
    rows = terms[0].shape[0] // 4

    def kernel(*refs):
        me = first_place(lax.axis_index("gx") % 2)
        for step in range(4):
            at = pl.ds((me ^ step) * rows, rows)
            total = refs[0][at]
            for ref in refs[1 : len(terms)]:
                total = total + ref[at]
            refs[len(terms) + step][...] = total

    return small_kernel(kernel, [shape((rows, C), F32)] * 4, terms, ties)


def sum_kernel(a, b, c, d, o):
    o[...] = (a[...] + c[...]) + (b[...] + d[...])


def write(sources, mine, target, tie):
    arrays = [a for a, _ in sources]
    rows = HALF * C // 4
    short = 27 * C - 2 * HALF * C + rows
    count = sum(len(steps) for _, steps in sources)

    def kernel(*refs):
        o_ref, left = refs[-2:]
        at = lax.axis_index("gx")
        half = at % 2 if mine else 1 - at % 2
        me = first_place(half)
        for act in ("start", "wait"):
            sem = 0
            for ref, (_, steps) in zip(refs, sources, strict=False):
                for at, step in enumerate(steps):
                    chunk = half * 4 + (me ^ step)

                    def move(size, ref=ref, at=at, chunk=chunk, sem=sem):
                        target = o_ref.at[pl.ds(chunk * rows, size)]
                        copy = pltpu.make_async_copy(ref.at[pl.ds(at * rows, size)], target, left.at[sem])
                        getattr(copy, act)()

                    pl.when(chunk < 7)(lambda move=move: move(rows))
                    pl.when(chunk == 7)(lambda move=move: move(short))
                    sem += 1

    operands = arrays + [tie] + ([] if target is None else [target])
    return pl.pallas_call(
        kernel,
        in_specs=[VMEM] * len(arrays) + [ANY] * (len(operands) - len(arrays)),
        out_specs=ANY,
        out_shape=shape((27 * C, C), F32),
        scratch_shapes=[pltpu.SemaphoreType.DMA((count,))],
        input_output_aliases={} if target is None else {len(operands) - 1: 0},
        compiler_params=params(),
        cost_estimate=pl.CostEstimate(flops=1000, bytes_accessed=1 << 20, transcendentals=0),
    )(*operands)


def join_kernel(a, b, c, o):
    rows = a.shape[0]
    for k, ref in enumerate((a, b, c)):
        o[k * rows : (k + 1) * rows] = ref[...]


def shift(value, axis, step):
    count = lax.axis_size(axis)
    return lax.ppermute(value, axis, [(i, (i + step) % count) for i in range(count)])


def body(features, occupancy, weight, cotangent):
    slabs, mask, faces = prepare(occupancy, features, cotangent)
    zlo, zhi, ylo, yhi = faces
    near_zlo = shift(zhi, "gz", 1)
    near_zhi = shift(zlo, "gz", -1)
    near_ylo = shift(yhi, "gy", 1)
    near_yhi = shift(ylo, "gy", -1)
    own = own_grad(slabs, 0, None, zlo)

    edge = shape((2, 2, X, C), BF16)
    edge_lo, edge_hi = small_kernel(edge_kernel, [edge, edge], [near_zlo, near_zhi], [own])
    edges = (shift(edge_hi, "gy", 1), shift(edge_lo, "gy", -1))
    forward, flipped = small_kernel(
        arrange_kernel, [shape((TAPS, WIDE), BF16)] * 2, [weight.reshape(27, C, C)], [edge_lo]
    )
    own = small_kernel(
        z_rim_kernel, shape((TAPS, WIDE), F32), [own, zlo, zhi, near_zlo, near_zhi], [edge_lo]
    )

    face = shape((2, X, Z, C), BF16)
    column = shape((2, X, 24, C), BF16)
    message = shape((2, Y + 5, Z, C), BF16)
    held_ylo, held_yhi, col_lo, col_hi, to_lo, to_hi = small_kernel(
        message_kernel,
        [face, face, column, column, message, message],
        [*slabs, near_ylo, near_yhi, near_zlo, near_zhi, *edges],
        [forward, own],
    )
    far = (shift(to_hi, "gx", 1), shift(to_lo, "gx", -1))
    own = own_grad(slabs, X // 2, own, to_lo)
    keep, send = rim_grad(own, slabs[1], [ylo, yhi, held_ylo, held_yhi, *edges, *far])

    field = [*slabs, held_ylo, held_yhi, col_lo, col_hi]
    made = [None, None]
    weights = (forward, flipped)
    order = [(0, 0, 2), (0, 8, 4), (0, 24, 2), (1, 0, 4), (1, 16, 4)]
    state = {}

    def convolve(tie):
        part, first, groups = order.pop(0)
        following = order[0][:2] if order else None
        made[part], kept = conv_piece(
            part, first, groups, following, mask, field, far, weights[part], state, made[part], tie
        )
        state.update(kept)
        return [kept["carry"]]

    swap = [(i, i ^ 1) for i in range(8)]
    came = lax.ppermute(send, "gx", swap)
    ties = convolve(send)
    flat = (HALF * C, C)
    own, *parts = deal([keep.reshape(flat), came.reshape(flat)], ties)
    came = exchange(0, parts)
    chunk, ties = own, convolve(parts[0])
    for turn in (1, 2):
        chunk = small_kernel(sum_kernel, shape(chunk.shape, F32), [chunk, *came], ties)
        came = exchange(turn, [chunk] * 3)
        ties = convolve(chunk)
    chunk = small_kernel(sum_kernel, shape(chunk.shape, F32), [chunk, *came], ties)
    came = exchange(0, [chunk] * 3)
    beside = lax.ppermute(chunk, "gx", swap)
    ties = convolve(chunk)
    joined = small_kernel(join_kernel, shape((3 * chunk.shape[0], C), F32), came, [beside, *ties])
    others = lax.ppermute(joined, "gx", swap)
    full = write([(chunk, (0,)), (joined, (1, 2, 3))], True, None, joined)
    full = write([(beside, (0,))], False, full, joined)
    full = write([(others, (1, 2, 3))], False, full, joined)
    return (made[0], made[1], full.reshape(3, 3, 3, C, C))


def solution(mesh):
    placed = (P("gx", "gy", "gz", None), P("gx", "gy", "gz"), P(), P("gx", "gy", "gz", None))
    return jax.shard_map(
        body,
        mesh=mesh,
        in_specs=placed,
        out_specs=(P("gx", "gy", "gz", None), P("gx", "gy", "gz", None), P()),
        check_vma=False,
    )
```

```python
import math

import jax
import jax.numpy as jnp
from jax import lax
from jax.experimental import pallas as pl
from jax.experimental.pallas import tpu as pltpu
from jax.sharding import PartitionSpec as P

SHARE = 8
X, Y, Z, C = 32, 16, 16, 128
E = 8
ROWS = Y * Z
GROUP = 4
SPAN = 8
TAPS = 9 * C
WIDE = 3 * C
HALF = 14
F32 = jnp.float32
BF16 = jnp.bfloat16
VMEM = pl.BlockSpec(memory_space=pltpu.VMEM)
SMEM = pl.BlockSpec(memory_space=pltpu.SMEM)
ANY = pl.BlockSpec(memory_space=pl.ANY)
DEPTH_FIRST = (((0,), (0,)), ((), ()))


def shape(dims, dtype):
    return jax.ShapeDtypeStruct(dims, dtype)


def params(mebibytes=24):
    return pltpu.CompilerParams(vmem_limit_bytes=mebibytes * 1024 * 1024)


def cost(slabs, moved):
    return pl.CostEstimate(flops=2 * 27 * C * C * slabs * ROWS, bytes_accessed=moved, transcendentals=0)


def inside(axis, side):
    at = lax.axis_index(axis)
    return at > 0 if side == 0 else at < lax.axis_size(axis) - 1


def held(value, axis, side):
    return jnp.where(inside(axis, side), value, jnp.zeros_like(value))


def brick_flags(occ_ref, brick):
    low_z = lax.broadcasted_iota(jnp.int32, (E, Z, C), 1) < E
    halves = [jnp.where(low_z, occ_ref[j, 0, brick], occ_ref[j, 1, brick]) for j in range(2)]
    return jnp.concatenate(halves, axis=0) == 1


def mask_slabs(part, source, mask_ref, s_ref, faces):
    zlo_ref, zhi_ref, ylo_ref, yhi_ref = faces
    for end in (0, X + 1):
        s_ref[end] = jnp.zeros((Y, Z, C), BF16)

    def one(brick, carry):
        span = pl.ds(brick * E, E)
        keep = mask_ref[brick].astype(F32) > 0.0
        value = jnp.where(keep[None], source[span].astype(F32), 0.0).astype(BF16)
        s_ref[pl.ds(brick * E + 1, E)] = value
        zlo_ref[part, span] = value[:, :, 0, :]
        zhi_ref[part, span] = value[:, :, Z - 1, :]
        ylo_ref[part, span] = value[:, 0]
        yhi_ref[part, span] = value[:, Y - 1]
        return carry

    lax.fori_loop(0, X // E, one, 0)


def mask_kernel(occ_ref, mask_ref):
    for brick in range(X // E):
        mask_ref[brick] = jnp.where(brick_flags(occ_ref, brick), 1.0, 0.0).astype(BF16)


def prepare_x_kernel(f_ref, mask_ref, s_ref, *faces):
    mask_slabs(0, f_ref, mask_ref, s_ref, faces)


def prepare_g_kernel(c_ref, mask_ref, *refs):
    given, s_ref, faces = refs[:4], refs[4], refs[5:]
    for face, ref in zip(faces, given, strict=True):
        face[0] = ref[0]
    mask_slabs(1, c_ref, mask_ref, s_ref, faces)


def prepare(occupancy, features, cotangent):
    slabs = shape((X + 2, Y, Z, C), BF16)
    own_cost = pl.CostEstimate(flops=1000000, bytes_accessed=5 << 20, transcendentals=0)
    mask = small_kernel(
        mask_kernel, shape((X // E, Y, Z, C), BF16), [jnp.transpose(occupancy, (1, 2, 0))], specs=[SMEM],
        moved=16 << 20,
    )
    fields, *given = pl.pallas_call(
        prepare_x_kernel,
        in_specs=[VMEM] * 2,
        out_specs=[VMEM] * 5,
        out_shape=[slabs] + [shape((1, X, Z, C), BF16)] * 4,
        compiler_params=params(),
        cost_estimate=own_cost,
    )(features, mask)
    cotangents, *faces = pl.pallas_call(
        prepare_g_kernel,
        in_specs=[VMEM] * 6,
        out_specs=[VMEM] * 5,
        out_shape=[slabs] + [shape((2, X, Z, C), BF16)] * 4,
        compiler_params=params(),
        cost_estimate=own_cost,
    )(cotangent, mask, *given)
    return (fields, cotangents), mask, faces


def moved_z(whole, step):
    rows = whole.shape[0] * whole.shape[1]
    flat = whole.reshape(rows, C)
    return pltpu.roll(flat, -step % rows, 0).reshape(whole.shape)


def put_slab(scratch, slot, center, ylo, yhi, zlo, zhi):
    whole = jnp.concatenate([ylo[None], center, yhi[None]], axis=0)
    scratch[1, slot] = whole
    whole = whole.astype(F32)
    at = lax.broadcasted_iota(jnp.int32, (Y + 2, Z, C), 1)
    low = zlo.astype(F32)[: Y + 2, None, :]
    high = zhi.astype(F32)[: Y + 2, None, :]
    scratch[0, slot] = jnp.where(at == 0, low, moved_z(whole, -1)).astype(BF16)
    scratch[2, slot] = jnp.where(at == Z - 1, high, moved_z(whole, 1)).astype(BF16)


def put_own(scratch, slot, center):
    scratch[1, slot, 1 : Y + 1] = center
    whole = center.astype(F32)
    at = lax.broadcasted_iota(jnp.int32, (Y, Z, C), 1)
    scratch[0, slot, 1 : Y + 1] = jnp.where(at == 0, 0.0, moved_z(whole, -1)).astype(BF16)
    scratch[2, slot, 1 : Y + 1] = jnp.where(at == Z - 1, 0.0, moved_z(whole, 1)).astype(BF16)


def patches(shifted, slots):
    pieces = []
    for ty in range(3):
        for tz in range(3):
            pieces.append(shifted[tz, :slots, ty : ty + Y].reshape(slots * ROWS, C))
    return jnp.concatenate(pieces, axis=1)


def put_far(scratch, slot, far_ref, part, side):
    slab = held(far_ref[part], "gx", side)
    rims = slab[Y + 2 :].reshape(-1, C)
    put_slab(scratch, slot, slab[:Y], slab[Y], slab[Y + 1], rims[:24], rims[24:])


def own_grad_kernel(first, more, x_ref, g_ref, *refs):
    total, even, odd = refs[-3:]
    for shifted in (even, odd):
        shifted[:, :, 0:1] = jnp.zeros((3, SPAN, 1, Z, C), BF16)
        shifted[:, :, Y + 1 :] = jnp.zeros((3, SPAN, 1, Z, C), BF16)

    def put(shifted, x):
        for slot in range(SPAN):
            put_own(shifted, slot, x_ref[x + 1 + slot])

    def product(shifted, x):
        columns = [g_ref[x + 2 - tx : x + 2 - tx + SPAN].reshape(SPAN * ROWS, C) for tx in range(3)]
        beside = jnp.concatenate(columns, axis=1)
        return lax.dot_general(beside, patches(shifted, SPAN), DEPTH_FIRST, preferred_element_type=F32)

    put(even, first)
    made = product(even, first)
    put(odd, first + SPAN)
    total[...] = refs[0][...] + made if more else made
    total[...] += product(odd, first + SPAN)


def own_grad(slabs, first, before, tie):
    more = before is not None
    return pl.pallas_call(
        lambda *refs: own_grad_kernel(first, more, *refs),
        in_specs=[VMEM] * (2 + more) + [ANY],
        out_specs=VMEM,
        out_shape=shape((WIDE, TAPS), F32),
        scratch_shapes=[pltpu.VMEM((3, SPAN, Y + 2, Z, C), BF16)] * 2,
        compiler_params=params(),
        cost_estimate=cost(2 * SPAN, 8 << 20),
    )(*slabs, *([before] if more else []), tie)


def add_rim(total, row, stride, trio, face_ref):
    blank = jnp.zeros((1, Z, C), BF16)
    padded = jnp.concatenate([blank, face_ref[1], blank], axis=0)
    around = jnp.concatenate([padded[2 - tx : 2 - tx + X].reshape(X * Z, C) for tx in range(3)], axis=1)
    left = jnp.concatenate([a.astype(BF16).reshape(X * Z, C) for a in trio], axis=1)
    made = lax.dot_general(around, left, DEPTH_FIRST, preferred_element_type=F32)
    for k in range(3):
        start = (row + k * stride) * C
        total[:, start : start + C] += made[:, k * C : (k + 1) * C]


def z_rim_kernel(own_ref, gzlo, gzhi, nzlo, nzhi, total):
    total[...] = own_ref[...]
    at = lax.broadcasted_iota(jnp.int32, (X, Z, C), 1)
    for side, row, near, face in ((0, 0, nzlo, gzlo), (1, 2, nzhi, gzhi)):
        whole = held(near[0].astype(F32), "gz", side)
        before = jnp.where(at == 0, 0.0, moved_z(whole, -1))
        after = jnp.where(at == Z - 1, 0.0, moved_z(whole, 1))
        add_rim(total, row, 3, (before, whole, after), face)


def rim_grad_kernel(
    own_ref, g_ref, gylo, gyhi, nylo, nyhi, elo, ehi, far_lo, far_hi, keep_ref, send_ref, scratch, total
):
    total[...] = own_ref[...]
    for side, far, plane, tx in ((0, far_lo, 1, 0), (1, far_hi, X, 2)):
        put_far(scratch.at[:, side : side + 1], 0, far, 0, side)
        left = patches(scratch.at[:, side : side + 1], 1)
        beside = g_ref[plane].reshape(ROWS, C)
        total[tx * C : (tx + 1) * C] += lax.dot_general(
            beside, left, DEPTH_FIRST, preferred_element_type=F32
        )
    at = lax.broadcasted_iota(jnp.int32, (X, Z, C), 1)
    for side, row, near, edges, face in ((0, 0, nylo, elo, gylo), (1, 6, nyhi, ehi, gyhi)):
        whole = near[0].astype(F32)
        corners = held(edges[0].astype(F32), "gy", side)
        low = corners[0][:, None, :]
        high = corners[1][:, None, :]
        before = jnp.where(at == 0, low, moved_z(whole, -1))
        after = jnp.where(at == Z - 1, high, moved_z(whole, 1))
        add_rim(total, row, 1, (before, whole, after), face)

    scale = 1.0 / math.sqrt(SHARE * 128 * E**3)
    core = lax.axis_index("gx") % 2
    for mine in range(2):

        @pl.when(core == mine)
        def _():
            for tap in range(27):
                tx, row = tap // 9, tap % 9
                ref = keep_ref if tap // HALF == mine else send_ref
                ref[tap % HALF] = total[tx * C : (tx + 1) * C, row * C : (row + 1) * C].T * scale
            ref = keep_ref if mine == 1 else send_ref
            ref[HALF - 1] = jnp.zeros((C, C), F32)


def rim_grad(own, cotangents, operands):
    return pl.pallas_call(
        rim_grad_kernel,
        in_specs=[VMEM] * (2 + len(operands)),
        out_specs=[VMEM, VMEM],
        out_shape=[shape((HALF, C, C), F32)] * 2,
        scratch_shapes=[pltpu.VMEM((3, 2, Y + 2, Z, C), BF16), pltpu.VMEM((WIDE, TAPS), F32)],
        compiler_params=params(),
        cost_estimate=cost(3, 6 << 20),
    )(own, cotangents, *operands)


def conv_kernel(part, first, groups, following, mask_ref, *refs):
    starts, ends = first == 0, first + groups * GROUP == X
    refs = list(refs)
    slabs = [refs.pop(0) for _ in range(2)]
    rims = [refs.pop(0) for _ in range(4)]
    w_ref = refs.pop(0)
    far_lo = refs.pop(0) if starts else None
    far_hi = refs.pop(0) if ends else None
    before = None if starts else refs.pop(0)
    late_in = None if starts else refs.pop(0)
    ready = None if starts and part == 0 else refs.pop(0)
    late = None if ends else refs.pop(-5)
    o_ref, carry_ref, even, others, edge, made_ref, left = refs[-7:]
    odd = others.at[0]
    count = groups * GROUP
    own_copies = groups if ends else groups - 1
    late_copy = None
    if not starts:
        skip = 1 if first == GROUP else 0
        target = o_ref.at[pl.ds(first - GROUP - 1 + skip, GROUP - skip)]
        late_copy = pltpu.make_async_copy(late_in.at[pl.ds(skip, GROUP - skip)], target, left.at[groups + 1])
        late_copy.start()

    def put(shifted, at, x):
        for slot in range(GROUP):
            put_slab(shifted, slot, slabs[at][x + 1 + slot], *(ref[at, x + slot] for ref in rims))

    def finish(x, total):
        keep = mask_ref[jnp.maximum(x, 0) // E].astype(F32) > 0.0
        made_ref[x - first + 1] = jnp.where(keep, total.reshape(Y, Z, C), 0.0).astype(BF16)

    def copy(x, size, sem):
        source = made_ref.at[pl.ds(x - first, size)]
        return pltpu.make_async_copy(source, o_ref.at[pl.ds(x - 1, size)], left.at[sem])

    def group(shifted, x, sem, near, next_, opens):
        made = jnp.dot(patches(shifted, GROUP), w_ref[...], preferred_element_type=F32)

        def term(slot, tx):
            return made[slot * ROWS : (slot + 1) * ROWS, tx * C : (tx + 1) * C]

        if opens is True:
            made_ref[0] = jnp.zeros((Y, Z, C), BF16)
        else:
            finish(x - 1, near + term(0, 2))
        finish(x, next_ + term(0, 1) + term(1, 2))
        for slot in range(1, GROUP - 1):
            finish(x + slot, term(slot - 1, 0) + term(slot, 1) + term(slot + 1, 2))
        if opens is None:
            pl.when(sem == 0)(lambda: copy(x + 1, GROUP - 1, sem).start())
            pl.when(sem > 0)(lambda: copy(x, GROUP, sem).start())
        elif opens:
            if own_copies > 0:
                copy(x + 1, GROUP - 1, sem).start()
        elif ends:
            copy(x, GROUP, sem).start()
        else:
            pl.when(sem < own_copies)(lambda: copy(x, GROUP, sem).start())
        return term(GROUP - 2, 0) + term(GROUP - 1, 1), term(GROUP - 1, 0)

    if starts:
        put_far(edge, 0, far_lo, part, 0)
        near = jnp.zeros((ROWS, C), F32)
        next_ = jnp.dot(patches(edge, 1), w_ref[:, :C], preferred_element_type=F32)
    else:
        near, next_ = before[0], before[1]
    if groups > 3:
        if ready is None:
            put(even, part, 0)
        else:
            even[...] = ready[...]
        carry_ref[0] = near
        carry_ref[1] = next_

        def trip(i, carry):
            x = first + i * 2 * GROUP
            near, next_ = group(even, x, 2 * i, carry_ref[0], carry_ref[1], None if starts else False)
            put(odd, part, x + GROUP)
            near, next_ = group(odd, x + GROUP, 2 * i + 1, near, next_, False)
            after = i + 1 == groups // 2
            then = following[1] if following is not None else X - GROUP
            put(even, part, jnp.where(after, then, x + 2 * GROUP))
            carry_ref[0] = near
            carry_ref[1] = next_
            return carry

        lax.fori_loop(0, groups // 2, trip, 0)
        near = carry_ref[0]
    else:
        if ready is None:
            put(odd, part, first)
        shifted = [odd] if ready is None else [ready, odd, others.at[1]]
        for at in range(groups):
            x = first + at * GROUP
            near, next_ = group(shifted[at], x, at, near, next_, starts and at == 0)
            if at + 1 < groups:
                put(shifted[at + 1], part, x + GROUP)
        put(even, *following)
        carry_ref[0] = near
        carry_ref[1] = next_
    if ends:
        put_far(edge, 0, far_hi, part, 1)
        last = jnp.dot(patches(edge, 1), w_ref[:, 2 * C :], preferred_element_type=F32)
        finish(X - 1, near + last)
        copy(X, 1, groups).start()
    if late is not None:
        late[...] = made_ref[count - GROUP : count]
    for sem in range(own_copies):
        x = first + sem * GROUP
        if starts and sem == 0:
            copy(x + 1, GROUP - 1, sem).wait()
        else:
            copy(x, GROUP, sem).wait()
    if ends:
        copy(X, 1, groups).wait()
    if late_copy is not None:
        late_copy.wait()


def conv_piece(part, first, groups, following, mask, field, far, weight, state, done, tie):
    operands = [mask, *field, weight]
    starts, ends = first == 0, first + groups * GROUP == X
    if starts:
        operands.append(far[0])
    if ends:
        operands.append(far[1])
    if not starts:
        operands += [state["carry"], state["late"]]
    if "ready" in state:
        operands.append(state["ready"])
    aliases = {}
    specs = [VMEM] * len(operands)
    operands.append(tie)
    specs.append(ANY)
    if not starts:
        aliases = {len(operands): 0}
        operands.append(done)
        specs.append(ANY)
    shifted = (3, GROUP, Y + 2, Z, C)
    more = following is not None
    buffers = [shape((2, ROWS, C), F32), shape(shifted, BF16)]
    kept = buffers + ([] if ends else [shape((GROUP, Y, Z, C), BF16)])
    scratch = [
        pltpu.VMEM((2, *shifted), BF16),
        pltpu.VMEM((3, 1, Y + 2, Z, C), BF16),
        pltpu.VMEM((groups * GROUP + 1, Y, Z, C), BF16),
        pltpu.SemaphoreType.DMA((groups + 2,)),
    ]
    if not more:
        scratch = [pltpu.VMEM(b.shape, b.dtype) for b in buffers] + scratch
        kept = [shape((8, C), F32)]

    def plain(*refs):
        conv_kernel(part, first, groups, following, *refs)

    def final(*refs):
        refs[-7][...] = jnp.zeros((8, C), F32)
        conv_kernel(part, first, groups, following, *refs[:-7], *refs[-6:])

    made, *kept = pl.pallas_call(
        plain if more else final,
        in_specs=specs,
        out_specs=[ANY] + [VMEM] * len(kept),
        out_shape=[shape((X, Y, Z, C), BF16)] + kept,
        scratch_shapes=scratch,
        input_output_aliases=aliases,
        compiler_params=params(),
        cost_estimate=cost(groups * GROUP, 2 << 20),
    )(*operands)
    return made, dict(zip(("carry", "ready", "late"), kept, strict=False))


def small_kernel(kernel, out_shape, operands, ties=(), specs=None, moved=1 << 20):
    count = len(operands)

    def run(*refs):
        kernel(*refs[:count], *refs[count + len(ties) :])

    return pl.pallas_call(
        run,
        in_specs=(specs or [VMEM] * count) + [ANY] * len(ties),
        out_specs=jax.tree.map(lambda _: VMEM, out_shape),
        out_shape=out_shape,
        compiler_params=params(),
        cost_estimate=pl.CostEstimate(flops=1000, bytes_accessed=moved, transcendentals=0),
    )(*operands, *ties)


def edge_kernel(zlo, zhi, lo, hi):
    for side, ref in enumerate((zlo, zhi)):
        lo[:, side] = held(ref[:, :, 0, :], "gz", side)
        hi[:, side] = held(ref[:, :, Y - 1, :], "gz", side)


def message_kernel(x_ref, g_ref, ylo, yhi, zlo, zhi, elo, ehi, held_ylo, held_yhi, col_lo, col_hi, to_lo, to_hi):
    held_ylo[...] = held(ylo[...], "gy", 0)
    held_yhi[...] = held(yhi[...], "gy", 1)
    tail = jnp.zeros((2, X, 24 - Y - 2, C), F32)
    for side, (near, col) in enumerate(((zlo, col_lo), (zhi, col_hi))):
        own = held(near[...].astype(F32), "gz", side)
        low = held(elo[:, side].astype(F32), "gy", 0)[:, :, None, :]
        high = held(ehi[:, side].astype(F32), "gy", 1)[:, :, None, :]
        col[...] = jnp.concatenate([low, own, high, tail], axis=2).astype(BF16)
    for at, to in ((0, to_lo), (X - 1, to_hi)):
        to[0, :Y] = x_ref[at + 1]
        to[1, :Y] = g_ref[at + 1]
        to[:, Y] = held_ylo[:, at]
        to[:, Y + 1] = held_yhi[:, at]
        rims = jnp.concatenate([col_lo[:, at], col_hi[:, at]], axis=1)
        to[:, Y + 2 :] = rims.reshape(2, 3, Z, C)


def arrange_kernel(w_ref, forward, flipped):
    for tap in range(27):
        tx, row = tap // 9, tap % 9
        forward[row * C : (row + 1) * C, tx * C : (tx + 1) * C] = w_ref[tap]
        flipped[row * C : (row + 1) * C, tx * C : (tx + 1) * C] = w_ref[26 - tap].astype(F32).T.astype(BF16)


ORDER = ("zyx", "yxz")


def first_place(core):
    return lax.axis_index("gx") // 2 * (1 - core) + lax.axis_index("gy") * core


def pairs(turn, step):
    found = []
    for z in range(4):
        for core in range(2):
            for y in range(4):
                for x in range(4):
                    at = {"z": z, "y": y, "x": x}
                    to = dict(at)
                    to[ORDER[core][turn]] ^= step
                    found.append(tuple(((2 * p["z"] + core) * 4 + p["y"]) * 4 + p["x"] for p in (at, to)))
    return found


def exchange(turn, values):
    steps = zip((1, 2, 3), values, strict=True)
    return [lax.ppermute(value, ("gx", "gy", "gz"), pairs(turn, step)) for step, value in steps]


def deal(terms, ties):
    rows = terms[0].shape[0] // 4

    def kernel(*refs):
        me = first_place(lax.axis_index("gx") % 2)
        for step in range(4):
            at = pl.ds((me ^ step) * rows, rows)
            total = refs[0][at]
            for ref in refs[1 : len(terms)]:
                total = total + ref[at]
            refs[len(terms) + step][...] = total

    return small_kernel(kernel, [shape((rows, C), F32)] * 4, terms, ties)


def sum_kernel(a, b, c, d, o):
    o[...] = (a[...] + c[...]) + (b[...] + d[...])


def write(sources, mine, target, tie):
    arrays = [a for a, _ in sources]
    rows = HALF * C // 4
    short = 27 * C - 2 * HALF * C + rows
    count = sum(len(steps) for _, steps in sources)

    def kernel(*refs):
        o_ref, left = refs[-2:]
        at = lax.axis_index("gx")
        half = at % 2 if mine else 1 - at % 2
        me = first_place(half)
        for act in ("start", "wait"):
            sem = 0
            for ref, (_, steps) in zip(refs, sources, strict=False):
                for at, step in enumerate(steps):
                    chunk = half * 4 + (me ^ step)

                    def move(size, ref=ref, at=at, chunk=chunk, sem=sem):
                        target = o_ref.at[pl.ds(chunk * rows, size)]
                        copy = pltpu.make_async_copy(ref.at[pl.ds(at * rows, size)], target, left.at[sem])
                        getattr(copy, act)()

                    pl.when(chunk < 7)(lambda move=move: move(rows))
                    pl.when(chunk == 7)(lambda move=move: move(short))
                    sem += 1

    operands = arrays + [tie] + ([] if target is None else [target])
    return pl.pallas_call(
        kernel,
        in_specs=[VMEM] * len(arrays) + [ANY] * (len(operands) - len(arrays)),
        out_specs=ANY,
        out_shape=shape((27 * C, C), F32),
        scratch_shapes=[pltpu.SemaphoreType.DMA((count,))],
        input_output_aliases={} if target is None else {len(operands) - 1: 0},
        compiler_params=params(),
        cost_estimate=pl.CostEstimate(flops=1000, bytes_accessed=1 << 20, transcendentals=0),
    )(*operands)


def join_kernel(a, b, c, o):
    rows = a.shape[0]
    for k, ref in enumerate((a, b, c)):
        o[k * rows : (k + 1) * rows] = ref[...]


def shift(value, axis, step):
    count = lax.axis_size(axis)
    return lax.ppermute(value, axis, [(i, (i + step) % count) for i in range(count)])


def body(features, occupancy, weight, cotangent):
    slabs, mask, faces = prepare(occupancy, features, cotangent)
    zlo, zhi, ylo, yhi = faces
    near_zlo = shift(zhi, "gz", 1)
    near_zhi = shift(zlo, "gz", -1)
    near_ylo = shift(yhi, "gy", 1)
    near_yhi = shift(ylo, "gy", -1)
    own = own_grad(slabs, 0, None, zlo)

    edge = shape((2, 2, X, C), BF16)
    edge_lo, edge_hi = small_kernel(edge_kernel, [edge, edge], [near_zlo, near_zhi], [own])
    edges = (shift(edge_hi, "gy", 1), shift(edge_lo, "gy", -1))
    forward, flipped = small_kernel(
        arrange_kernel, [shape((TAPS, WIDE), BF16)] * 2, [weight.reshape(27, C, C)], [edge_lo]
    )
    own = small_kernel(
        z_rim_kernel, shape((WIDE, TAPS), F32), [own, zlo, zhi, near_zlo, near_zhi], [edge_lo]
    )

    face = shape((2, X, Z, C), BF16)
    column = shape((2, X, 24, C), BF16)
    message = shape((2, Y + 5, Z, C), BF16)
    held_ylo, held_yhi, col_lo, col_hi, to_lo, to_hi = small_kernel(
        message_kernel,
        [face, face, column, column, message, message],
        [*slabs, near_ylo, near_yhi, near_zlo, near_zhi, *edges],
        [forward, own],
    )
    far = (shift(to_hi, "gx", 1), shift(to_lo, "gx", -1))
    own = own_grad(slabs, X // 2, own, to_lo)
    keep, send = rim_grad(own, slabs[1], [ylo, yhi, held_ylo, held_yhi, *edges, *far])

    field = [*slabs, held_ylo, held_yhi, col_lo, col_hi]
    made = [None, None]
    weights = (forward, flipped)
    order = [(0, 0, 1), (0, 4, 4), (0, 20, 3), (1, 0, 4), (1, 16, 4)]
    state = {}

    def convolve(tie):
        part, first, groups = order.pop(0)
        following = order[0][:2] if order else None
        made[part], kept = conv_piece(
            part, first, groups, following, mask, field, far, weights[part], state, made[part], tie
        )
        state.update(kept)
        return [kept["carry"]]

    swap = [(i, i ^ 1) for i in range(8)]
    came = lax.ppermute(send, "gx", swap)
    ties = convolve(send)
    flat = (HALF * C, C)
    own, *parts = deal([keep.reshape(flat), came.reshape(flat)], ties)
    came = exchange(0, parts)
    chunk, ties = own, convolve(parts[0])
    for turn in (1, 2):
        chunk = small_kernel(sum_kernel, shape(chunk.shape, F32), [chunk, *came], ties)
        came = exchange(turn, [chunk] * 3)
        ties = convolve(chunk)
    chunk = small_kernel(sum_kernel, shape(chunk.shape, F32), [chunk, *came], ties)
    came = exchange(0, [chunk] * 3)
    beside = lax.ppermute(chunk, "gx", swap)
    ties = convolve(chunk)
    joined = small_kernel(join_kernel, shape((3 * chunk.shape[0], C), F32), came, [beside, *ties])
    others = lax.ppermute(joined, "gx", swap)
    full = write([(chunk, (0,)), (joined, (1, 2, 3))], True, None, joined)
    full = write([(beside, (0,))], False, full, joined)
    full = write([(others, (1, 2, 3))], False, full, joined)
    return (made[0], made[1], full.reshape(3, 3, 3, C, C))


def solution(mesh):
    placed = (P("gx", "gy", "gz", None), P("gx", "gy", "gz"), P(), P("gx", "gy", "gz", None))
    return jax.shard_map(
        body,
        mesh=mesh,
        in_specs=placed,
        out_specs=(P("gx", "gy", "gz", None), P("gx", "gy", "gz", None), P()),
        check_vma=False,
    )
```

```python
import math

import jax
import jax.numpy as jnp
from jax import lax
from jax.experimental import pallas as pl
from jax.experimental.pallas import tpu as pltpu
from jax.sharding import PartitionSpec as P

SHARE = 8
X, Y, Z, C = 32, 16, 16, 128
E = 8
ROWS = Y * Z
GROUP = 4
SPAN = 8
TAPS = 9 * C
WIDE = 3 * C
HALF = 27 * C // 2
F32 = jnp.float32
BF16 = jnp.bfloat16
VMEM = pl.BlockSpec(memory_space=pltpu.VMEM)
SMEM = pl.BlockSpec(memory_space=pltpu.SMEM)
ANY = pl.BlockSpec(memory_space=pl.ANY)
DEPTH_FIRST = (((0,), (0,)), ((), ()))


def shape(dims, dtype):
    return jax.ShapeDtypeStruct(dims, dtype)


def params(mebibytes=24):
    return pltpu.CompilerParams(vmem_limit_bytes=mebibytes * 1024 * 1024)


def cost(slabs, moved):
    return pl.CostEstimate(flops=2 * 27 * C * C * slabs * ROWS, bytes_accessed=moved, transcendentals=0)


def inside(axis, side):
    at = lax.axis_index(axis)
    return at > 0 if side == 0 else at < lax.axis_size(axis) - 1


def held(value, axis, side):
    return jnp.where(inside(axis, side), value, jnp.zeros_like(value))


def brick_flags(occ_ref, brick):
    low_z = lax.broadcasted_iota(jnp.int32, (E, Z, C), 1) < E
    halves = [jnp.where(low_z, occ_ref[j, 0, brick], occ_ref[j, 1, brick]) for j in range(2)]
    return jnp.concatenate(halves, axis=0) == 1


def mask_slabs(part, source, mask_ref, s_ref, faces):
    zlo_ref, zhi_ref, ylo_ref, yhi_ref = faces
    for end in (0, X + 1):
        s_ref[end] = jnp.zeros((Y, Z, C), BF16)

    def one(brick, carry):
        span = pl.ds(brick * E, E)
        keep = mask_ref[brick].astype(F32) > 0.0
        value = jnp.where(keep[None], source[span].astype(F32), 0.0).astype(BF16)
        s_ref[pl.ds(brick * E + 1, E)] = value
        zlo_ref[part, span] = value[:, :, 0, :]
        zhi_ref[part, span] = value[:, :, Z - 1, :]
        ylo_ref[part, span] = value[:, 0]
        yhi_ref[part, span] = value[:, Y - 1]
        return carry

    lax.fori_loop(0, X // E, one, 0)


def mask_kernel(occ_ref, mask_ref):
    for brick in range(X // E):
        mask_ref[brick] = jnp.where(brick_flags(occ_ref, brick), 1.0, 0.0).astype(BF16)


def prepare_x_kernel(f_ref, mask_ref, s_ref, *faces):
    mask_slabs(0, f_ref, mask_ref, s_ref, faces)


def prepare_g_kernel(c_ref, mask_ref, *refs):
    given, s_ref, faces = refs[:4], refs[4], refs[5:]
    for face, ref in zip(faces, given, strict=True):
        face[0] = ref[0]
    mask_slabs(1, c_ref, mask_ref, s_ref, faces)


def prepare(occupancy, features, cotangent):
    slabs = shape((X + 2, Y, Z, C), BF16)
    own_cost = pl.CostEstimate(flops=1000000, bytes_accessed=5 << 20, transcendentals=0)
    mask = small_kernel(
        mask_kernel, shape((X // E, Y, Z, C), BF16), [jnp.transpose(occupancy, (1, 2, 0))], specs=[SMEM],
        moved=16 << 20,
    )
    fields, *given = pl.pallas_call(
        prepare_x_kernel,
        in_specs=[VMEM] * 2,
        out_specs=[VMEM] * 5,
        out_shape=[slabs] + [shape((1, X, Z, C), BF16)] * 4,
        compiler_params=params(),
        cost_estimate=own_cost,
    )(features, mask)
    cotangents, *faces = pl.pallas_call(
        prepare_g_kernel,
        in_specs=[VMEM] * 6,
        out_specs=[VMEM] * 5,
        out_shape=[slabs] + [shape((2, X, Z, C), BF16)] * 4,
        compiler_params=params(),
        cost_estimate=own_cost,
    )(cotangent, mask, *given)
    return (fields, cotangents), mask, faces


def moved_z(whole, step):
    rows = whole.shape[0] * whole.shape[1]
    flat = whole.reshape(rows, C)
    return pltpu.roll(flat, -step % rows, 0).reshape(whole.shape)


def put_slab(scratch, slot, center, ylo, yhi, zlo, zhi):
    whole = jnp.concatenate([ylo[None], center, yhi[None]], axis=0)
    scratch[1, slot] = whole
    whole = whole.astype(F32)
    at = lax.broadcasted_iota(jnp.int32, (Y + 2, Z, C), 1)
    low = zlo.astype(F32)[: Y + 2, None, :]
    high = zhi.astype(F32)[: Y + 2, None, :]
    scratch[0, slot] = jnp.where(at == 0, low, moved_z(whole, -1)).astype(BF16)
    scratch[2, slot] = jnp.where(at == Z - 1, high, moved_z(whole, 1)).astype(BF16)


def put_own(scratch, slot, center):
    scratch[1, slot, 1 : Y + 1] = center
    whole = center.astype(F32)
    at = lax.broadcasted_iota(jnp.int32, (Y, Z, C), 1)
    scratch[0, slot, 1 : Y + 1] = jnp.where(at == 0, 0.0, moved_z(whole, -1)).astype(BF16)
    scratch[2, slot, 1 : Y + 1] = jnp.where(at == Z - 1, 0.0, moved_z(whole, 1)).astype(BF16)


def patches(shifted, slots):
    pieces = []
    for ty in range(3):
        for tz in range(3):
            pieces.append(shifted[tz, :slots, ty : ty + Y].reshape(slots * ROWS, C))
    return jnp.concatenate(pieces, axis=1)


def put_far(scratch, slot, far_ref, part, side):
    slab = held(far_ref[part], "gx", side)
    rims = slab[Y + 2 :].reshape(-1, C)
    put_slab(scratch, slot, slab[:Y], slab[Y], slab[Y + 1], rims[:24], rims[24:])


def own_grad_kernel(first, spans, more, x_ref, g_ref, *refs):
    total, even, odd = refs[-3:]
    for shifted in (even, odd):
        shifted[:, :, 0:1] = jnp.zeros((3, SPAN, 1, Z, C), BF16)
        shifted[:, :, Y + 1 :] = jnp.zeros((3, SPAN, 1, Z, C), BF16)

    def put(shifted, x):
        for slot in range(SPAN):
            put_own(shifted, slot, x_ref[x + 1 + slot])

    def product(shifted, x):
        columns = [g_ref[x + 2 - tx : x + 2 - tx + SPAN].reshape(SPAN * ROWS, C) for tx in range(3)]
        beside = jnp.concatenate(columns, axis=1)
        return lax.dot_general(beside, patches(shifted, SPAN), DEPTH_FIRST, preferred_element_type=F32)

    put(even, first)
    made = product(even, first)
    if spans == 2:
        put(odd, first + SPAN)
    total[...] = refs[0][...] + made if more else made
    if spans == 2:
        total[...] += product(odd, first + SPAN)


def own_grad(slabs, first, spans, before, tie):
    more = before is not None
    return pl.pallas_call(
        lambda *refs: own_grad_kernel(first, spans, more, *refs),
        in_specs=[VMEM] * (2 + more) + [ANY],
        out_specs=VMEM,
        out_shape=shape((WIDE, TAPS), F32),
        scratch_shapes=[pltpu.VMEM((3, SPAN, Y + 2, Z, C), BF16)] * 2,
        compiler_params=params(),
        cost_estimate=cost(spans * SPAN, 8 << 20),
    )(*slabs, *([before] if more else []), tie)


def add_rim(total, row, stride, trio, face_ref):
    blank = jnp.zeros((1, Z, C), BF16)
    padded = jnp.concatenate([blank, face_ref[1], blank], axis=0)
    around = jnp.concatenate([padded[2 - tx : 2 - tx + X].reshape(X * Z, C) for tx in range(3)], axis=1)
    left = jnp.concatenate([a.astype(BF16).reshape(X * Z, C) for a in trio], axis=1)
    made = lax.dot_general(around, left, DEPTH_FIRST, preferred_element_type=F32)
    for k in range(3):
        start = (row + k * stride) * C
        total[:, start : start + C] += made[:, k * C : (k + 1) * C]


def z_rim_kernel(own_ref, gzlo, gzhi, nzlo, nzhi, total):
    total[...] = own_ref[...]
    at = lax.broadcasted_iota(jnp.int32, (X, Z, C), 1)
    for side, row, near, face in ((0, 0, nzlo, gzlo), (1, 2, nzhi, gzhi)):
        whole = held(near[0].astype(F32), "gz", side)
        before = jnp.where(at == 0, 0.0, moved_z(whole, -1))
        after = jnp.where(at == Z - 1, 0.0, moved_z(whole, 1))
        add_rim(total, row, 3, (before, whole, after), face)


def rim_grad_kernel(
    own_ref, g_ref, gylo, gyhi, nylo, nyhi, elo, ehi, far_lo, far_hi, keep_ref, send_ref, scratch, total
):
    total[...] = own_ref[...]
    for side, far, plane, tx in ((0, far_lo, 1, 0), (1, far_hi, X, 2)):
        put_far(scratch.at[:, side : side + 1], 0, far, 0, side)
        left = patches(scratch.at[:, side : side + 1], 1)
        beside = g_ref[plane].reshape(ROWS, C)
        total[tx * C : (tx + 1) * C] += lax.dot_general(
            beside, left, DEPTH_FIRST, preferred_element_type=F32
        )
    at = lax.broadcasted_iota(jnp.int32, (X, Z, C), 1)
    for side, row, near, edges, face in ((0, 0, nylo, elo, gylo), (1, 6, nyhi, ehi, gyhi)):
        whole = near[0].astype(F32)
        corners = held(edges[0].astype(F32), "gy", side)
        low = corners[0][:, None, :]
        high = corners[1][:, None, :]
        before = jnp.where(at == 0, low, moved_z(whole, -1))
        after = jnp.where(at == Z - 1, high, moved_z(whole, 1))
        add_rim(total, row, 1, (before, whole, after), face)

    scale = 1.0 / math.sqrt(SHARE * 128 * E**3)
    core = lax.axis_index("gx") % 2
    for mine in range(2):

        @pl.when(core == mine)
        def _():
            for tap in range(27):
                tx, row = tap // 9, tap % 9
                block = total[tx * C : (tx + 1) * C, row * C : (row + 1) * C].T * scale
                for side, ref in ((mine, keep_ref), (1 - mine, send_ref)):
                    start = tap * C - side * HALF
                    low, high = max(start, 0), min(start + C, HALF)
                    if low < high:
                        ref[low:high] = block[low - start : high - start]


def rim_grad(own, cotangents, operands):
    return pl.pallas_call(
        rim_grad_kernel,
        in_specs=[VMEM] * (2 + len(operands)),
        out_specs=[VMEM, VMEM],
        out_shape=[shape((HALF, C), F32)] * 2,
        scratch_shapes=[pltpu.VMEM((3, 2, Y + 2, Z, C), BF16), pltpu.VMEM((WIDE, TAPS), F32)],
        compiler_params=params(),
        cost_estimate=cost(3, 6 << 20),
    )(own, cotangents, *operands)


def conv_kernel(part, first, groups, following, mask_ref, *refs):
    starts, ends = first == 0, first + groups * GROUP == X
    refs = list(refs)
    slabs = [refs.pop(0) for _ in range(2)]
    rims = [refs.pop(0) for _ in range(4)]
    w_ref = refs.pop(0)
    far_lo = refs.pop(0) if starts else None
    far_hi = refs.pop(0) if ends else None
    before = None if starts else refs.pop(0)
    late_in = None if starts else refs.pop(0)
    ready = None if starts and part == 0 else refs.pop(0)
    late = None if ends else refs.pop(-5)
    o_ref, carry_ref, even, others, edge, made_ref, left = refs[-7:]
    odd = others.at[0]
    count = groups * GROUP
    own_copies = groups if ends else groups - 1
    late_copy = None
    if not starts:
        skip = 1 if first == GROUP else 0
        target = o_ref.at[pl.ds(first - GROUP - 1 + skip, GROUP - skip)]
        late_copy = pltpu.make_async_copy(late_in.at[pl.ds(skip, GROUP - skip)], target, left.at[groups + 1])
        late_copy.start()

    def put(shifted, at, x):
        for slot in range(GROUP):
            put_slab(shifted, slot, slabs[at][x + 1 + slot], *(ref[at, x + slot] for ref in rims))

    def finish(x, total):
        keep = mask_ref[jnp.maximum(x, 0) // E].astype(F32) > 0.0
        made_ref[x - first + 1] = jnp.where(keep, total.reshape(Y, Z, C), 0.0).astype(BF16)

    def copy(x, size, sem):
        source = made_ref.at[pl.ds(x - first, size)]
        return pltpu.make_async_copy(source, o_ref.at[pl.ds(x - 1, size)], left.at[sem])

    def group(shifted, x, sem, near, next_, opens):
        made = jnp.dot(patches(shifted, GROUP), w_ref[...], preferred_element_type=F32)

        def term(slot, tx):
            return made[slot * ROWS : (slot + 1) * ROWS, tx * C : (tx + 1) * C]

        if opens is True:
            made_ref[0] = jnp.zeros((Y, Z, C), BF16)
        else:
            finish(x - 1, near + term(0, 2))
        finish(x, next_ + term(0, 1) + term(1, 2))
        for slot in range(1, GROUP - 1):
            finish(x + slot, term(slot - 1, 0) + term(slot, 1) + term(slot + 1, 2))
        if opens is None:
            pl.when(sem == 0)(lambda: copy(x + 1, GROUP - 1, sem).start())
            pl.when(sem > 0)(lambda: copy(x, GROUP, sem).start())
        elif opens:
            if own_copies > 0:
                copy(x + 1, GROUP - 1, sem).start()
        elif ends:
            copy(x, GROUP, sem).start()
        else:
            pl.when(sem < own_copies)(lambda: copy(x, GROUP, sem).start())
        return term(GROUP - 2, 0) + term(GROUP - 1, 1), term(GROUP - 1, 0)

    if starts:
        put_far(edge, 0, far_lo, part, 0)
        near = jnp.zeros((ROWS, C), F32)
        next_ = jnp.dot(patches(edge, 1), w_ref[:, :C], preferred_element_type=F32)
    else:
        near, next_ = before[0], before[1]
    if groups > 3:
        if ready is None:
            put(even, part, 0)
        else:
            even[...] = ready[...]
        carry_ref[0] = near
        carry_ref[1] = next_

        def trip(i, carry):
            x = first + i * 2 * GROUP
            near, next_ = group(even, x, 2 * i, carry_ref[0], carry_ref[1], None if starts else False)
            put(odd, part, x + GROUP)
            near, next_ = group(odd, x + GROUP, 2 * i + 1, near, next_, False)
            after = i + 1 == groups // 2
            then = following[1] if following is not None else X - GROUP
            put(even, part, jnp.where(after, then, x + 2 * GROUP))
            carry_ref[0] = near
            carry_ref[1] = next_
            return carry

        lax.fori_loop(0, groups // 2, trip, 0)
        near = carry_ref[0]
    else:
        if ready is None:
            put(odd, part, first)
        shifted = [odd] if ready is None else [ready, odd, others.at[1]]
        for at in range(groups):
            x = first + at * GROUP
            near, next_ = group(shifted[at], x, at, near, next_, starts and at == 0)
            if at + 1 < groups:
                put(shifted[at + 1], part, x + GROUP)
        put(even, *following)
        carry_ref[0] = near
        carry_ref[1] = next_
    if ends:
        put_far(edge, 0, far_hi, part, 1)
        last = jnp.dot(patches(edge, 1), w_ref[:, 2 * C :], preferred_element_type=F32)
        finish(X - 1, near + last)
        copy(X, 1, groups).start()
    if late is not None:
        late[...] = made_ref[count - GROUP : count]
    for sem in range(own_copies):
        x = first + sem * GROUP
        if starts and sem == 0:
            copy(x + 1, GROUP - 1, sem).wait()
        else:
            copy(x, GROUP, sem).wait()
    if ends:
        copy(X, 1, groups).wait()
    if late_copy is not None:
        late_copy.wait()


def conv_piece(part, first, groups, following, mask, field, far, weight, state, done, tie):
    operands = [mask, *field, weight]
    starts, ends = first == 0, first + groups * GROUP == X
    if starts:
        operands.append(far[0])
    if ends:
        operands.append(far[1])
    if not starts:
        operands += [state["carry"], state["late"]]
    if "ready" in state:
        operands.append(state["ready"])
    aliases = {}
    specs = [VMEM] * len(operands)
    operands.append(tie)
    specs.append(ANY)
    if not starts:
        aliases = {len(operands): 0}
        operands.append(done)
        specs.append(ANY)
    shifted = (3, GROUP, Y + 2, Z, C)
    more = following is not None
    buffers = [shape((2, ROWS, C), F32), shape(shifted, BF16)]
    kept = buffers + ([] if ends else [shape((GROUP, Y, Z, C), BF16)])
    scratch = [
        pltpu.VMEM((2, *shifted), BF16),
        pltpu.VMEM((3, 1, Y + 2, Z, C), BF16),
        pltpu.VMEM((groups * GROUP + 1, Y, Z, C), BF16),
        pltpu.SemaphoreType.DMA((groups + 2,)),
    ]
    if not more:
        scratch = [pltpu.VMEM(b.shape, b.dtype) for b in buffers] + scratch
        kept = [shape((8, C), F32)]

    def plain(*refs):
        conv_kernel(part, first, groups, following, *refs)

    def final(*refs):
        refs[-7][...] = jnp.zeros((8, C), F32)
        conv_kernel(part, first, groups, following, *refs[:-7], *refs[-6:])

    made, *kept = pl.pallas_call(
        plain if more else final,
        in_specs=specs,
        out_specs=[ANY] + [VMEM] * len(kept),
        out_shape=[shape((X, Y, Z, C), BF16)] + kept,
        scratch_shapes=scratch,
        input_output_aliases=aliases,
        compiler_params=params(),
        cost_estimate=cost(groups * GROUP, 2 << 20),
    )(*operands)
    return made, dict(zip(("carry", "ready", "late"), kept, strict=False))


def small_kernel(kernel, out_shape, operands, ties=(), specs=None, moved=1 << 20):
    count = len(operands)

    def run(*refs):
        kernel(*refs[:count], *refs[count + len(ties) :])

    return pl.pallas_call(
        run,
        in_specs=(specs or [VMEM] * count) + [ANY] * len(ties),
        out_specs=jax.tree.map(lambda _: VMEM, out_shape),
        out_shape=out_shape,
        compiler_params=params(),
        cost_estimate=pl.CostEstimate(flops=1000, bytes_accessed=moved, transcendentals=0),
    )(*operands, *ties)


def copy_kernel(a, b, c, d):
    c[...] = a[...]
    d[...] = b[...]


def edge_kernel(zlo, zhi, lo, hi):
    for side, ref in enumerate((zlo, zhi)):
        lo[:, side] = held(ref[:, :, 0, :], "gz", side)
        hi[:, side] = held(ref[:, :, Y - 1, :], "gz", side)


def message_kernel(x_ref, g_ref, ylo, yhi, zlo, zhi, elo, ehi, held_ylo, held_yhi, col_lo, col_hi, to_lo, to_hi):
    held_ylo[...] = held(ylo[...], "gy", 0)
    held_yhi[...] = held(yhi[...], "gy", 1)
    tail = jnp.zeros((2, X, 24 - Y - 2, C), F32)
    for side, (near, col) in enumerate(((zlo, col_lo), (zhi, col_hi))):
        own = held(near[...].astype(F32), "gz", side)
        low = held(elo[:, side].astype(F32), "gy", 0)[:, :, None, :]
        high = held(ehi[:, side].astype(F32), "gy", 1)[:, :, None, :]
        col[...] = jnp.concatenate([low, own, high, tail], axis=2).astype(BF16)
    for at, to in ((0, to_lo), (X - 1, to_hi)):
        to[0, :Y] = x_ref[at + 1]
        to[1, :Y] = g_ref[at + 1]
        to[:, Y] = held_ylo[:, at]
        to[:, Y + 1] = held_yhi[:, at]
        rims = jnp.concatenate([col_lo[:, at], col_hi[:, at]], axis=1)
        to[:, Y + 2 :] = rims.reshape(2, 3, Z, C)


def arrange_kernel(w_ref, forward, flipped):
    for tap in range(27):
        tx, row = tap // 9, tap % 9
        forward[row * C : (row + 1) * C, tx * C : (tx + 1) * C] = w_ref[tap]
        flipped[row * C : (row + 1) * C, tx * C : (tx + 1) * C] = w_ref[26 - tap].astype(F32).T.astype(BF16)


ORDER = ("zyx", "yxz")


def first_place(core):
    return lax.axis_index("gx") // 2 * (1 - core) + lax.axis_index("gy") * core


def pairs(turn, step):
    found = []
    for z in range(4):
        for core in range(2):
            for y in range(4):
                for x in range(4):
                    at = {"z": z, "y": y, "x": x}
                    to = dict(at)
                    to[ORDER[core][turn]] ^= step
                    found.append(tuple(((2 * p["z"] + core) * 4 + p["y"]) * 4 + p["x"] for p in (at, to)))
    return found


def exchange(turn, values):
    steps = zip((1, 2, 3), values, strict=True)
    return [lax.ppermute(value, ("gx", "gy", "gz"), pairs(turn, step)) for step, value in steps]


def deal(terms, ties):
    rows = terms[0].shape[0] // 4

    def kernel(*refs):
        me = first_place(lax.axis_index("gx") % 2)
        for step in range(4):
            at = pl.ds((me ^ step) * rows, rows)
            total = refs[0][at]
            for ref in refs[1 : len(terms)]:
                total = total + ref[at]
            refs[len(terms) + step][...] = total

    return small_kernel(kernel, [shape((rows, C), F32)] * 4, terms, ties)


def sum_kernel(a, b, c, d, o):
    o[...] = (a[...] + c[...]) + (b[...] + d[...])


def write(sources, mine, target, tie):
    arrays = [a for a, _ in sources]
    rows = HALF // 4
    count = sum(len(steps) for _, steps in sources)

    def kernel(*refs):
        o_ref, left = refs[-2:]
        at = lax.axis_index("gx")
        half = at % 2 if mine else 1 - at % 2
        me = first_place(half)
        for act in ("start", "wait"):
            sem = 0
            for ref, (_, steps) in zip(refs, sources, strict=False):
                for at, step in enumerate(steps):
                    chunk = half * 4 + (me ^ step)

                    place = o_ref.at[pl.ds(chunk * rows, rows)]
                    copy = pltpu.make_async_copy(ref.at[pl.ds(at * rows, rows)], place, left.at[sem])
                    if act == "start":
                        copy.start()
                    else:
                        copy.wait()
                    sem += 1

    operands = arrays + [tie] + ([] if target is None else [target])
    return pl.pallas_call(
        kernel,
        in_specs=[VMEM] * len(arrays) + [ANY] * (len(operands) - len(arrays)),
        out_specs=ANY,
        out_shape=shape((27 * C, C), F32),
        scratch_shapes=[pltpu.SemaphoreType.DMA((count,))],
        input_output_aliases={} if target is None else {len(operands) - 1: 0},
        compiler_params=params(),
        cost_estimate=pl.CostEstimate(flops=1000, bytes_accessed=1 << 20, transcendentals=0),
    )(*operands)


def join_kernel(a, b, c, o):
    rows = a.shape[0]
    for k, ref in enumerate((a, b, c)):
        o[k * rows : (k + 1) * rows] = ref[...]


def shift(value, axis, step):
    count = lax.axis_size(axis)
    return lax.ppermute(value, axis, [(i, (i + step) % count) for i in range(count)])


def body(features, occupancy, weight, cotangent):
    slabs, mask, faces = prepare(occupancy, features, cotangent)
    zlo, zhi, ylo, yhi = faces
    near_zlo = shift(zhi, "gz", 1)
    near_zhi = shift(zlo, "gz", -1)
    own = own_grad(slabs, 0, 1, None, zlo)
    face = shape((2, X, Z, C), BF16)
    to_ylo, to_yhi = small_kernel(copy_kernel, [face, face], [ylo, yhi], [own])
    near_ylo = shift(to_yhi, "gy", 1)
    near_yhi = shift(to_ylo, "gy", -1)
    own = own_grad(slabs, SPAN, 1, own, to_ylo)

    edge = shape((2, 2, X, C), BF16)
    edge_lo, edge_hi = small_kernel(edge_kernel, [edge, edge], [near_zlo, near_zhi], [own])
    edges = (shift(edge_hi, "gy", 1), shift(edge_lo, "gy", -1))
    forward, flipped = small_kernel(
        arrange_kernel, [shape((TAPS, WIDE), BF16)] * 2, [weight.reshape(27, C, C)], [edge_lo]
    )
    own = small_kernel(
        z_rim_kernel, shape((WIDE, TAPS), F32), [own, zlo, zhi, near_zlo, near_zhi], [edge_lo]
    )

    column = shape((2, X, 24, C), BF16)
    message = shape((2, Y + 5, Z, C), BF16)
    held_ylo, held_yhi, col_lo, col_hi, to_lo, to_hi = small_kernel(
        message_kernel,
        [face, face, column, column, message, message],
        [*slabs, near_ylo, near_yhi, near_zlo, near_zhi, *edges],
        [forward, own],
    )
    far = (shift(to_hi, "gx", 1), shift(to_lo, "gx", -1))
    own = own_grad(slabs, X // 2, 2, own, to_lo)
    keep, send = rim_grad(own, slabs[1], [ylo, yhi, held_ylo, held_yhi, *edges, *far])

    field = [*slabs, held_ylo, held_yhi, col_lo, col_hi]
    made = [None, None]
    weights = (forward, flipped)
    order = [(0, 0, 1), (0, 4, 4), (0, 20, 3), (1, 0, 4), (1, 16, 4)]
    state = {}

    def convolve(tie):
        part, first, groups = order.pop(0)
        following = order[0][:2] if order else None
        made[part], kept = conv_piece(
            part, first, groups, following, mask, field, far, weights[part], state, made[part], tie
        )
        state.update(kept)
        return [kept["carry"]]

    swap = [(i, i ^ 1) for i in range(8)]
    came = lax.ppermute(send, "gx", swap)
    ties = convolve(send)
    own, *parts = deal([keep, came], ties)
    came = exchange(0, parts)
    chunk, ties = own, convolve(parts[0])
    for turn in (1, 2):
        chunk = small_kernel(sum_kernel, shape(chunk.shape, F32), [chunk, *came], ties)
        came = exchange(turn, [chunk] * 3)
        ties = convolve(chunk)
    chunk = small_kernel(sum_kernel, shape(chunk.shape, F32), [chunk, *came], ties)
    came = exchange(0, [chunk] * 3)
    beside = lax.ppermute(chunk, "gx", swap)
    ties = convolve(chunk)
    joined = small_kernel(join_kernel, shape((3 * chunk.shape[0], C), F32), came, [beside, *ties])
    others = lax.ppermute(joined, "gx", swap)
    full = write([(chunk, (0,)), (joined, (1, 2, 3))], True, None, joined)
    full = write([(beside, (0,))], False, full, joined)
    full = write([(others, (1, 2, 3))], False, full, joined)
    return (made[0], made[1], full.reshape(3, 3, 3, C, C))


def solution(mesh):
    placed = (P("gx", "gy", "gz", None), P("gx", "gy", "gz"), P(), P("gx", "gy", "gz", None))
    return jax.shard_map(
        body,
        mesh=mesh,
        in_specs=placed,
        out_specs=(P("gx", "gy", "gz", None), P("gx", "gy", "gz", None), P()),
        check_vma=False,
    )
```

```python
import math

import jax
import jax.numpy as jnp
from jax import lax
from jax.experimental import pallas as pl
from jax.experimental.pallas import tpu as pltpu
from jax.sharding import PartitionSpec as P

SHARE = 8
X, Y, Z, C = 32, 16, 16, 128
E = 8
ROWS = Y * Z
GROUP = 4
SPAN = 8
TAPS = 9 * C
WIDE = 3 * C
HALF = 27 * C // 2
F32 = jnp.float32
BF16 = jnp.bfloat16
VMEM = pl.BlockSpec(memory_space=pltpu.VMEM)
SMEM = pl.BlockSpec(memory_space=pltpu.SMEM)
ANY = pl.BlockSpec(memory_space=pl.ANY)
DEPTH_FIRST = (((0,), (0,)), ((), ()))


def shape(dims, dtype):
    return jax.ShapeDtypeStruct(dims, dtype)


def params(mebibytes=24):
    return pltpu.CompilerParams(vmem_limit_bytes=mebibytes * 1024 * 1024)


def cost(slabs, moved):
    return pl.CostEstimate(flops=2 * 27 * C * C * slabs * ROWS, bytes_accessed=moved, transcendentals=0)


def inside(axis, side):
    at = lax.axis_index(axis)
    return at > 0 if side == 0 else at < lax.axis_size(axis) - 1


def held(value, axis, side):
    return jnp.where(inside(axis, side), value, jnp.zeros_like(value))


def brick_flags(occ_ref, brick):
    low_z = lax.broadcasted_iota(jnp.int32, (E, Z, C), 1) < E
    halves = [jnp.where(low_z, occ_ref[j, 0, brick], occ_ref[j, 1, brick]) for j in range(2)]
    return jnp.concatenate(halves, axis=0) == 1


def mask_slabs(part, source, mask_ref, s_ref, faces):
    zlo_ref, zhi_ref, ylo_ref, yhi_ref = faces
    for end in (0, X + 1):
        s_ref[end] = jnp.zeros((Y, Z, C), BF16)

    def one(brick, carry):
        span = pl.ds(brick * E, E)
        keep = mask_ref[brick].astype(F32) > 0.0
        value = jnp.where(keep[None], source[span].astype(F32), 0.0).astype(BF16)
        s_ref[pl.ds(brick * E + 1, E)] = value
        zlo_ref[part, span] = value[:, :, 0, :]
        zhi_ref[part, span] = value[:, :, Z - 1, :]
        ylo_ref[part, span] = value[:, 0]
        yhi_ref[part, span] = value[:, Y - 1]
        return carry

    lax.fori_loop(0, X // E, one, 0)


def mask_kernel(occ_ref, mask_ref):
    for brick in range(X // E):
        mask_ref[brick] = jnp.where(brick_flags(occ_ref, brick), 1.0, 0.0).astype(BF16)


def prepare_x_kernel(f_ref, mask_ref, s_ref, *faces):
    mask_slabs(0, f_ref, mask_ref, s_ref, faces)


def prepare_g_kernel(c_ref, mask_ref, *refs):
    given, s_ref, faces = refs[:4], refs[4], refs[5:]
    for face, ref in zip(faces, given, strict=True):
        face[0] = ref[0]
    mask_slabs(1, c_ref, mask_ref, s_ref, faces)


def prepare(occupancy, features, cotangent):
    slabs = shape((X + 2, Y, Z, C), BF16)
    own_cost = pl.CostEstimate(flops=1000, bytes_accessed=1000, transcendentals=0)
    mask = small_kernel(
        mask_kernel, shape((X // E, Y, Z, C), BF16), [jnp.transpose(occupancy, (1, 2, 0))], specs=[SMEM],
        flops=10**10,
    )
    fields, *given = pl.pallas_call(
        prepare_x_kernel,
        in_specs=[VMEM] * 2,
        out_specs=[VMEM] * 5,
        out_shape=[slabs] + [shape((1, X, Z, C), BF16)] * 4,
        compiler_params=params(),
        cost_estimate=own_cost,
    )(features, mask)
    cotangents, *faces = pl.pallas_call(
        prepare_g_kernel,
        in_specs=[VMEM] * 6,
        out_specs=[VMEM] * 5,
        out_shape=[slabs] + [shape((2, X, Z, C), BF16)] * 4,
        compiler_params=params(),
        cost_estimate=own_cost,
    )(cotangent, mask, *given)
    return (fields, cotangents), mask, faces


def moved_z(whole, step):
    rows = whole.shape[0] * whole.shape[1]
    flat = whole.reshape(rows, C)
    return pltpu.roll(flat, -step % rows, 0).reshape(whole.shape)


def put_slab(scratch, slot, center, ylo, yhi, zlo, zhi):
    whole = jnp.concatenate([ylo[None], center, yhi[None]], axis=0)
    scratch[1, slot] = whole
    whole = whole.astype(F32)
    at = lax.broadcasted_iota(jnp.int32, (Y + 2, Z, C), 1)
    low = zlo.astype(F32)[: Y + 2, None, :]
    high = zhi.astype(F32)[: Y + 2, None, :]
    scratch[0, slot] = jnp.where(at == 0, low, moved_z(whole, -1)).astype(BF16)
    scratch[2, slot] = jnp.where(at == Z - 1, high, moved_z(whole, 1)).astype(BF16)


def put_own(scratch, slot, center):
    scratch[1, slot, 1 : Y + 1] = center
    whole = center.astype(F32)
    at = lax.broadcasted_iota(jnp.int32, (Y, Z, C), 1)
    scratch[0, slot, 1 : Y + 1] = jnp.where(at == 0, 0.0, moved_z(whole, -1)).astype(BF16)
    scratch[2, slot, 1 : Y + 1] = jnp.where(at == Z - 1, 0.0, moved_z(whole, 1)).astype(BF16)


def patches(shifted, slots):
    pieces = []
    for ty in range(3):
        for tz in range(3):
            pieces.append(shifted[tz, :slots, ty : ty + Y].reshape(slots * ROWS, C))
    return jnp.concatenate(pieces, axis=1)


def put_far(scratch, slot, far_ref, part, side):
    slab = held(far_ref[part], "gx", side)
    rims = slab[Y + 2 :].reshape(-1, C)
    put_slab(scratch, slot, slab[:Y], slab[Y], slab[Y + 1], rims[:24], rims[24:])


def own_grad_kernel(first, spans, more, x_ref, g_ref, *refs):
    total, even, odd = refs[-3:]
    for shifted in (even, odd):
        shifted[:, :, 0:1] = jnp.zeros((3, SPAN, 1, Z, C), BF16)
        shifted[:, :, Y + 1 :] = jnp.zeros((3, SPAN, 1, Z, C), BF16)

    def put(shifted, x):
        for slot in range(SPAN):
            put_own(shifted, slot, x_ref[x + 1 + slot])

    def product(shifted, x):
        columns = [g_ref[x + 2 - tx : x + 2 - tx + SPAN].reshape(SPAN * ROWS, C) for tx in range(3)]
        beside = jnp.concatenate(columns, axis=1)
        return lax.dot_general(beside, patches(shifted, SPAN), DEPTH_FIRST, preferred_element_type=F32)

    put(even, first)
    made = product(even, first)
    if spans == 2:
        put(odd, first + SPAN)
    total[...] = refs[0][...] + made if more else made
    if spans == 2:
        total[...] += product(odd, first + SPAN)


def own_grad(slabs, first, spans, before, tie):
    more = before is not None
    return pl.pallas_call(
        lambda *refs: own_grad_kernel(first, spans, more, *refs),
        in_specs=[VMEM] * (2 + more) + [ANY],
        out_specs=VMEM,
        out_shape=shape((WIDE, TAPS), F32),
        scratch_shapes=[pltpu.VMEM((3, SPAN, Y + 2, Z, C), BF16)] * 2,
        compiler_params=params(),
        cost_estimate=cost(spans * SPAN, 8 << 20),
    )(*slabs, *([before] if more else []), tie)


def add_rim(total, row, stride, trio, face_ref):
    blank = jnp.zeros((1, Z, C), BF16)
    padded = jnp.concatenate([blank, face_ref[1], blank], axis=0)
    around = jnp.concatenate([padded[2 - tx : 2 - tx + X].reshape(X * Z, C) for tx in range(3)], axis=1)
    left = jnp.concatenate([a.astype(BF16).reshape(X * Z, C) for a in trio], axis=1)
    made = lax.dot_general(around, left, DEPTH_FIRST, preferred_element_type=F32)
    for k in range(3):
        start = (row + k * stride) * C
        total[:, start : start + C] += made[:, k * C : (k + 1) * C]


def z_rim_kernel(own_ref, gzlo, gzhi, nzlo, nzhi, total):
    total[...] = own_ref[...]
    at = lax.broadcasted_iota(jnp.int32, (X, Z, C), 1)
    for side, row, near, face in ((0, 0, nzlo, gzlo), (1, 2, nzhi, gzhi)):
        whole = held(near[0].astype(F32), "gz", side)
        before = jnp.where(at == 0, 0.0, moved_z(whole, -1))
        after = jnp.where(at == Z - 1, 0.0, moved_z(whole, 1))
        add_rim(total, row, 3, (before, whole, after), face)


def rim_grad_kernel(
    own_ref, g_ref, gylo, gyhi, nylo, nyhi, elo, ehi, far_lo, far_hi, keep_ref, send_ref, scratch, total
):
    total[...] = own_ref[...]
    for side, far, plane, tx in ((0, far_lo, 1, 0), (1, far_hi, X, 2)):
        put_far(scratch.at[:, side : side + 1], 0, far, 0, side)
        left = patches(scratch.at[:, side : side + 1], 1)
        beside = g_ref[plane].reshape(ROWS, C)
        total[tx * C : (tx + 1) * C] += lax.dot_general(
            beside, left, DEPTH_FIRST, preferred_element_type=F32
        )
    at = lax.broadcasted_iota(jnp.int32, (X, Z, C), 1)
    for side, row, near, edges, face in ((0, 0, nylo, elo, gylo), (1, 6, nyhi, ehi, gyhi)):
        whole = near[0].astype(F32)
        corners = held(edges[0].astype(F32), "gy", side)
        low = corners[0][:, None, :]
        high = corners[1][:, None, :]
        before = jnp.where(at == 0, low, moved_z(whole, -1))
        after = jnp.where(at == Z - 1, high, moved_z(whole, 1))
        add_rim(total, row, 1, (before, whole, after), face)

    scale = 1.0 / math.sqrt(SHARE * 128 * E**3)
    core = lax.axis_index("gx") % 2
    for mine in range(2):

        @pl.when(core == mine)
        def _():
            for tap in range(27):
                tx, row = tap // 9, tap % 9
                block = total[tx * C : (tx + 1) * C, row * C : (row + 1) * C].T * scale
                for side, ref in ((mine, keep_ref), (1 - mine, send_ref)):
                    start = tap * C - side * HALF
                    low, high = max(start, 0), min(start + C, HALF)
                    if low < high:
                        ref[low:high] = block[low - start : high - start]


def rim_grad(own, cotangents, operands):
    return pl.pallas_call(
        rim_grad_kernel,
        in_specs=[VMEM] * (2 + len(operands)),
        out_specs=[VMEM, VMEM],
        out_shape=[shape((HALF, C), F32)] * 2,
        scratch_shapes=[pltpu.VMEM((3, 2, Y + 2, Z, C), BF16), pltpu.VMEM((WIDE, TAPS), F32)],
        compiler_params=params(),
        cost_estimate=cost(3, 6 << 20),
    )(own, cotangents, *operands)


def conv_kernel(part, first, groups, following, mask_ref, *refs):
    starts, ends = first == 0, first + groups * GROUP == X
    refs = list(refs)
    slabs = [refs.pop(0) for _ in range(2)]
    rims = [refs.pop(0) for _ in range(4)]
    w_ref = refs.pop(0)
    far_lo = refs.pop(0) if starts else None
    far_hi = refs.pop(0) if ends else None
    before = None if starts else refs.pop(0)
    late_in = None if starts else refs.pop(0)
    ready = None if starts and part == 0 else refs.pop(0)
    late = None if ends else refs.pop(-5)
    o_ref, carry_ref, even, others, edge, made_ref, left = refs[-7:]
    odd = others.at[0]
    count = groups * GROUP
    own_copies = groups if ends else groups - 1
    late_copy = None
    if not starts:
        skip = 1 if first == GROUP else 0
        target = o_ref.at[pl.ds(first - GROUP - 1 + skip, GROUP - skip)]
        late_copy = pltpu.make_async_copy(late_in.at[pl.ds(skip, GROUP - skip)], target, left.at[groups + 1])
        late_copy.start()

    def put(shifted, at, x):
        for slot in range(GROUP):
            put_slab(shifted, slot, slabs[at][x + 1 + slot], *(ref[at, x + slot] for ref in rims))

    def finish(x, total):
        keep = mask_ref[jnp.maximum(x, 0) // E].astype(F32) > 0.0
        made_ref[x - first + 1] = jnp.where(keep, total.reshape(Y, Z, C), 0.0).astype(BF16)

    def copy(x, size, sem):
        source = made_ref.at[pl.ds(x - first, size)]
        return pltpu.make_async_copy(source, o_ref.at[pl.ds(x - 1, size)], left.at[sem])

    def group(shifted, x, sem, near, next_, opens):
        made = jnp.dot(patches(shifted, GROUP), w_ref[...], preferred_element_type=F32)

        def term(slot, tx):
            return made[slot * ROWS : (slot + 1) * ROWS, tx * C : (tx + 1) * C]

        if opens is True:
            made_ref[0] = jnp.zeros((Y, Z, C), BF16)
        else:
            finish(x - 1, near + term(0, 2))
        finish(x, next_ + term(0, 1) + term(1, 2))
        for slot in range(1, GROUP - 1):
            finish(x + slot, term(slot - 1, 0) + term(slot, 1) + term(slot + 1, 2))
        if opens is None:
            pl.when(sem == 0)(lambda: copy(x + 1, GROUP - 1, sem).start())
            pl.when(sem > 0)(lambda: copy(x, GROUP, sem).start())
        elif opens:
            if own_copies > 0:
                copy(x + 1, GROUP - 1, sem).start()
        elif ends:
            copy(x, GROUP, sem).start()
        else:
            pl.when(sem < own_copies)(lambda: copy(x, GROUP, sem).start())
        return term(GROUP - 2, 0) + term(GROUP - 1, 1), term(GROUP - 1, 0)

    if starts:
        put_far(edge, 0, far_lo, part, 0)
        near = jnp.zeros((ROWS, C), F32)
        next_ = jnp.dot(patches(edge, 1), w_ref[:, :C], preferred_element_type=F32)
    else:
        near, next_ = before[0], before[1]
    if groups > 3 and following is not None:
        if ready is None:
            put(even, part, 0)
        else:
            even[...] = ready[...]
        carry_ref[0] = near
        carry_ref[1] = next_

        def trip(i, carry):
            x = first + i * 2 * GROUP
            near, next_ = group(even, x, 2 * i, carry_ref[0], carry_ref[1], None if starts else False)
            put(odd, part, x + GROUP)
            near, next_ = group(odd, x + GROUP, 2 * i + 1, near, next_, False)
            after = i + 1 == groups // 2
            put(even, part, jnp.where(after, following[1], x + 2 * GROUP))
            carry_ref[0] = near
            carry_ref[1] = next_
            return carry

        lax.fori_loop(0, groups // 2, trip, 0)
        near = carry_ref[0]
    else:
        if ready is None:
            put(odd, part, first)
        shifted = [odd] if ready is None else [ready, odd, others.at[1], even]
        for at in range(groups):
            x = first + at * GROUP
            near, next_ = group(shifted[at], x, at, near, next_, starts and at == 0)
            if at + 1 < groups:
                put(shifted[at + 1], part, x + GROUP)
        if following is not None:
            put(even, *following)
        carry_ref[0] = near
        carry_ref[1] = next_
    if ends:
        put_far(edge, 0, far_hi, part, 1)
        last = jnp.dot(patches(edge, 1), w_ref[:, 2 * C :], preferred_element_type=F32)
        finish(X - 1, near + last)
        copy(X, 1, groups).start()
    if late is not None:
        late[...] = made_ref[count - GROUP : count]
    for sem in range(own_copies):
        x = first + sem * GROUP
        if starts and sem == 0:
            copy(x + 1, GROUP - 1, sem).wait()
        else:
            copy(x, GROUP, sem).wait()
    if ends:
        copy(X, 1, groups).wait()
    if late_copy is not None:
        late_copy.wait()


def conv_piece(part, first, groups, following, mask, field, far, weight, state, done, tie):
    operands = [mask, *field, weight]
    starts, ends = first == 0, first + groups * GROUP == X
    if starts:
        operands.append(far[0])
    if ends:
        operands.append(far[1])
    if not starts:
        operands += [state["carry"], state["late"]]
    if "ready" in state:
        operands.append(state["ready"])
    aliases = {}
    specs = [VMEM] * len(operands)
    operands.append(tie)
    specs.append(ANY)
    if not starts:
        aliases = {len(operands): 0}
        operands.append(done)
        specs.append(ANY)
    shifted = (3, GROUP, Y + 2, Z, C)
    more = following is not None
    buffers = [shape((2, ROWS, C), F32), shape(shifted, BF16)]
    kept = buffers + ([] if ends else [shape((GROUP, Y, Z, C), BF16)])
    scratch = [
        pltpu.VMEM((2, *shifted), BF16),
        pltpu.VMEM((3, 1, Y + 2, Z, C), BF16),
        pltpu.VMEM((groups * GROUP + 1, Y, Z, C), BF16),
        pltpu.SemaphoreType.DMA((groups + 2,)),
    ]
    if not more:
        scratch = [pltpu.VMEM(b.shape, b.dtype) for b in buffers] + scratch
        kept = [shape((8, C), F32)]

    def plain(*refs):
        conv_kernel(part, first, groups, following, *refs)

    def final(*refs):
        refs[-7][...] = jnp.zeros((8, C), F32)
        conv_kernel(part, first, groups, following, *refs[:-7], *refs[-6:])

    made, *kept = pl.pallas_call(
        plain if more else final,
        in_specs=specs,
        out_specs=[ANY] + [VMEM] * len(kept),
        out_shape=[shape((X, Y, Z, C), BF16)] + kept,
        scratch_shapes=scratch,
        input_output_aliases=aliases,
        compiler_params=params(),
        cost_estimate=cost(groups * GROUP, 2 << 20),
    )(*operands)
    return made, dict(zip(("carry", "ready", "late"), kept, strict=False))


def small_kernel(kernel, out_shape, operands, ties=(), specs=None, flops=1000):
    count = len(operands)

    def run(*refs):
        kernel(*refs[:count], *refs[count + len(ties) :])

    return pl.pallas_call(
        run,
        in_specs=(specs or [VMEM] * count) + [ANY] * len(ties),
        out_specs=jax.tree.map(lambda _: VMEM, out_shape),
        out_shape=out_shape,
        compiler_params=params(),
        cost_estimate=pl.CostEstimate(flops=flops, bytes_accessed=1 << 20, transcendentals=0),
    )(*operands, *ties)


def copy_kernel(a, b, c, d):
    c[...] = a[...]
    d[...] = b[...]


def edge_kernel(zlo, zhi, lo, hi):
    for side, ref in enumerate((zlo, zhi)):
        lo[:, side] = held(ref[:, :, 0, :], "gz", side)
        hi[:, side] = held(ref[:, :, Y - 1, :], "gz", side)


def message_kernel(x_ref, g_ref, ylo, yhi, zlo, zhi, elo, ehi, held_ylo, held_yhi, col_lo, col_hi, to_lo, to_hi):
    held_ylo[...] = held(ylo[...], "gy", 0)
    held_yhi[...] = held(yhi[...], "gy", 1)
    tail = jnp.zeros((2, X, 24 - Y - 2, C), F32)
    for side, (near, col) in enumerate(((zlo, col_lo), (zhi, col_hi))):
        own = held(near[...].astype(F32), "gz", side)
        low = held(elo[:, side].astype(F32), "gy", 0)[:, :, None, :]
        high = held(ehi[:, side].astype(F32), "gy", 1)[:, :, None, :]
        col[...] = jnp.concatenate([low, own, high, tail], axis=2).astype(BF16)
    for at, to in ((0, to_lo), (X - 1, to_hi)):
        to[0, :Y] = x_ref[at + 1]
        to[1, :Y] = g_ref[at + 1]
        to[:, Y] = held_ylo[:, at]
        to[:, Y + 1] = held_yhi[:, at]
        rims = jnp.concatenate([col_lo[:, at], col_hi[:, at]], axis=1)
        to[:, Y + 2 :] = rims.reshape(2, 3, Z, C)


def arrange_kernel(w_ref, forward, flipped):
    for tap in range(27):
        tx, row = tap // 9, tap % 9
        forward[row * C : (row + 1) * C, tx * C : (tx + 1) * C] = w_ref[tap]
        flipped[row * C : (row + 1) * C, tx * C : (tx + 1) * C] = w_ref[26 - tap].astype(F32).T.astype(BF16)


ORDER = ("zyx", "yxz")


def first_place(core):
    return lax.axis_index("gx") // 2 * (1 - core) + lax.axis_index("gy") * core


def pairs(turn, step):
    found = []
    for z in range(4):
        for core in range(2):
            for y in range(4):
                for x in range(4):
                    at = {"z": z, "y": y, "x": x}
                    to = dict(at)
                    to[ORDER[core][turn]] ^= step
                    found.append(tuple(((2 * p["z"] + core) * 4 + p["y"]) * 4 + p["x"] for p in (at, to)))
    return found


def exchange(turn, values):
    steps = zip((1, 2, 3), values, strict=True)
    return [lax.ppermute(value, ("gx", "gy", "gz"), pairs(turn, step)) for step, value in steps]


def deal(terms, ties):
    rows = terms[0].shape[0] // 4

    def kernel(*refs):
        me = first_place(lax.axis_index("gx") % 2)
        for step in range(4):
            at = pl.ds((me ^ step) * rows, rows)
            total = refs[0][at]
            for ref in refs[1 : len(terms)]:
                total = total + ref[at]
            refs[len(terms) + step][...] = total

    return small_kernel(kernel, [shape((rows, C), F32)] * 4, terms, ties)


def sum_kernel(a, b, c, d, o):
    o[...] = (a[...] + c[...]) + (b[...] + d[...])


def write(sources, mine, target, tie):
    arrays = [a for a, _ in sources]
    rows = HALF // 4
    count = sum(len(steps) for _, steps in sources)

    def kernel(*refs):
        o_ref, left = refs[-2:]
        at = lax.axis_index("gx")
        half = at % 2 if mine else 1 - at % 2
        me = first_place(half)
        for act in ("start", "wait"):
            sem = 0
            for ref, (_, steps) in zip(refs, sources, strict=False):
                for at, step in enumerate(steps):
                    chunk = half * 4 + (me ^ step)

                    place = o_ref.at[pl.ds(chunk * rows, rows)]
                    copy = pltpu.make_async_copy(ref.at[pl.ds(at * rows, rows)], place, left.at[sem])
                    if act == "start":
                        copy.start()
                    else:
                        copy.wait()
                    sem += 1

    operands = arrays + [tie] + ([] if target is None else [target])
    return pl.pallas_call(
        kernel,
        in_specs=[VMEM] * len(arrays) + [ANY] * (len(operands) - len(arrays)),
        out_specs=ANY,
        out_shape=shape((27 * C, C), F32),
        scratch_shapes=[pltpu.SemaphoreType.DMA((count,))],
        input_output_aliases={} if target is None else {len(operands) - 1: 0},
        compiler_params=params(),
        cost_estimate=pl.CostEstimate(flops=1000, bytes_accessed=1 << 20, transcendentals=0),
    )(*operands)


def join_kernel(a, b, c, o):
    rows = a.shape[0]
    for k, ref in enumerate((a, b, c)):
        o[k * rows : (k + 1) * rows] = ref[...]


def shift(value, axis, step):
    count = lax.axis_size(axis)
    return lax.ppermute(value, axis, [(i, (i + step) % count) for i in range(count)])


def body(features, occupancy, weight, cotangent):
    slabs, mask, faces = prepare(occupancy, features, cotangent)
    zlo, zhi, ylo, yhi = faces
    near_zlo = shift(zhi, "gz", 1)
    near_zhi = shift(zlo, "gz", -1)
    own = own_grad(slabs, 0, 1, None, zlo)
    face = shape((2, X, Z, C), BF16)
    to_ylo, to_yhi = small_kernel(copy_kernel, [face, face], [ylo, yhi], [own])
    near_ylo = shift(to_yhi, "gy", 1)
    near_yhi = shift(to_ylo, "gy", -1)
    own = own_grad(slabs, SPAN, 1, own, to_ylo)

    edge = shape((2, 2, X, C), BF16)
    edge_lo, edge_hi = small_kernel(edge_kernel, [edge, edge], [near_zlo, near_zhi], [own])
    edges = (shift(edge_hi, "gy", 1), shift(edge_lo, "gy", -1))
    forward, flipped = small_kernel(
        arrange_kernel, [shape((TAPS, WIDE), BF16)] * 2, [weight.reshape(27, C, C)], [edge_lo]
    )
    own = small_kernel(
        z_rim_kernel, shape((WIDE, TAPS), F32), [own, zlo, zhi, near_zlo, near_zhi], [edge_lo]
    )

    column = shape((2, X, 24, C), BF16)
    message = shape((2, Y + 5, Z, C), BF16)
    held_ylo, held_yhi, col_lo, col_hi, to_lo, to_hi = small_kernel(
        message_kernel,
        [face, face, column, column, message, message],
        [*slabs, near_ylo, near_yhi, near_zlo, near_zhi, *edges],
        [forward, own],
    )
    far = (shift(to_hi, "gx", 1), shift(to_lo, "gx", -1))
    own = own_grad(slabs, X // 2, 2, own, to_lo)
    keep, send = rim_grad(own, slabs[1], [ylo, yhi, held_ylo, held_yhi, *edges, *far])

    field = [*slabs, held_ylo, held_yhi, col_lo, col_hi]
    made = [None, None]
    weights = (forward, flipped)
    order = [(0, 0, 1), (0, 4, 4), (0, 20, 3), (1, 0, 4), (1, 16, 4)]
    state = {}

    def convolve(tie):
        part, first, groups = order.pop(0)
        following = order[0][:2] if order else None
        made[part], kept = conv_piece(
            part, first, groups, following, mask, field, far, weights[part], state, made[part], tie
        )
        state.update(kept)
        return [kept["carry"]]

    swap = [(i, i ^ 1) for i in range(8)]
    came = lax.ppermute(send, "gx", swap)
    ties = convolve(send)
    own, *parts = deal([keep, came], ties)
    came = exchange(0, parts)
    chunk, ties = own, convolve(parts[0])
    for turn in (1, 2):
        chunk = small_kernel(sum_kernel, shape(chunk.shape, F32), [chunk, *came], ties)
        came = exchange(turn, [chunk] * 3)
        ties = convolve(chunk)
    chunk = small_kernel(sum_kernel, shape(chunk.shape, F32), [chunk, *came], ties)
    came = exchange(0, [chunk] * 3)
    beside = lax.ppermute(chunk, "gx", swap)
    ties = convolve(chunk)
    joined = small_kernel(join_kernel, shape((3 * chunk.shape[0], C), F32), came, [beside, *ties])
    others = lax.ppermute(joined, "gx", swap)
    full = write([(chunk, (0,)), (joined, (1, 2, 3))], True, None, joined)
    full = write([(beside, (0,))], False, full, joined)
    full = write([(others, (1, 2, 3))], False, full, joined)
    return (made[0], made[1], full.reshape(3, 3, 3, C, C))


def solution(mesh):
    placed = (P("gx", "gy", "gz", None), P("gx", "gy", "gz"), P(), P("gx", "gy", "gz", None))
    return jax.shard_map(
        body,
        mesh=mesh,
        in_specs=placed,
        out_specs=(P("gx", "gy", "gz", None), P("gx", "gy", "gz", None), P()),
        check_vma=False,
    )
```

```python
import math

import jax
import jax.numpy as jnp
from jax import lax
from jax.experimental import pallas as pl
from jax.experimental.pallas import tpu as pltpu
from jax.sharding import PartitionSpec as P

SHARE = 8
X, Y, Z, C = 32, 16, 16, 128
E = 8
ROWS = Y * Z
GROUP = 4
SPAN = 8
TAPS = 9 * C
WIDE = 3 * C
HALF = 27 * C // 2
F32 = jnp.float32
BF16 = jnp.bfloat16
VMEM = pl.BlockSpec(memory_space=pltpu.VMEM)
SMEM = pl.BlockSpec(memory_space=pltpu.SMEM)
ANY = pl.BlockSpec(memory_space=pl.ANY)
DEPTH_FIRST = (((0,), (0,)), ((), ()))


def shape(dims, dtype):
    return jax.ShapeDtypeStruct(dims, dtype)


def params(mebibytes=24):
    return pltpu.CompilerParams(vmem_limit_bytes=mebibytes * 1024 * 1024)


def cost(slabs, moved):
    return pl.CostEstimate(flops=2 * 27 * C * C * slabs * ROWS, bytes_accessed=moved, transcendentals=0)


def inside(axis, side):
    at = lax.axis_index(axis)
    return at > 0 if side == 0 else at < lax.axis_size(axis) - 1


def held(value, axis, side):
    return jnp.where(inside(axis, side), value, jnp.zeros_like(value))


def brick_flags(occ_ref, brick):
    low_z = lax.broadcasted_iota(jnp.int32, (E, Z, C), 1) < E
    halves = [jnp.where(low_z, occ_ref[j, 0, brick], occ_ref[j, 1, brick]) for j in range(2)]
    return jnp.concatenate(halves, axis=0) == 1


def mask_slabs(part, source, mask_ref, s_ref, faces):
    zlo_ref, zhi_ref, ylo_ref, yhi_ref = faces
    for end in (0, X + 1):
        s_ref[end] = jnp.zeros((Y, Z, C), BF16)

    def one(brick, carry):
        span = pl.ds(brick * E, E)
        keep = mask_ref[brick].astype(F32) > 0.0
        value = jnp.where(keep[None], source[span].astype(F32), 0.0).astype(BF16)
        s_ref[pl.ds(brick * E + 1, E)] = value
        zlo_ref[part, span] = value[:, :, 0, :]
        zhi_ref[part, span] = value[:, :, Z - 1, :]
        ylo_ref[part, span] = value[:, 0]
        yhi_ref[part, span] = value[:, Y - 1]
        return carry

    lax.fori_loop(0, X // E, one, 0)


def first_kernel(o_ref):
    o_ref[...] = jnp.zeros_like(o_ref)


def mask_kernel(occ_ref, mask_ref):
    for brick in range(X // E):
        mask_ref[brick] = jnp.where(brick_flags(occ_ref, brick), 1.0, 0.0).astype(BF16)


def prepare_x_kernel(f_ref, mask_ref, s_ref, *faces):
    mask_slabs(0, f_ref, mask_ref, s_ref, faces)


def prepare_g_kernel(c_ref, mask_ref, *refs):
    given, s_ref, faces = refs[:4], refs[4], refs[5:]
    for face, ref in zip(faces, given, strict=True):
        face[0] = ref[0]
    mask_slabs(1, c_ref, mask_ref, s_ref, faces)


def prepare(occupancy, features, cotangent):
    slabs = shape((X + 2, Y, Z, C), BF16)
    own_cost = pl.CostEstimate(flops=1000, bytes_accessed=1000, transcendentals=0)
    lead = small_kernel(first_kernel, shape((8, C), F32), [], flops=10**10)
    mask = small_kernel(
        mask_kernel,
        shape((X // E, Y, Z, C), BF16),
        [jnp.transpose(occupancy, (1, 2, 0))],
        [lead],
        specs=[SMEM],
    )
    fields, *given = pl.pallas_call(
        prepare_x_kernel,
        in_specs=[VMEM] * 2,
        out_specs=[VMEM] * 5,
        out_shape=[slabs] + [shape((1, X, Z, C), BF16)] * 4,
        compiler_params=params(),
        cost_estimate=own_cost,
    )(features, mask)
    cotangents, *faces = pl.pallas_call(
        prepare_g_kernel,
        in_specs=[VMEM] * 6,
        out_specs=[VMEM] * 5,
        out_shape=[slabs] + [shape((2, X, Z, C), BF16)] * 4,
        compiler_params=params(),
        cost_estimate=own_cost,
    )(cotangent, mask, *given)
    return (fields, cotangents), mask, faces


def moved_z(whole, step):
    rows = whole.shape[0] * whole.shape[1]
    flat = whole.reshape(rows, C)
    return pltpu.roll(flat, -step % rows, 0).reshape(whole.shape)


def put_slab(scratch, slot, center, ylo, yhi, zlo, zhi):
    whole = jnp.concatenate([ylo[None], center, yhi[None]], axis=0)
    scratch[1, slot] = whole
    whole = whole.astype(F32)
    at = lax.broadcasted_iota(jnp.int32, (Y + 2, Z, C), 1)
    low = zlo.astype(F32)[: Y + 2, None, :]
    high = zhi.astype(F32)[: Y + 2, None, :]
    scratch[0, slot] = jnp.where(at == 0, low, moved_z(whole, -1)).astype(BF16)
    scratch[2, slot] = jnp.where(at == Z - 1, high, moved_z(whole, 1)).astype(BF16)


def put_own(scratch, slot, center):
    scratch[1, slot, 1 : Y + 1] = center
    whole = center.astype(F32)
    at = lax.broadcasted_iota(jnp.int32, (Y, Z, C), 1)
    scratch[0, slot, 1 : Y + 1] = jnp.where(at == 0, 0.0, moved_z(whole, -1)).astype(BF16)
    scratch[2, slot, 1 : Y + 1] = jnp.where(at == Z - 1, 0.0, moved_z(whole, 1)).astype(BF16)


def patches(shifted, slots):
    pieces = []
    for ty in range(3):
        for tz in range(3):
            pieces.append(shifted[tz, :slots, ty : ty + Y].reshape(slots * ROWS, C))
    return jnp.concatenate(pieces, axis=1)


def put_far(scratch, slot, far_ref, part, side):
    slab = held(far_ref[part], "gx", side)
    rims = slab[Y + 2 :].reshape(-1, C)
    put_slab(scratch, slot, slab[:Y], slab[Y], slab[Y + 1], rims[:24], rims[24:])


def own_grad_kernel(first, spans, more, x_ref, g_ref, *refs):
    total, even, odd = refs[-3:]
    for shifted in (even, odd):
        shifted[:, :, 0:1] = jnp.zeros((3, SPAN, 1, Z, C), BF16)
        shifted[:, :, Y + 1 :] = jnp.zeros((3, SPAN, 1, Z, C), BF16)

    def put(shifted, x):
        for slot in range(SPAN):
            put_own(shifted, slot, x_ref[x + 1 + slot])

    def product(shifted, x):
        columns = [g_ref[x + 2 - tx : x + 2 - tx + SPAN].reshape(SPAN * ROWS, C) for tx in range(3)]
        beside = jnp.concatenate(columns, axis=1)
        return lax.dot_general(beside, patches(shifted, SPAN), DEPTH_FIRST, preferred_element_type=F32)

    put(even, first)
    made = product(even, first)
    if spans == 2:
        put(odd, first + SPAN)
    total[...] = refs[0][...] + made if more else made
    if spans == 2:
        total[...] += product(odd, first + SPAN)


def own_grad(slabs, first, spans, before, tie):
    more = before is not None
    return pl.pallas_call(
        lambda *refs: own_grad_kernel(first, spans, more, *refs),
        in_specs=[VMEM] * (2 + more) + [ANY],
        out_specs=VMEM,
        out_shape=shape((WIDE, TAPS), F32),
        scratch_shapes=[pltpu.VMEM((3, SPAN, Y + 2, Z, C), BF16)] * 2,
        compiler_params=params(),
        cost_estimate=cost(spans * SPAN, 8 << 20),
    )(*slabs, *([before] if more else []), tie)


def add_rim(total, row, stride, trio, face_ref):
    blank = jnp.zeros((1, Z, C), BF16)
    padded = jnp.concatenate([blank, face_ref[1], blank], axis=0)
    around = jnp.concatenate([padded[2 - tx : 2 - tx + X].reshape(X * Z, C) for tx in range(3)], axis=1)
    left = jnp.concatenate([a.astype(BF16).reshape(X * Z, C) for a in trio], axis=1)
    made = lax.dot_general(around, left, DEPTH_FIRST, preferred_element_type=F32)
    for k in range(3):
        start = (row + k * stride) * C
        total[:, start : start + C] += made[:, k * C : (k + 1) * C]


def z_rim_kernel(own_ref, gzlo, gzhi, nzlo, nzhi, total):
    total[...] = own_ref[...]
    at = lax.broadcasted_iota(jnp.int32, (X, Z, C), 1)
    for side, row, near, face in ((0, 0, nzlo, gzlo), (1, 2, nzhi, gzhi)):
        whole = held(near[0].astype(F32), "gz", side)
        before = jnp.where(at == 0, 0.0, moved_z(whole, -1))
        after = jnp.where(at == Z - 1, 0.0, moved_z(whole, 1))
        add_rim(total, row, 3, (before, whole, after), face)


def rim_grad_kernel(
    own_ref, g_ref, gylo, gyhi, nylo, nyhi, elo, ehi, far_lo, far_hi, keep_ref, send_ref, scratch, total
):
    total[...] = own_ref[...]
    for side, far, plane, tx in ((0, far_lo, 1, 0), (1, far_hi, X, 2)):
        put_far(scratch.at[:, side : side + 1], 0, far, 0, side)
        left = patches(scratch.at[:, side : side + 1], 1)
        beside = g_ref[plane].reshape(ROWS, C)
        total[tx * C : (tx + 1) * C] += lax.dot_general(
            beside, left, DEPTH_FIRST, preferred_element_type=F32
        )
    at = lax.broadcasted_iota(jnp.int32, (X, Z, C), 1)
    for side, row, near, edges, face in ((0, 0, nylo, elo, gylo), (1, 6, nyhi, ehi, gyhi)):
        whole = near[0].astype(F32)
        corners = held(edges[0].astype(F32), "gy", side)
        low = corners[0][:, None, :]
        high = corners[1][:, None, :]
        before = jnp.where(at == 0, low, moved_z(whole, -1))
        after = jnp.where(at == Z - 1, high, moved_z(whole, 1))
        add_rim(total, row, 1, (before, whole, after), face)

    scale = 1.0 / math.sqrt(SHARE * 128 * E**3)
    core = lax.axis_index("gx") % 2
    for mine in range(2):

        @pl.when(core == mine)
        def _():
            for tap in range(27):
                tx, row = tap // 9, tap % 9
                block = total[tx * C : (tx + 1) * C, row * C : (row + 1) * C].T * scale
                for side, ref in ((mine, keep_ref), (1 - mine, send_ref)):
                    start = tap * C - side * HALF
                    low, high = max(start, 0), min(start + C, HALF)
                    if low < high:
                        ref[low:high] = block[low - start : high - start]


def rim_grad(own, cotangents, operands):
    return pl.pallas_call(
        rim_grad_kernel,
        in_specs=[VMEM] * (2 + len(operands)),
        out_specs=[VMEM, VMEM],
        out_shape=[shape((HALF, C), F32)] * 2,
        scratch_shapes=[pltpu.VMEM((3, 2, Y + 2, Z, C), BF16), pltpu.VMEM((WIDE, TAPS), F32)],
        compiler_params=params(),
        cost_estimate=cost(3, 6 << 20),
    )(own, cotangents, *operands)


def conv_kernel(part, first, groups, following, mask_ref, *refs):
    starts, ends = first == 0, first + groups * GROUP == X
    refs = list(refs)
    slabs = [refs.pop(0) for _ in range(2)]
    rims = [refs.pop(0) for _ in range(4)]
    w_ref = refs.pop(0)
    far_lo = refs.pop(0) if starts else None
    far_hi = refs.pop(0) if ends else None
    before = None if starts else refs.pop(0)
    late_in = None if starts else refs.pop(0)
    ready = None if starts and part == 0 else refs.pop(0)
    late = None if ends else refs.pop(-5)
    o_ref, carry_ref, even, others, edge, made_ref, left = refs[-7:]
    odd = others.at[0]
    count = groups * GROUP
    own_copies = groups if ends else groups - 1
    late_copy = None
    if not starts:
        skip = 1 if first == GROUP else 0
        target = o_ref.at[pl.ds(first - GROUP - 1 + skip, GROUP - skip)]
        late_copy = pltpu.make_async_copy(late_in.at[pl.ds(skip, GROUP - skip)], target, left.at[groups + 1])
        late_copy.start()

    def put(shifted, at, x):
        for slot in range(GROUP):
            put_slab(shifted, slot, slabs[at][x + 1 + slot], *(ref[at, x + slot] for ref in rims))

    def finish(x, total):
        keep = mask_ref[jnp.maximum(x, 0) // E].astype(F32) > 0.0
        made_ref[x - first + 1] = jnp.where(keep, total.reshape(Y, Z, C), 0.0).astype(BF16)

    def copy(x, size, sem):
        source = made_ref.at[pl.ds(x - first, size)]
        return pltpu.make_async_copy(source, o_ref.at[pl.ds(x - 1, size)], left.at[sem])

    def group(shifted, x, sem, near, next_, opens):
        made = jnp.dot(patches(shifted, GROUP), w_ref[...], preferred_element_type=F32)

        def term(slot, tx):
            return made[slot * ROWS : (slot + 1) * ROWS, tx * C : (tx + 1) * C]

        if opens is True:
            made_ref[0] = jnp.zeros((Y, Z, C), BF16)
        else:
            finish(x - 1, near + term(0, 2))
        finish(x, next_ + term(0, 1) + term(1, 2))
        for slot in range(1, GROUP - 1):
            finish(x + slot, term(slot - 1, 0) + term(slot, 1) + term(slot + 1, 2))
        if opens is None:
            pl.when(sem == 0)(lambda: copy(x + 1, GROUP - 1, sem).start())
            pl.when(sem > 0)(lambda: copy(x, GROUP, sem).start())
        elif opens:
            if own_copies > 0:
                copy(x + 1, GROUP - 1, sem).start()
        elif ends:
            copy(x, GROUP, sem).start()
        else:
            pl.when(sem < own_copies)(lambda: copy(x, GROUP, sem).start())
        return term(GROUP - 2, 0) + term(GROUP - 1, 1), term(GROUP - 1, 0)

    if starts:
        put_far(edge, 0, far_lo, part, 0)
        near = jnp.zeros((ROWS, C), F32)
        next_ = jnp.dot(patches(edge, 1), w_ref[:, :C], preferred_element_type=F32)
    else:
        near, next_ = before[0], before[1]
    if groups > 3 and following is not None:
        if ready is None:
            put(even, part, 0)
        else:
            even[...] = ready[...]
        carry_ref[0] = near
        carry_ref[1] = next_

        def trip(i, carry):
            x = first + i * 2 * GROUP
            near, next_ = group(even, x, 2 * i, carry_ref[0], carry_ref[1], None if starts else False)
            put(odd, part, x + GROUP)
            near, next_ = group(odd, x + GROUP, 2 * i + 1, near, next_, False)
            after = i + 1 == groups // 2
            put(even, part, jnp.where(after, following[1], x + 2 * GROUP))
            carry_ref[0] = near
            carry_ref[1] = next_
            return carry

        lax.fori_loop(0, groups // 2, trip, 0)
        near = carry_ref[0]
    else:
        if ready is None:
            put(odd, part, first)
        shifted = [odd] if ready is None else [ready, odd, others.at[1], even]
        for at in range(groups):
            x = first + at * GROUP
            near, next_ = group(shifted[at], x, at, near, next_, starts and at == 0)
            if at + 1 < groups:
                put(shifted[at + 1], part, x + GROUP)
        if following is not None:
            put(even, *following)
        carry_ref[0] = near
        carry_ref[1] = next_
    if ends:
        put_far(edge, 0, far_hi, part, 1)
        last = jnp.dot(patches(edge, 1), w_ref[:, 2 * C :], preferred_element_type=F32)
        finish(X - 1, near + last)
        copy(X, 1, groups).start()
    if late is not None:
        late[...] = made_ref[count - GROUP : count]
    for sem in range(own_copies):
        x = first + sem * GROUP
        if starts and sem == 0:
            copy(x + 1, GROUP - 1, sem).wait()
        else:
            copy(x, GROUP, sem).wait()
    if ends:
        copy(X, 1, groups).wait()
    if late_copy is not None:
        late_copy.wait()


def conv_piece(part, first, groups, following, mask, field, far, weight, state, done, tie):
    operands = [mask, *field, weight]
    starts, ends = first == 0, first + groups * GROUP == X
    if starts:
        operands.append(far[0])
    if ends:
        operands.append(far[1])
    if not starts:
        operands += [state["carry"], state["late"]]
    if "ready" in state:
        operands.append(state["ready"])
    aliases = {}
    specs = [VMEM] * len(operands)
    operands.append(tie)
    specs.append(ANY)
    if not starts:
        aliases = {len(operands): 0}
        operands.append(done)
        specs.append(ANY)
    shifted = (3, GROUP, Y + 2, Z, C)
    more = following is not None
    buffers = [shape((2, ROWS, C), F32), shape(shifted, BF16)]
    kept = buffers + ([] if ends else [shape((GROUP, Y, Z, C), BF16)])
    scratch = [
        pltpu.VMEM((2, *shifted), BF16),
        pltpu.VMEM((3, 1, Y + 2, Z, C), BF16),
        pltpu.VMEM((groups * GROUP + 1, Y, Z, C), BF16),
        pltpu.SemaphoreType.DMA((groups + 2,)),
    ]
    if not more:
        scratch = [pltpu.VMEM(b.shape, b.dtype) for b in buffers] + scratch
        kept = [shape((8, C), F32)]

    def plain(*refs):
        conv_kernel(part, first, groups, following, *refs)

    def final(*refs):
        refs[-7][...] = jnp.zeros((8, C), F32)
        conv_kernel(part, first, groups, following, *refs[:-7], *refs[-6:])

    made, *kept = pl.pallas_call(
        plain if more else final,
        in_specs=specs,
        out_specs=[ANY] + [VMEM] * len(kept),
        out_shape=[shape((X, Y, Z, C), BF16)] + kept,
        scratch_shapes=scratch,
        input_output_aliases=aliases,
        compiler_params=params(),
        cost_estimate=cost(groups * GROUP, 2 << 20),
    )(*operands)
    return made, dict(zip(("carry", "ready", "late"), kept, strict=False))


def small_kernel(kernel, out_shape, operands, ties=(), specs=None, flops=1000):
    count = len(operands)

    def run(*refs):
        kernel(*refs[:count], *refs[count + len(ties) :])

    return pl.pallas_call(
        run,
        in_specs=(specs or [VMEM] * count) + [ANY] * len(ties),
        out_specs=jax.tree.map(lambda _: VMEM, out_shape),
        out_shape=out_shape,
        compiler_params=params(),
        cost_estimate=pl.CostEstimate(flops=flops, bytes_accessed=1 << 20, transcendentals=0),
    )(*operands, *ties)


def copy_kernel(a, b, c, d):
    c[...] = a[...]
    d[...] = b[...]


def edge_kernel(zlo, zhi, lo, hi):
    for side, ref in enumerate((zlo, zhi)):
        lo[:, side] = held(ref[:, :, 0, :], "gz", side)
        hi[:, side] = held(ref[:, :, Y - 1, :], "gz", side)


def message_kernel(x_ref, g_ref, ylo, yhi, zlo, zhi, elo, ehi, held_ylo, held_yhi, col_lo, col_hi, to_lo, to_hi):
    held_ylo[...] = held(ylo[...], "gy", 0)
    held_yhi[...] = held(yhi[...], "gy", 1)
    tail = jnp.zeros((2, X, 24 - Y - 2, C), F32)
    for side, (near, col) in enumerate(((zlo, col_lo), (zhi, col_hi))):
        own = held(near[...].astype(F32), "gz", side)
        low = held(elo[:, side].astype(F32), "gy", 0)[:, :, None, :]
        high = held(ehi[:, side].astype(F32), "gy", 1)[:, :, None, :]
        col[...] = jnp.concatenate([low, own, high, tail], axis=2).astype(BF16)
    for at, to in ((0, to_lo), (X - 1, to_hi)):
        to[0, :Y] = x_ref[at + 1]
        to[1, :Y] = g_ref[at + 1]
        to[:, Y] = held_ylo[:, at]
        to[:, Y + 1] = held_yhi[:, at]
        rims = jnp.concatenate([col_lo[:, at], col_hi[:, at]], axis=1)
        to[:, Y + 2 :] = rims.reshape(2, 3, Z, C)


def arrange_kernel(w_ref, forward, flipped):
    for tap in range(27):
        tx, row = tap // 9, tap % 9
        forward[row * C : (row + 1) * C, tx * C : (tx + 1) * C] = w_ref[tap]
        flipped[row * C : (row + 1) * C, tx * C : (tx + 1) * C] = w_ref[26 - tap].astype(F32).T.astype(BF16)


ORDER = ("zyx", "yxz")


def first_place(core):
    return lax.axis_index("gx") // 2 * (1 - core) + lax.axis_index("gy") * core


def pairs(turn, step):
    found = []
    for z in range(4):
        for core in range(2):
            for y in range(4):
                for x in range(4):
                    at = {"z": z, "y": y, "x": x}
                    to = dict(at)
                    to[ORDER[core][turn]] ^= step
                    found.append(tuple(((2 * p["z"] + core) * 4 + p["y"]) * 4 + p["x"] for p in (at, to)))
    return found


def exchange(turn, values):
    steps = zip((1, 2, 3), values, strict=True)
    return [lax.ppermute(value, ("gx", "gy", "gz"), pairs(turn, step)) for step, value in steps]


def deal(terms, ties):
    rows = terms[0].shape[0] // 4

    def kernel(*refs):
        me = first_place(lax.axis_index("gx") % 2)
        for step in range(4):
            at = pl.ds((me ^ step) * rows, rows)
            total = refs[0][at]
            for ref in refs[1 : len(terms)]:
                total = total + ref[at]
            refs[len(terms) + step][...] = total

    return small_kernel(kernel, [shape((rows, C), F32)] * 4, terms, ties)


def sum_kernel(a, b, c, d, o):
    o[...] = (a[...] + c[...]) + (b[...] + d[...])


def write(sources, mine, target, tie):
    arrays = [a for a, _ in sources]
    rows = HALF // 4
    count = sum(len(steps) for _, steps in sources)

    def kernel(*refs):
        o_ref, left = refs[-2:]
        at = lax.axis_index("gx")
        half = at % 2 if mine else 1 - at % 2
        me = first_place(half)
        for act in ("start", "wait"):
            sem = 0
            for ref, (_, steps) in zip(refs, sources, strict=False):
                for at, step in enumerate(steps):
                    chunk = half * 4 + (me ^ step)

                    place = o_ref.at[pl.ds(chunk * rows, rows)]
                    copy = pltpu.make_async_copy(ref.at[pl.ds(at * rows, rows)], place, left.at[sem])
                    if act == "start":
                        copy.start()
                    else:
                        copy.wait()
                    sem += 1

    operands = arrays + [tie] + ([] if target is None else [target])
    return pl.pallas_call(
        kernel,
        in_specs=[VMEM] * len(arrays) + [ANY] * (len(operands) - len(arrays)),
        out_specs=ANY,
        out_shape=shape((27 * C, C), F32),
        scratch_shapes=[pltpu.SemaphoreType.DMA((count,))],
        input_output_aliases={} if target is None else {len(operands) - 1: 0},
        compiler_params=params(),
        cost_estimate=pl.CostEstimate(flops=1000, bytes_accessed=1 << 20, transcendentals=0),
    )(*operands)


def join_kernel(a, b, c, o):
    rows = a.shape[0]
    for k, ref in enumerate((a, b, c)):
        o[k * rows : (k + 1) * rows] = ref[...]


def shift(value, axis, step):
    count = lax.axis_size(axis)
    return lax.ppermute(value, axis, [(i, (i + step) % count) for i in range(count)])


def body(features, occupancy, weight, cotangent):
    slabs, mask, faces = prepare(occupancy, features, cotangent)
    zlo, zhi, ylo, yhi = faces
    near_zlo = shift(zhi, "gz", 1)
    near_zhi = shift(zlo, "gz", -1)
    own = own_grad(slabs, 0, 1, None, zlo)
    face = shape((2, X, Z, C), BF16)
    to_ylo, to_yhi = small_kernel(copy_kernel, [face, face], [ylo, yhi], [own])
    near_ylo = shift(to_yhi, "gy", 1)
    near_yhi = shift(to_ylo, "gy", -1)
    own = own_grad(slabs, SPAN, 1, own, to_ylo)

    edge = shape((2, 2, X, C), BF16)
    edge_lo, edge_hi = small_kernel(edge_kernel, [edge, edge], [near_zlo, near_zhi], [own])
    edges = (shift(edge_hi, "gy", 1), shift(edge_lo, "gy", -1))
    forward, flipped = small_kernel(
        arrange_kernel, [shape((TAPS, WIDE), BF16)] * 2, [weight.reshape(27, C, C)], [edge_lo]
    )
    own = small_kernel(
        z_rim_kernel, shape((WIDE, TAPS), F32), [own, zlo, zhi, near_zlo, near_zhi], [edge_lo]
    )

    column = shape((2, X, 24, C), BF16)
    message = shape((2, Y + 5, Z, C), BF16)
    held_ylo, held_yhi, col_lo, col_hi, to_lo, to_hi = small_kernel(
        message_kernel,
        [face, face, column, column, message, message],
        [*slabs, near_ylo, near_yhi, near_zlo, near_zhi, *edges],
        [forward, own],
    )
    far = (shift(to_hi, "gx", 1), shift(to_lo, "gx", -1))
    own = own_grad(slabs, X // 2, 2, own, to_lo)
    keep, send = rim_grad(own, slabs[1], [ylo, yhi, held_ylo, held_yhi, *edges, *far])

    field = [*slabs, held_ylo, held_yhi, col_lo, col_hi]
    made = [None, None]
    weights = (forward, flipped)
    order = [(0, 0, 1), (0, 4, 4), (0, 20, 3), (1, 0, 4), (1, 16, 4)]
    state = {}

    def convolve(tie):
        part, first, groups = order.pop(0)
        following = order[0][:2] if order else None
        made[part], kept = conv_piece(
            part, first, groups, following, mask, field, far, weights[part], state, made[part], tie
        )
        state.update(kept)
        return [kept["carry"]]

    swap = [(i, i ^ 1) for i in range(8)]
    came = lax.ppermute(send, "gx", swap)
    ties = convolve(send)
    own, *parts = deal([keep, came], ties)
    came = exchange(0, parts)
    chunk, ties = own, convolve(parts[0])
    for turn in (1, 2):
        chunk = small_kernel(sum_kernel, shape(chunk.shape, F32), [chunk, *came], ties)
        came = exchange(turn, [chunk] * 3)
        ties = convolve(chunk)
    chunk = small_kernel(sum_kernel, shape(chunk.shape, F32), [chunk, *came], ties)
    came = exchange(0, [chunk] * 3)
    beside = lax.ppermute(chunk, "gx", swap)
    ties = convolve(chunk)
    joined = small_kernel(join_kernel, shape((3 * chunk.shape[0], C), F32), came, [beside, *ties])
    others = lax.ppermute(joined, "gx", swap)
    full = write([(chunk, (0,)), (joined, (1, 2, 3))], True, None, joined)
    full = write([(beside, (0,))], False, full, joined)
    full = write([(others, (1, 2, 3))], False, full, joined)
    return (made[0], made[1], full.reshape(3, 3, 3, C, C))


def solution(mesh):
    placed = (P("gx", "gy", "gz", None), P("gx", "gy", "gz"), P(), P("gx", "gy", "gz", None))
    return jax.shard_map(
        body,
        mesh=mesh,
        in_specs=placed,
        out_specs=(P("gx", "gy", "gz", None), P("gx", "gy", "gz", None), P()),
        check_vma=False,
    )
```

```python
import math

import jax
import jax.numpy as jnp
from jax import lax
from jax.experimental import pallas as pl
from jax.experimental.pallas import tpu as pltpu
from jax.sharding import PartitionSpec as P

SHARE = 8
X, Y, Z, C = 32, 16, 16, 128
E = 8
ROWS = Y * Z
GROUP = 4
SPAN = 8
TAPS = 9 * C
WIDE = 3 * C
HALF = 27 * C // 2
F32 = jnp.float32
BF16 = jnp.bfloat16
VMEM = pl.BlockSpec(memory_space=pltpu.VMEM)
SMEM = pl.BlockSpec(memory_space=pltpu.SMEM)
ANY = pl.BlockSpec(memory_space=pl.ANY)
DEPTH_FIRST = (((0,), (0,)), ((), ()))


def shape(dims, dtype):
    return jax.ShapeDtypeStruct(dims, dtype)


def params(mebibytes=24):
    return pltpu.CompilerParams(vmem_limit_bytes=mebibytes * 1024 * 1024)


def cost(slabs, moved):
    return pl.CostEstimate(flops=2 * 27 * C * C * slabs * ROWS, bytes_accessed=moved, transcendentals=0)


def inside(axis, side):
    at = lax.axis_index(axis)
    return at > 0 if side == 0 else at < lax.axis_size(axis) - 1


def held(value, axis, side):
    return jnp.where(inside(axis, side), value, jnp.zeros_like(value))


def brick_flags(occ_ref, brick):
    low_z = lax.broadcasted_iota(jnp.int32, (E, Z, C), 1) < E
    halves = [jnp.where(low_z, occ_ref[j, 0, brick], occ_ref[j, 1, brick]) for j in range(2)]
    return jnp.concatenate(halves, axis=0) == 1


def mask_slabs(part, source, mask_ref, s_ref, faces):
    zlo_ref, zhi_ref, ylo_ref, yhi_ref = faces
    for end in (0, X + 1):
        s_ref[end] = jnp.zeros((Y, Z, C), BF16)

    def one(brick, carry):
        span = pl.ds(brick * E, E)
        keep = mask_ref[brick].astype(F32) > 0.0
        value = jnp.where(keep[None], source[span].astype(F32), 0.0).astype(BF16)
        s_ref[pl.ds(brick * E + 1, E)] = value
        zlo_ref[part, span] = value[:, :, 0, :]
        zhi_ref[part, span] = value[:, :, Z - 1, :]
        ylo_ref[part, span] = value[:, 0]
        yhi_ref[part, span] = value[:, Y - 1]
        return carry

    lax.fori_loop(0, X // E, one, 0)


def first_kernel(o_ref):
    o_ref[...] = jnp.zeros_like(o_ref)


def mask_kernel(occ_ref, mask_ref):
    for brick in range(X // E):
        mask_ref[brick] = jnp.where(brick_flags(occ_ref, brick), 1.0, 0.0).astype(BF16)


def prepare_x_kernel(f_ref, mask_ref, s_ref, *faces):
    mask_slabs(0, f_ref, mask_ref, s_ref, faces)


def prepare_g_kernel(c_ref, mask_ref, *refs):
    given, s_ref, faces = refs[:4], refs[4], refs[5:]
    for face, ref in zip(faces, given, strict=True):
        face[0] = ref[0]
    mask_slabs(1, c_ref, mask_ref, s_ref, faces)


def prepare(occupancy, features, cotangent):
    slabs = shape((X + 2, Y, Z, C), BF16)
    own_cost = pl.CostEstimate(flops=1000, bytes_accessed=1000, transcendentals=0)
    lead = small_kernel(first_kernel, shape((8, C), F32), [], flops=10**10)
    mask = small_kernel(
        mask_kernel,
        shape((X // E, Y, Z, C), BF16),
        [jnp.transpose(occupancy, (1, 2, 0))],
        [lead],
        specs=[SMEM],
    )
    fields, *given = pl.pallas_call(
        prepare_x_kernel,
        in_specs=[VMEM] * 2,
        out_specs=[VMEM] * 5,
        out_shape=[slabs] + [shape((1, X, Z, C), BF16)] * 4,
        compiler_params=params(),
        cost_estimate=own_cost,
    )(features, mask)
    cotangents, *faces = pl.pallas_call(
        prepare_g_kernel,
        in_specs=[VMEM] * 6,
        out_specs=[VMEM] * 5,
        out_shape=[slabs] + [shape((2, X, Z, C), BF16)] * 4,
        compiler_params=params(),
        cost_estimate=own_cost,
    )(cotangent, mask, *given)
    return (fields, cotangents), mask, faces


def moved_z(whole, step):
    rows = whole.shape[0] * whole.shape[1]
    flat = whole.reshape(rows, C)
    return pltpu.roll(flat, -step % rows, 0).reshape(whole.shape)


def put_slab(scratch, slot, center, ylo, yhi, zlo, zhi):
    whole = jnp.concatenate([ylo[None], center, yhi[None]], axis=0)
    scratch[1, slot] = whole
    whole = whole.astype(F32)
    at = lax.broadcasted_iota(jnp.int32, (Y + 2, Z, C), 1)
    low = zlo.astype(F32)[: Y + 2, None, :]
    high = zhi.astype(F32)[: Y + 2, None, :]
    scratch[0, slot] = jnp.where(at == 0, low, moved_z(whole, -1)).astype(BF16)
    scratch[2, slot] = jnp.where(at == Z - 1, high, moved_z(whole, 1)).astype(BF16)


def put_own(scratch, slot, center):
    scratch[1, slot, 1 : Y + 1] = center
    whole = center.astype(F32)
    at = lax.broadcasted_iota(jnp.int32, (Y, Z, C), 1)
    scratch[0, slot, 1 : Y + 1] = jnp.where(at == 0, 0.0, moved_z(whole, -1)).astype(BF16)
    scratch[2, slot, 1 : Y + 1] = jnp.where(at == Z - 1, 0.0, moved_z(whole, 1)).astype(BF16)


def patches(shifted, slots):
    pieces = []
    for ty in range(3):
        for tz in range(3):
            pieces.append(shifted[tz, :slots, ty : ty + Y].reshape(slots * ROWS, C))
    return jnp.concatenate(pieces, axis=1)


def put_far(scratch, slot, far_ref, part, side):
    slab = held(far_ref[part], "gx", side)
    rims = slab[Y + 2 :].reshape(-1, C)
    put_slab(scratch, slot, slab[:Y], slab[Y], slab[Y + 1], rims[:24], rims[24:])


def own_grad_kernel(first, spans, more, x_ref, g_ref, *refs):
    total, even, odd = refs[-3:]
    for shifted in (even, odd):
        shifted[:, :, 0:1] = jnp.zeros((3, SPAN, 1, Z, C), BF16)
        shifted[:, :, Y + 1 :] = jnp.zeros((3, SPAN, 1, Z, C), BF16)

    def put(shifted, x):
        for slot in range(SPAN):
            put_own(shifted, slot, x_ref[x + 1 + slot])

    def product(shifted, x):
        columns = [g_ref[x + 2 - tx : x + 2 - tx + SPAN].reshape(SPAN * ROWS, C) for tx in range(3)]
        beside = jnp.concatenate(columns, axis=1)
        return lax.dot_general(beside, patches(shifted, SPAN), DEPTH_FIRST, preferred_element_type=F32)

    put(even, first)
    made = product(even, first)
    if spans == 2:
        put(odd, first + SPAN)
    total[...] = refs[0][...] + made if more else made
    if spans == 2:
        total[...] += product(odd, first + SPAN)


def own_grad(slabs, first, spans, before, tie):
    more = before is not None
    return pl.pallas_call(
        lambda *refs: own_grad_kernel(first, spans, more, *refs),
        in_specs=[VMEM] * (2 + more) + [ANY],
        out_specs=VMEM,
        out_shape=shape((WIDE, TAPS), F32),
        scratch_shapes=[pltpu.VMEM((3, SPAN, Y + 2, Z, C), BF16)] * 2,
        compiler_params=params(),
        cost_estimate=cost(spans * SPAN, 8 << 20),
    )(*slabs, *([before] if more else []), tie)


def add_rim(total, row, stride, trio, face_ref):
    blank = jnp.zeros((1, Z, C), BF16)
    padded = jnp.concatenate([blank, face_ref[1], blank], axis=0)
    around = jnp.concatenate([padded[2 - tx : 2 - tx + X].reshape(X * Z, C) for tx in range(3)], axis=1)
    left = jnp.concatenate([a.astype(BF16).reshape(X * Z, C) for a in trio], axis=1)
    made = lax.dot_general(around, left, DEPTH_FIRST, preferred_element_type=F32)
    for k in range(3):
        start = (row + k * stride) * C
        total[:, start : start + C] += made[:, k * C : (k + 1) * C]


def z_rim_kernel(own_ref, gzlo, gzhi, nzlo, nzhi, total):
    total[...] = own_ref[...]
    at = lax.broadcasted_iota(jnp.int32, (X, Z, C), 1)
    for side, row, near, face in ((0, 0, nzlo, gzlo), (1, 2, nzhi, gzhi)):
        whole = held(near[0].astype(F32), "gz", side)
        before = jnp.where(at == 0, 0.0, moved_z(whole, -1))
        after = jnp.where(at == Z - 1, 0.0, moved_z(whole, 1))
        add_rim(total, row, 3, (before, whole, after), face)


def rim_grad_kernel(
    own_ref, g_ref, gylo, gyhi, nylo, nyhi, elo, ehi, far_lo, far_hi, keep_ref, send_ref, scratch, total
):
    total[...] = own_ref[...]
    for side, far, plane, tx in ((0, far_lo, 1, 0), (1, far_hi, X, 2)):
        put_far(scratch.at[:, side : side + 1], 0, far, 0, side)
        left = patches(scratch.at[:, side : side + 1], 1)
        beside = g_ref[plane].reshape(ROWS, C)
        total[tx * C : (tx + 1) * C] += lax.dot_general(
            beside, left, DEPTH_FIRST, preferred_element_type=F32
        )
    at = lax.broadcasted_iota(jnp.int32, (X, Z, C), 1)
    for side, row, near, edges, face in ((0, 0, nylo, elo, gylo), (1, 6, nyhi, ehi, gyhi)):
        whole = near[0].astype(F32)
        corners = held(edges[0].astype(F32), "gy", side)
        low = corners[0][:, None, :]
        high = corners[1][:, None, :]
        before = jnp.where(at == 0, low, moved_z(whole, -1))
        after = jnp.where(at == Z - 1, high, moved_z(whole, 1))
        add_rim(total, row, 1, (before, whole, after), face)

    scale = 1.0 / math.sqrt(SHARE * 128 * E**3)
    core = lax.axis_index("gx") % 2
    for mine in range(2):

        @pl.when(core == mine)
        def _():
            for tap in range(27):
                tx, row = tap // 9, tap % 9
                block = total[tx * C : (tx + 1) * C, row * C : (row + 1) * C].T * scale
                for side, ref in ((mine, keep_ref), (1 - mine, send_ref)):
                    start = tap * C - side * HALF
                    low, high = max(start, 0), min(start + C, HALF)
                    if low < high:
                        ref[low:high] = block[low - start : high - start]


def rim_grad(own, cotangents, operands):
    return pl.pallas_call(
        rim_grad_kernel,
        in_specs=[VMEM] * (2 + len(operands)),
        out_specs=[VMEM, VMEM],
        out_shape=[shape((HALF, C), F32)] * 2,
        scratch_shapes=[pltpu.VMEM((3, 2, Y + 2, Z, C), BF16), pltpu.VMEM((WIDE, TAPS), F32)],
        compiler_params=params(),
        cost_estimate=cost(3, 6 << 20),
    )(own, cotangents, *operands)


def conv_kernel(part, first, groups, following, mask_ref, *refs):
    starts, ends = first == 0, first + groups * GROUP == X
    refs = list(refs)
    slabs = [refs.pop(0) for _ in range(2)]
    rims = [refs.pop(0) for _ in range(4)]
    w_ref = refs.pop(0)
    far_lo = refs.pop(0) if starts else None
    far_hi = refs.pop(0) if ends else None
    before = None if starts else refs.pop(0)
    late_in = None if starts else refs.pop(0)
    ready = None if starts and part == 0 else refs.pop(0)
    late = None if ends else refs.pop(-5)
    o_ref, carry_ref, even, others, edge, made_ref, left = refs[-7:]
    odd = others.at[0]
    count = groups * GROUP
    own_copies = groups if ends else groups - 1
    late_copy = None
    if not starts:
        skip = 1 if first == GROUP else 0
        target = o_ref.at[pl.ds(first - GROUP - 1 + skip, GROUP - skip)]
        late_copy = pltpu.make_async_copy(late_in.at[pl.ds(skip, GROUP - skip)], target, left.at[groups + 1])
        late_copy.start()

    def put(shifted, at, x):
        for slot in range(GROUP):
            put_slab(shifted, slot, slabs[at][x + 1 + slot], *(ref[at, x + slot] for ref in rims))

    def finish(x, total):
        keep = mask_ref[jnp.maximum(x, 0) // E].astype(F32) > 0.0
        made_ref[x - first + 1] = jnp.where(keep, total.reshape(Y, Z, C), 0.0).astype(BF16)

    def copy(x, size, sem):
        source = made_ref.at[pl.ds(x - first, size)]
        return pltpu.make_async_copy(source, o_ref.at[pl.ds(x - 1, size)], left.at[sem])

    def group(shifted, x, sem, near, next_, opens):
        made = jnp.dot(patches(shifted, GROUP), w_ref[...], preferred_element_type=F32)

        def term(slot, tx):
            return made[slot * ROWS : (slot + 1) * ROWS, tx * C : (tx + 1) * C]

        if opens is True:
            made_ref[0] = jnp.zeros((Y, Z, C), BF16)
        else:
            finish(x - 1, near + term(0, 2))
        finish(x, next_ + term(0, 1) + term(1, 2))
        for slot in range(1, GROUP - 1):
            finish(x + slot, term(slot - 1, 0) + term(slot, 1) + term(slot + 1, 2))
        if opens is None:
            pl.when(sem == 0)(lambda: copy(x + 1, GROUP - 1, sem).start())
            pl.when(sem > 0)(lambda: copy(x, GROUP, sem).start())
        elif opens:
            if own_copies > 0:
                copy(x + 1, GROUP - 1, sem).start()
        elif ends:
            copy(x, GROUP, sem).start()
        else:
            pl.when(sem < own_copies)(lambda: copy(x, GROUP, sem).start())
        return term(GROUP - 2, 0) + term(GROUP - 1, 1), term(GROUP - 1, 0)

    if starts:
        put_far(edge, 0, far_lo, part, 0)
        near = jnp.zeros((ROWS, C), F32)
        next_ = jnp.dot(patches(edge, 1), w_ref[:, :C], preferred_element_type=F32)
    else:
        near, next_ = before[0], before[1]
    if groups > 3 and following is not None:
        if ready is None:
            put(even, part, 0)
        else:
            even[...] = ready[...]
        carry_ref[0] = near
        carry_ref[1] = next_

        def trip(i, carry):
            x = first + i * 2 * GROUP
            near, next_ = group(even, x, 2 * i, carry_ref[0], carry_ref[1], None if starts else False)
            put(odd, part, x + GROUP)
            near, next_ = group(odd, x + GROUP, 2 * i + 1, near, next_, False)
            after = i + 1 == groups // 2
            put(even, part, jnp.where(after, following[1], x + 2 * GROUP))
            carry_ref[0] = near
            carry_ref[1] = next_
            return carry

        lax.fori_loop(0, groups // 2, trip, 0)
        near = carry_ref[0]
    else:
        if ready is None:
            put(odd, part, first)
        shifted = [odd] if ready is None else [ready, odd, others.at[1], even]
        for at in range(groups):
            x = first + at * GROUP
            near, next_ = group(shifted[at], x, at, near, next_, starts and at == 0)
            if at + 1 < groups:
                put(shifted[at + 1], part, x + GROUP)
        if following is not None:
            put(even, *following)
        carry_ref[0] = near
        carry_ref[1] = next_
    if ends:
        put_far(edge, 0, far_hi, part, 1)
        last = jnp.dot(patches(edge, 1), w_ref[:, 2 * C :], preferred_element_type=F32)
        finish(X - 1, near + last)
        copy(X, 1, groups).start()
    if late is not None:
        late[...] = made_ref[count - GROUP : count]
    for sem in range(own_copies):
        x = first + sem * GROUP
        if starts and sem == 0:
            copy(x + 1, GROUP - 1, sem).wait()
        else:
            copy(x, GROUP, sem).wait()
    if ends:
        copy(X, 1, groups).wait()
    if late_copy is not None:
        late_copy.wait()


def conv_piece(part, first, groups, following, mask, field, far, weight, state, done, tie):
    operands = [mask, *field, weight]
    starts, ends = first == 0, first + groups * GROUP == X
    if starts:
        operands.append(far[0])
    if ends:
        operands.append(far[1])
    if not starts:
        operands += [state["carry"], state["late"]]
    if "ready" in state:
        operands.append(state["ready"])
    aliases = {}
    specs = [VMEM] * len(operands)
    operands.append(tie)
    specs.append(ANY)
    if not starts:
        aliases = {len(operands): 0}
        operands.append(done)
        specs.append(ANY)
    shifted = (3, GROUP, Y + 2, Z, C)
    more = following is not None
    buffers = [shape((2, ROWS, C), F32), shape(shifted, BF16)]
    kept = buffers + ([] if ends else [shape((GROUP, Y, Z, C), BF16)])
    scratch = [
        pltpu.VMEM((2, *shifted), BF16),
        pltpu.VMEM((3, 1, Y + 2, Z, C), BF16),
        pltpu.VMEM((groups * GROUP + 1, Y, Z, C), BF16),
        pltpu.SemaphoreType.DMA((groups + 2,)),
    ]
    if not more:
        scratch = [pltpu.VMEM(b.shape, b.dtype) for b in buffers] + scratch
        kept = [shape((8, C), F32)]

    def plain(*refs):
        conv_kernel(part, first, groups, following, *refs)

    def final(*refs):
        refs[-7][...] = jnp.zeros((8, C), F32)
        conv_kernel(part, first, groups, following, *refs[:-7], *refs[-6:])

    made, *kept = pl.pallas_call(
        plain if more else final,
        in_specs=specs,
        out_specs=[ANY] + [VMEM] * len(kept),
        out_shape=[shape((X, Y, Z, C), BF16)] + kept,
        scratch_shapes=scratch,
        input_output_aliases=aliases,
        compiler_params=params(),
        cost_estimate=cost(groups * GROUP, 2 << 20),
    )(*operands)
    return made, dict(zip(("carry", "ready", "late"), kept, strict=False))


def small_kernel(kernel, out_shape, operands, ties=(), specs=None, flops=1000):
    count = len(operands)

    def run(*refs):
        kernel(*refs[:count], *refs[count + len(ties) :])

    return pl.pallas_call(
        run,
        in_specs=(specs or [VMEM] * count) + [ANY] * len(ties),
        out_specs=jax.tree.map(lambda _: VMEM, out_shape),
        out_shape=out_shape,
        compiler_params=params(),
        cost_estimate=pl.CostEstimate(flops=flops, bytes_accessed=1 << 20, transcendentals=0),
    )(*operands, *ties)


def copy_kernel(a, b, c, d):
    c[...] = a[...]
    d[...] = b[...]


def edge_kernel(zlo, zhi, lo, hi):
    for side, ref in enumerate((zlo, zhi)):
        lo[:, side] = held(ref[:, :, 0, :], "gz", side)
        hi[:, side] = held(ref[:, :, Y - 1, :], "gz", side)


def message_kernel(x_ref, g_ref, ylo, yhi, zlo, zhi, elo, ehi, held_ylo, held_yhi, col_lo, col_hi, to_lo, to_hi):
    held_ylo[...] = held(ylo[...], "gy", 0)
    held_yhi[...] = held(yhi[...], "gy", 1)
    tail = jnp.zeros((2, X, 24 - Y - 2, C), F32)
    for side, (near, col) in enumerate(((zlo, col_lo), (zhi, col_hi))):
        own = held(near[...].astype(F32), "gz", side)
        low = held(elo[:, side].astype(F32), "gy", 0)[:, :, None, :]
        high = held(ehi[:, side].astype(F32), "gy", 1)[:, :, None, :]
        col[...] = jnp.concatenate([low, own, high, tail], axis=2).astype(BF16)
    for at, to in ((0, to_lo), (X - 1, to_hi)):
        to[0, :Y] = x_ref[at + 1]
        to[1, :Y] = g_ref[at + 1]
        to[:, Y] = held_ylo[:, at]
        to[:, Y + 1] = held_yhi[:, at]
        rims = jnp.concatenate([col_lo[:, at], col_hi[:, at]], axis=1)
        to[:, Y + 2 :] = rims.reshape(2, 3, Z, C)


def arrange_kernel(w_ref, forward, flipped):
    for tap in range(27):
        tx, row = tap // 9, tap % 9
        forward[row * C : (row + 1) * C, tx * C : (tx + 1) * C] = w_ref[tap]
        flipped[row * C : (row + 1) * C, tx * C : (tx + 1) * C] = w_ref[26 - tap].astype(F32).T.astype(BF16)


ORDER = ("zyx", "yxz")


def first_place(core):
    return lax.axis_index("gx") // 2 * (1 - core) + lax.axis_index("gy") * core


def pairs(turn, step):
    found = []
    for z in range(4):
        for core in range(2):
            for y in range(4):
                for x in range(4):
                    at = {"z": z, "y": y, "x": x}
                    to = dict(at)
                    to[ORDER[core][turn]] ^= step
                    found.append(tuple(((2 * p["z"] + core) * 4 + p["y"]) * 4 + p["x"] for p in (at, to)))
    return found


def exchange(turn, values):
    one, two, three = (
        lax.ppermute(value, ("gx", "gy", "gz"), pairs(turn, step))
        for step, value in zip((1, 2, 3), values, strict=True)
    )
    return [one, three, two]


def deal(terms, ties):
    rows = terms[0].shape[0] // 4

    def kernel(*refs):
        me = first_place(lax.axis_index("gx") % 2)
        for step in range(4):
            at = pl.ds((me ^ step) * rows, rows)
            total = refs[0][at]
            for ref in refs[1 : len(terms)]:
                total = total + ref[at]
            refs[len(terms) + step][...] = total

    return small_kernel(kernel, [shape((rows, C), F32)] * 4, terms, ties)


def scatter_sum_kernel(own, one, two, three, o):
    o[...] = (own[...] + two[...]) + (one[...] + three[...])


def sum_kernel(own, one, three, two, o):
    o[...] = (own[...] + two[...]) + (one[...] + three[...])


def write(sources, mine, target, tie):
    arrays = [a for a, _ in sources]
    rows = HALF // 4
    count = sum(len(steps) for _, steps in sources)

    def kernel(*refs):
        o_ref, left = refs[-2:]
        at = lax.axis_index("gx")
        half = at % 2 if mine else 1 - at % 2
        me = first_place(half)
        for act in ("start", "wait"):
            sem = 0
            for ref, (_, steps) in zip(refs, sources, strict=False):
                for at, step in enumerate(steps):
                    chunk = half * 4 + (me ^ step)

                    place = o_ref.at[pl.ds(chunk * rows, rows)]
                    copy = pltpu.make_async_copy(ref.at[pl.ds(at * rows, rows)], place, left.at[sem])
                    if act == "start":
                        copy.start()
                    else:
                        copy.wait()
                    sem += 1

    operands = arrays + [tie] + ([] if target is None else [target])
    return pl.pallas_call(
        kernel,
        in_specs=[VMEM] * len(arrays) + [ANY] * (len(operands) - len(arrays)),
        out_specs=ANY,
        out_shape=shape((27 * C, C), F32),
        scratch_shapes=[pltpu.SemaphoreType.DMA((count,))],
        input_output_aliases={} if target is None else {len(operands) - 1: 0},
        compiler_params=params(),
        cost_estimate=pl.CostEstimate(flops=1000, bytes_accessed=1 << 20, transcendentals=0),
    )(*operands)


def join_kernel(a, b, c, o):
    rows = a.shape[0]
    for k, ref in enumerate((a, b, c)):
        o[k * rows : (k + 1) * rows] = ref[...]


def shift(value, axis, step):
    count = lax.axis_size(axis)
    return lax.ppermute(value, axis, [(i, (i + step) % count) for i in range(count)])


def body(features, occupancy, weight, cotangent):
    slabs, mask, faces = prepare(occupancy, features, cotangent)
    zlo, zhi, ylo, yhi = faces
    near_zlo = shift(zhi, "gz", 1)
    near_zhi = shift(zlo, "gz", -1)
    own = own_grad(slabs, 0, 1, None, zlo)
    face = shape((2, X, Z, C), BF16)
    to_ylo, to_yhi = small_kernel(copy_kernel, [face, face], [ylo, yhi], [own])
    near_ylo = shift(to_yhi, "gy", 1)
    near_yhi = shift(to_ylo, "gy", -1)
    own = own_grad(slabs, SPAN, 1, own, to_ylo)

    edge = shape((2, 2, X, C), BF16)
    edge_lo, edge_hi = small_kernel(edge_kernel, [edge, edge], [near_zlo, near_zhi], [own])
    edges = (shift(edge_hi, "gy", 1), shift(edge_lo, "gy", -1))
    forward, flipped = small_kernel(
        arrange_kernel, [shape((TAPS, WIDE), BF16)] * 2, [weight.reshape(27, C, C)], [edge_lo]
    )
    own = small_kernel(
        z_rim_kernel, shape((WIDE, TAPS), F32), [own, zlo, zhi, near_zlo, near_zhi], [edge_lo]
    )

    column = shape((2, X, 24, C), BF16)
    message = shape((2, Y + 5, Z, C), BF16)
    held_ylo, held_yhi, col_lo, col_hi, to_lo, to_hi = small_kernel(
        message_kernel,
        [face, face, column, column, message, message],
        [*slabs, near_ylo, near_yhi, near_zlo, near_zhi, *edges],
        [forward, own],
    )
    far = (shift(to_hi, "gx", 1), shift(to_lo, "gx", -1))
    own = own_grad(slabs, X // 2, 2, own, to_lo)
    keep, send = rim_grad(own, slabs[1], [ylo, yhi, held_ylo, held_yhi, *edges, *far])

    field = [*slabs, held_ylo, held_yhi, col_lo, col_hi]
    made = [None, None]
    weights = (forward, flipped)
    order = [(0, 0, 1), (0, 4, 4), (0, 20, 3), (1, 0, 4), (1, 16, 4)]
    state = {}

    def convolve(tie):
        part, first, groups = order.pop(0)
        following = order[0][:2] if order else None
        made[part], kept = conv_piece(
            part, first, groups, following, mask, field, far, weights[part], state, made[part], tie
        )
        state.update(kept)
        return [kept["carry"]]

    swap = [(i, i ^ 1) for i in range(8)]
    came = lax.ppermute(send, "gx", swap)
    ties = convolve(send)
    own, *parts = deal([keep, came], ties)
    one, three, two = exchange(0, parts)
    ties = convolve(parts[0])
    chunk = small_kernel(scatter_sum_kernel, shape(own.shape, F32), [own, one, two, three], ties)
    for turn in (1, 2):
        if turn == 2:
            chunk = small_kernel(sum_kernel, shape(chunk.shape, F32), [chunk, *came], ties)
        came = exchange(turn, [chunk] * 3)
        ties = convolve(chunk)
    chunk = small_kernel(sum_kernel, shape(chunk.shape, F32), [chunk, *came], ties)
    came = exchange(0, [chunk] * 3)
    beside = lax.ppermute(chunk, "gx", swap)
    ties = convolve(chunk)
    joined = small_kernel(join_kernel, shape((3 * chunk.shape[0], C), F32), came, [beside, *ties])
    others = lax.ppermute(joined, "gx", swap)
    full = write([(chunk, (0,)), (joined, (1, 3, 2))], True, None, joined)
    full = write([(beside, (0,))], False, full, joined)
    full = write([(others, (1, 3, 2))], False, full, joined)
    return (made[0], made[1], full.reshape(3, 3, 3, C, C))


def solution(mesh):
    placed = (P("gx", "gy", "gz", None), P("gx", "gy", "gz"), P(), P("gx", "gy", "gz", None))
    return jax.shard_map(
        body,
        mesh=mesh,
        in_specs=placed,
        out_specs=(P("gx", "gy", "gz", None), P("gx", "gy", "gz", None), P()),
        check_vma=False,
    )
```

```python
import math

import jax
import jax.numpy as jnp
from jax import lax
from jax.experimental import pallas as pl
from jax.experimental.pallas import tpu as pltpu
from jax.sharding import PartitionSpec as P

SHARE = 8
X, Y, Z, C = 32, 16, 16, 128
E = 8
ROWS = Y * Z
GROUP = 4
SPAN = 8
TAPS = 9 * C
WIDE = 3 * C
HALF = 27 * C // 2
F32 = jnp.float32
BF16 = jnp.bfloat16
VMEM = pl.BlockSpec(memory_space=pltpu.VMEM)
SMEM = pl.BlockSpec(memory_space=pltpu.SMEM)
ANY = pl.BlockSpec(memory_space=pl.ANY)
DEPTH_FIRST = (((0,), (0,)), ((), ()))


def shape(dims, dtype):
    return jax.ShapeDtypeStruct(dims, dtype)


def params(mebibytes=24):
    return pltpu.CompilerParams(vmem_limit_bytes=mebibytes * 1024 * 1024)


def cost(slabs, moved):
    return pl.CostEstimate(flops=2 * 27 * C * C * slabs * ROWS, bytes_accessed=moved, transcendentals=0)


def inside(axis, side):
    at = lax.axis_index(axis)
    return at > 0 if side == 0 else at < lax.axis_size(axis) - 1


def held(value, axis, side):
    return jnp.where(inside(axis, side), value, jnp.zeros_like(value))


def brick_flags(occ_ref, brick):
    low_z = lax.broadcasted_iota(jnp.int32, (E, Z, C), 1) < E
    halves = [jnp.where(low_z, occ_ref[j, 0, brick], occ_ref[j, 1, brick]) for j in range(2)]
    return jnp.concatenate(halves, axis=0) == 1


def mask_slabs(part, source, mask_ref, s_ref, faces):
    zlo_ref, zhi_ref, ylo_ref, yhi_ref = faces
    for end in (0, X + 1):
        s_ref[end] = jnp.zeros((Y, Z, C), BF16)

    def one(brick, carry):
        span = pl.ds(brick * E, E)
        keep = mask_ref[brick].astype(F32) > 0.0
        value = jnp.where(keep[None], source[span].astype(F32), 0.0).astype(BF16)
        s_ref[pl.ds(brick * E + 1, E)] = value
        zlo_ref[part, span] = value[:, :, 0, :]
        zhi_ref[part, span] = value[:, :, Z - 1, :]
        ylo_ref[part, span] = value[:, 0]
        yhi_ref[part, span] = value[:, Y - 1]
        return carry

    lax.fori_loop(0, X // E, one, 0)


def first_kernel(o_ref):
    o_ref[...] = jnp.zeros_like(o_ref)


def mask_kernel(occ_ref, mask_ref):
    for brick in range(X // E):
        mask_ref[brick] = jnp.where(brick_flags(occ_ref, brick), 1.0, 0.0).astype(BF16)


def prepare_x_kernel(f_ref, mask_ref, s_ref, *faces):
    mask_slabs(0, f_ref, mask_ref, s_ref, faces)


def prepare_g_kernel(c_ref, mask_ref, *refs):
    given, s_ref, faces = refs[:4], refs[4], refs[5:]
    for face, ref in zip(faces, given, strict=True):
        face[0] = ref[0]
    mask_slabs(1, c_ref, mask_ref, s_ref, faces)


def prepare(occupancy, features, cotangent):
    slabs = shape((X + 2, Y, Z, C), BF16)
    own_cost = pl.CostEstimate(flops=1000, bytes_accessed=1000, transcendentals=0)
    lead = small_kernel(first_kernel, shape((8, C), F32), [], flops=10**10)
    mask = small_kernel(
        mask_kernel,
        shape((X // E, Y, Z, C), BF16),
        [jnp.transpose(occupancy, (1, 2, 0))],
        [lead],
        specs=[SMEM],
    )
    fields, *given = pl.pallas_call(
        prepare_x_kernel,
        in_specs=[VMEM] * 2,
        out_specs=[VMEM] * 5,
        out_shape=[slabs] + [shape((1, X, Z, C), BF16)] * 4,
        compiler_params=params(),
        cost_estimate=own_cost,
    )(features, mask)
    cotangents, *faces = pl.pallas_call(
        prepare_g_kernel,
        in_specs=[VMEM] * 6,
        out_specs=[VMEM] * 5,
        out_shape=[slabs] + [shape((2, X, Z, C), BF16)] * 4,
        compiler_params=params(),
        cost_estimate=own_cost,
    )(cotangent, mask, *given)
    return (fields, cotangents), mask, faces


def moved_z(whole, step):
    rows = whole.shape[0] * whole.shape[1]
    flat = whole.reshape(rows, C)
    return pltpu.roll(flat, -step % rows, 0).reshape(whole.shape)


def put_slab(scratch, slot, center, ylo, yhi, zlo, zhi):
    whole = jnp.concatenate([ylo[None], center, yhi[None]], axis=0)
    scratch[1, slot] = whole
    whole = whole.astype(F32)
    at = lax.broadcasted_iota(jnp.int32, (Y + 2, Z, C), 1)
    low = zlo.astype(F32)[: Y + 2, None, :]
    high = zhi.astype(F32)[: Y + 2, None, :]
    scratch[0, slot] = jnp.where(at == 0, low, moved_z(whole, -1)).astype(BF16)
    scratch[2, slot] = jnp.where(at == Z - 1, high, moved_z(whole, 1)).astype(BF16)


def put_own(scratch, slot, center):
    scratch[1, slot, 1 : Y + 1] = center
    whole = center.astype(F32)
    at = lax.broadcasted_iota(jnp.int32, (Y, Z, C), 1)
    scratch[0, slot, 1 : Y + 1] = jnp.where(at == 0, 0.0, moved_z(whole, -1)).astype(BF16)
    scratch[2, slot, 1 : Y + 1] = jnp.where(at == Z - 1, 0.0, moved_z(whole, 1)).astype(BF16)


def patches(shifted, slots):
    pieces = []
    for ty in range(3):
        for tz in range(3):
            pieces.append(shifted[tz, :slots, ty : ty + Y].reshape(slots * ROWS, C))
    return jnp.concatenate(pieces, axis=1)


def put_far(scratch, slot, far_ref, part, side):
    slab = held(far_ref[part], "gx", side)
    rims = slab[Y + 2 :].reshape(-1, C)
    put_slab(scratch, slot, slab[:Y], slab[Y], slab[Y + 1], rims[:24], rims[24:])


def own_grad_kernel(first, spans, more, x_ref, g_ref, *refs):
    total, even, odd = refs[-3:]
    for shifted in (even, odd):
        shifted[:, :, 0:1] = jnp.zeros((3, SPAN, 1, Z, C), BF16)
        shifted[:, :, Y + 1 :] = jnp.zeros((3, SPAN, 1, Z, C), BF16)

    def put(shifted, x):
        for slot in range(SPAN):
            put_own(shifted, slot, x_ref[x + 1 + slot])

    def product(shifted, x):
        columns = [g_ref[x + 2 - tx : x + 2 - tx + SPAN].reshape(SPAN * ROWS, C) for tx in range(3)]
        beside = jnp.concatenate(columns, axis=1)
        return lax.dot_general(beside, patches(shifted, SPAN), DEPTH_FIRST, preferred_element_type=F32)

    put(even, first)
    made = product(even, first)
    if spans == 2:
        put(odd, first + SPAN)
    total[...] = refs[0][...] + made if more else made
    if spans == 2:
        total[...] += product(odd, first + SPAN)


def own_grad(slabs, first, spans, before, tie):
    more = before is not None
    return pl.pallas_call(
        lambda *refs: own_grad_kernel(first, spans, more, *refs),
        in_specs=[VMEM] * (2 + more) + [ANY],
        out_specs=VMEM,
        out_shape=shape((WIDE, TAPS), F32),
        scratch_shapes=[pltpu.VMEM((3, SPAN, Y + 2, Z, C), BF16)] * 2,
        compiler_params=params(),
        cost_estimate=cost(spans * SPAN, 8 << 20),
    )(*slabs, *([before] if more else []), tie)


def add_rim(total, row, stride, trio, face_ref):
    blank = jnp.zeros((1, Z, C), BF16)
    padded = jnp.concatenate([blank, face_ref[1], blank], axis=0)
    around = jnp.concatenate([padded[2 - tx : 2 - tx + X].reshape(X * Z, C) for tx in range(3)], axis=1)
    left = jnp.concatenate([a.astype(BF16).reshape(X * Z, C) for a in trio], axis=1)
    made = lax.dot_general(around, left, DEPTH_FIRST, preferred_element_type=F32)
    for k in range(3):
        start = (row + k * stride) * C
        total[:, start : start + C] += made[:, k * C : (k + 1) * C]


def z_rim_kernel(own_ref, gzlo, gzhi, nzlo, nzhi, total):
    total[...] = own_ref[...]
    at = lax.broadcasted_iota(jnp.int32, (X, Z, C), 1)
    for side, row, near, face in ((0, 0, nzlo, gzlo), (1, 2, nzhi, gzhi)):
        whole = held(near[0].astype(F32), "gz", side)
        before = jnp.where(at == 0, 0.0, moved_z(whole, -1))
        after = jnp.where(at == Z - 1, 0.0, moved_z(whole, 1))
        add_rim(total, row, 3, (before, whole, after), face)


def rim_grad_kernel(
    own_ref, g_ref, gylo, gyhi, nylo, nyhi, elo, ehi, far_lo, far_hi, keep_ref, send_ref, scratch, total
):
    total[...] = own_ref[...]
    for side, far, plane, tx in ((0, far_lo, 1, 0), (1, far_hi, X, 2)):
        put_far(scratch.at[:, side : side + 1], 0, far, 0, side)
        left = patches(scratch.at[:, side : side + 1], 1)
        beside = g_ref[plane].reshape(ROWS, C)
        total[tx * C : (tx + 1) * C] += lax.dot_general(
            beside, left, DEPTH_FIRST, preferred_element_type=F32
        )
    at = lax.broadcasted_iota(jnp.int32, (X, Z, C), 1)
    for side, row, near, edges, face in ((0, 0, nylo, elo, gylo), (1, 6, nyhi, ehi, gyhi)):
        whole = near[0].astype(F32)
        corners = held(edges[0].astype(F32), "gy", side)
        low = corners[0][:, None, :]
        high = corners[1][:, None, :]
        before = jnp.where(at == 0, low, moved_z(whole, -1))
        after = jnp.where(at == Z - 1, high, moved_z(whole, 1))
        add_rim(total, row, 1, (before, whole, after), face)

    scale = 1.0 / math.sqrt(SHARE * 128 * E**3)
    core = lax.axis_index("gx") % 2
    for mine in range(2):

        @pl.when(core == mine)
        def _():
            for tap in range(27):
                tx, row = tap // 9, tap % 9
                block = total[tx * C : (tx + 1) * C, row * C : (row + 1) * C].T * scale
                for side, ref in ((mine, keep_ref), (1 - mine, send_ref)):
                    start = tap * C - side * HALF
                    low, high = max(start, 0), min(start + C, HALF)
                    if low < high:
                        ref[low:high] = block[low - start : high - start]


def rim_grad(own, cotangents, operands):
    return pl.pallas_call(
        rim_grad_kernel,
        in_specs=[VMEM] * (2 + len(operands)),
        out_specs=[VMEM, VMEM],
        out_shape=[shape((HALF, C), F32)] * 2,
        scratch_shapes=[pltpu.VMEM((3, 2, Y + 2, Z, C), BF16), pltpu.VMEM((WIDE, TAPS), F32)],
        compiler_params=params(),
        cost_estimate=cost(3, 6 << 20),
    )(own, cotangents, *operands)


def conv_kernel(part, first, groups, following, mask_ref, *refs):
    starts, ends = first == 0, first + groups * GROUP == X
    refs = list(refs)
    slabs = [refs.pop(0) for _ in range(2)]
    rims = [refs.pop(0) for _ in range(4)]
    w_ref = refs.pop(0)
    far_lo = refs.pop(0) if starts else None
    far_hi = refs.pop(0) if ends else None
    before = None if starts else refs.pop(0)
    late_in = None if starts else refs.pop(0)
    ready = None if starts and part == 0 else refs.pop(0)
    late = None if ends else refs.pop(-5)
    o_ref, carry_ref, even, others, edge, made_ref, left = refs[-7:]
    odd = others.at[0]
    count = groups * GROUP
    own_copies = groups if ends else groups - 1
    late_copy = None
    if not starts:
        skip = 1 if first == GROUP else 0
        target = o_ref.at[pl.ds(first - GROUP - 1 + skip, GROUP - skip)]
        late_copy = pltpu.make_async_copy(late_in.at[pl.ds(skip, GROUP - skip)], target, left.at[groups + 1])
        late_copy.start()

    def put(shifted, at, x):
        for slot in range(GROUP):
            put_slab(shifted, slot, slabs[at][x + 1 + slot], *(ref[at, x + slot] for ref in rims))

    def finish(x, total):
        keep = mask_ref[jnp.maximum(x, 0) // E].astype(F32) > 0.0
        made_ref[x - first + 1] = jnp.where(keep, total.reshape(Y, Z, C), 0.0).astype(BF16)

    def copy(x, size, sem):
        source = made_ref.at[pl.ds(x - first, size)]
        return pltpu.make_async_copy(source, o_ref.at[pl.ds(x - 1, size)], left.at[sem])

    def group(shifted, x, sem, near, next_, opens):
        made = jnp.dot(patches(shifted, GROUP), w_ref[...], preferred_element_type=F32)

        def term(slot, tx):
            return made[slot * ROWS : (slot + 1) * ROWS, tx * C : (tx + 1) * C]

        if opens is True:
            made_ref[0] = jnp.zeros((Y, Z, C), BF16)
        else:
            finish(x - 1, near + term(0, 2))
        finish(x, next_ + term(0, 1) + term(1, 2))
        for slot in range(1, GROUP - 1):
            finish(x + slot, term(slot - 1, 0) + term(slot, 1) + term(slot + 1, 2))
        if opens is None:
            pl.when(sem == 0)(lambda: copy(x + 1, GROUP - 1, sem).start())
            pl.when(sem > 0)(lambda: copy(x, GROUP, sem).start())
        elif opens:
            if own_copies > 0:
                copy(x + 1, GROUP - 1, sem).start()
        elif ends:
            copy(x, GROUP, sem).start()
        else:
            pl.when(sem < own_copies)(lambda: copy(x, GROUP, sem).start())
        return term(GROUP - 2, 0) + term(GROUP - 1, 1), term(GROUP - 1, 0)

    if starts:
        put_far(edge, 0, far_lo, part, 0)
        near = jnp.zeros((ROWS, C), F32)
        next_ = jnp.dot(patches(edge, 1), w_ref[:, :C], preferred_element_type=F32)
    else:
        near, next_ = before[0], before[1]
    if groups > 3 and following is not None:
        if ready is None:
            put(even, part, 0)
        else:
            even[...] = ready[...]
        carry_ref[0] = near
        carry_ref[1] = next_

        def trip(i, carry):
            x = first + i * 2 * GROUP
            near, next_ = group(even, x, 2 * i, carry_ref[0], carry_ref[1], None if starts else False)
            put(odd, part, x + GROUP)
            near, next_ = group(odd, x + GROUP, 2 * i + 1, near, next_, False)
            after = i + 1 == groups // 2
            put(even, part, jnp.where(after, following[1], x + 2 * GROUP))
            carry_ref[0] = near
            carry_ref[1] = next_
            return carry

        lax.fori_loop(0, groups // 2, trip, 0)
        near = carry_ref[0]
    else:
        if ready is None:
            put(odd, part, first)
        shifted = [odd] if ready is None else [ready, odd, others.at[1], even]
        for at in range(groups):
            x = first + at * GROUP
            near, next_ = group(shifted[at], x, at, near, next_, starts and at == 0)
            if at + 1 < groups:
                put(shifted[at + 1], part, x + GROUP)
        if following is not None:
            put(even, *following)
        carry_ref[0] = near
        carry_ref[1] = next_
    if ends:
        put_far(edge, 0, far_hi, part, 1)
        last = jnp.dot(patches(edge, 1), w_ref[:, 2 * C :], preferred_element_type=F32)
        finish(X - 1, near + last)
        copy(X, 1, groups).start()
    if late is not None:
        late[...] = made_ref[count - GROUP : count]
    for sem in range(own_copies):
        x = first + sem * GROUP
        if starts and sem == 0:
            copy(x + 1, GROUP - 1, sem).wait()
        else:
            copy(x, GROUP, sem).wait()
    if ends:
        copy(X, 1, groups).wait()
    if late_copy is not None:
        late_copy.wait()


def conv_piece(part, first, groups, following, mask, field, far, weight, state, done, tie):
    operands = [mask, *field, weight]
    starts, ends = first == 0, first + groups * GROUP == X
    if starts:
        operands.append(far[0])
    if ends:
        operands.append(far[1])
    if not starts:
        operands += [state["carry"], state["late"]]
    if "ready" in state:
        operands.append(state["ready"])
    aliases = {}
    specs = [VMEM] * len(operands)
    operands.append(tie)
    specs.append(ANY)
    if not starts:
        aliases = {len(operands): 0}
        operands.append(done)
        specs.append(ANY)
    shifted = (3, GROUP, Y + 2, Z, C)
    more = following is not None
    buffers = [shape((2, ROWS, C), F32), shape(shifted, BF16)]
    kept = buffers + ([] if ends else [shape((GROUP, Y, Z, C), BF16)])
    scratch = [
        pltpu.VMEM((2, *shifted), BF16),
        pltpu.VMEM((3, 1, Y + 2, Z, C), BF16),
        pltpu.VMEM((groups * GROUP + 1, Y, Z, C), BF16),
        pltpu.SemaphoreType.DMA((groups + 2,)),
    ]
    if not more:
        scratch = [pltpu.VMEM(b.shape, b.dtype) for b in buffers] + scratch
        kept = [shape((8, C), F32)]

    def plain(*refs):
        conv_kernel(part, first, groups, following, *refs)

    def final(*refs):
        refs[-7][...] = jnp.zeros((8, C), F32)
        conv_kernel(part, first, groups, following, *refs[:-7], *refs[-6:])

    made, *kept = pl.pallas_call(
        plain if more else final,
        in_specs=specs,
        out_specs=[ANY] + [VMEM] * len(kept),
        out_shape=[shape((X, Y, Z, C), BF16)] + kept,
        scratch_shapes=scratch,
        input_output_aliases=aliases,
        compiler_params=params(),
        cost_estimate=cost(groups * GROUP, 2 << 20),
    )(*operands)
    return made, dict(zip(("carry", "ready", "late"), kept, strict=False))


def small_kernel(kernel, out_shape, operands, ties=(), specs=None, flops=1000):
    count = len(operands)

    def run(*refs):
        kernel(*refs[:count], *refs[count + len(ties) :])

    return pl.pallas_call(
        run,
        in_specs=(specs or [VMEM] * count) + [ANY] * len(ties),
        out_specs=jax.tree.map(lambda _: VMEM, out_shape),
        out_shape=out_shape,
        compiler_params=params(),
        cost_estimate=pl.CostEstimate(flops=flops, bytes_accessed=1 << 20, transcendentals=0),
    )(*operands, *ties)


def copy_kernel(a, b, c, d):
    c[...] = a[...]
    d[...] = b[...]


def edge_kernel(zlo, zhi, lo, hi):
    for side, ref in enumerate((zlo, zhi)):
        lo[:, side] = held(ref[:, :, 0, :], "gz", side)
        hi[:, side] = held(ref[:, :, Y - 1, :], "gz", side)


def message_kernel(x_ref, g_ref, ylo, yhi, zlo, zhi, elo, ehi, held_ylo, held_yhi, col_lo, col_hi, to_lo, to_hi):
    held_ylo[...] = held(ylo[...], "gy", 0)
    held_yhi[...] = held(yhi[...], "gy", 1)
    tail = jnp.zeros((2, X, 24 - Y - 2, C), F32)
    for side, (near, col) in enumerate(((zlo, col_lo), (zhi, col_hi))):
        own = held(near[...].astype(F32), "gz", side)
        low = held(elo[:, side].astype(F32), "gy", 0)[:, :, None, :]
        high = held(ehi[:, side].astype(F32), "gy", 1)[:, :, None, :]
        col[...] = jnp.concatenate([low, own, high, tail], axis=2).astype(BF16)
    for at, to in ((0, to_lo), (X - 1, to_hi)):
        to[0, :Y] = x_ref[at + 1]
        to[1, :Y] = g_ref[at + 1]
        to[:, Y] = held_ylo[:, at]
        to[:, Y + 1] = held_yhi[:, at]
        rims = jnp.concatenate([col_lo[:, at], col_hi[:, at]], axis=1)
        to[:, Y + 2 :] = rims.reshape(2, 3, Z, C)


def arrange_kernel(w_ref, forward, flipped):
    for tap in range(27):
        tx, row = tap // 9, tap % 9
        forward[row * C : (row + 1) * C, tx * C : (tx + 1) * C] = w_ref[tap]
        flipped[row * C : (row + 1) * C, tx * C : (tx + 1) * C] = w_ref[26 - tap].astype(F32).T.astype(BF16)


ORDER = ("zyx", "yxz")


def first_place(core):
    return lax.axis_index("gx") // 2 * (1 - core) + lax.axis_index("gy") * core


def pairs(turn, step):
    found = []
    for z in range(4):
        for core in range(2):
            for y in range(4):
                for x in range(4):
                    at = {"z": z, "y": y, "x": x}
                    to = dict(at)
                    to[ORDER[core][turn]] ^= step
                    found.append(tuple(((2 * p["z"] + core) * 4 + p["y"]) * 4 + p["x"] for p in (at, to)))
    return found


def exchange(turn, values):
    one, two, three = (
        lax.ppermute(value, ("gx", "gy", "gz"), pairs(turn, step))
        for step, value in zip((1, 2, 3), values, strict=True)
    )
    return [one, three, two]


def deal(terms, ties):
    rows = terms[0].shape[0] // 4

    def kernel(*refs):
        me = first_place(lax.axis_index("gx") % 2)
        for step in range(4):
            at = pl.ds((me ^ step) * rows, rows)
            total = refs[0][at]
            for ref in refs[1 : len(terms)]:
                total = total + ref[at]
            refs[len(terms) + step][...] = total

    return small_kernel(kernel, [shape((rows, C), F32)] * 4, terms, ties)


def scatter_sum_kernel(own, one, two, three, o):
    o[...] = (own[...] + two[...]) + (one[...] + three[...])


def sum_kernel(own, one, three, two, o):
    o[...] = (own[...] + two[...]) + (one[...] + three[...])


def write(sources, mine, target, tie):
    arrays = [a for a, _ in sources]
    rows = HALF // 4
    count = sum(len(steps) for _, steps in sources)

    def kernel(*refs):
        o_ref, left = refs[-2:]
        at = lax.axis_index("gx")
        half = at % 2 if mine else 1 - at % 2
        me = first_place(half)
        for act in ("start", "wait"):
            sem = 0
            for ref, (_, steps) in zip(refs, sources, strict=False):
                for at, step in enumerate(steps):
                    chunk = half * 4 + (me ^ step)

                    place = o_ref.at[pl.ds(chunk * rows, rows)]
                    copy = pltpu.make_async_copy(ref.at[pl.ds(at * rows, rows)], place, left.at[sem])
                    if act == "start":
                        copy.start()
                    else:
                        copy.wait()
                    sem += 1

    operands = arrays + [tie] + ([] if target is None else [target])
    return pl.pallas_call(
        kernel,
        in_specs=[VMEM] * len(arrays) + [ANY] * (len(operands) - len(arrays)),
        out_specs=ANY,
        out_shape=shape((27 * C, C), F32),
        scratch_shapes=[pltpu.SemaphoreType.DMA((count,))],
        input_output_aliases={} if target is None else {len(operands) - 1: 0},
        compiler_params=params(),
        cost_estimate=pl.CostEstimate(flops=1000, bytes_accessed=1 << 20, transcendentals=0),
    )(*operands)


def join_kernel(a, b, c, o):
    rows = a.shape[0]
    for k, ref in enumerate((a, b, c)):
        o[k * rows : (k + 1) * rows] = ref[...]


def shift(value, axis, step):
    count = lax.axis_size(axis)
    return lax.ppermute(value, axis, [(i, (i + step) % count) for i in range(count)])


def body(features, occupancy, weight, cotangent):
    slabs, mask, faces = prepare(occupancy, features, cotangent)
    zlo, zhi, ylo, yhi = faces
    near_zlo = shift(zhi, "gz", 1)
    near_zhi = shift(zlo, "gz", -1)
    own = own_grad(slabs, 0, 1, None, zlo)
    face = shape((2, X, Z, C), BF16)
    to_ylo, to_yhi = small_kernel(copy_kernel, [face, face], [ylo, yhi], [own])
    near_ylo = shift(to_yhi, "gy", 1)
    near_yhi = shift(to_ylo, "gy", -1)
    forward, flipped = small_kernel(
        arrange_kernel, [shape((TAPS, WIDE), BF16)] * 2, [weight.reshape(27, C, C)], [to_ylo]
    )

    edge = shape((2, 2, X, C), BF16)
    edge_lo, edge_hi = small_kernel(edge_kernel, [edge, edge], [near_zlo, near_zhi], [forward])
    edges = (shift(edge_hi, "gy", 1), shift(edge_lo, "gy", -1))
    own = own_grad(slabs, SPAN, 1, own, edge_lo)
    own = small_kernel(
        z_rim_kernel, shape((WIDE, TAPS), F32), [own, zlo, zhi, near_zlo, near_zhi], [edge_lo]
    )

    column = shape((2, X, 24, C), BF16)
    message = shape((2, Y + 5, Z, C), BF16)
    held_ylo, held_yhi, col_lo, col_hi, to_lo, to_hi = small_kernel(
        message_kernel,
        [face, face, column, column, message, message],
        [*slabs, near_ylo, near_yhi, near_zlo, near_zhi, *edges],
        [own],
    )
    far = (shift(to_hi, "gx", 1), shift(to_lo, "gx", -1))
    own = own_grad(slabs, X // 2, 2, own, to_lo)
    keep, send = rim_grad(own, slabs[1], [ylo, yhi, held_ylo, held_yhi, *edges, *far])

    field = [*slabs, held_ylo, held_yhi, col_lo, col_hi]
    made = [None, None]
    weights = (forward, flipped)
    order = [(0, 0, 1), (0, 4, 4), (0, 20, 3), (1, 0, 4), (1, 16, 4)]
    state = {}

    def convolve(tie):
        part, first, groups = order.pop(0)
        following = order[0][:2] if order else None
        made[part], kept = conv_piece(
            part, first, groups, following, mask, field, far, weights[part], state, made[part], tie
        )
        state.update(kept)
        return [kept["carry"]]

    swap = [(i, i ^ 1) for i in range(8)]
    came = lax.ppermute(send, "gx", swap)
    ties = convolve(send)
    own, *parts = deal([keep, came], ties)
    one, three, two = exchange(0, parts)
    ties = convolve(parts[0])
    chunk = small_kernel(scatter_sum_kernel, shape(own.shape, F32), [own, one, two, three], ties)
    for turn in (1, 2):
        if turn == 2:
            chunk = small_kernel(sum_kernel, shape(chunk.shape, F32), [chunk, *came], ties)
        came = exchange(turn, [chunk] * 3)
        ties = convolve(chunk)
    chunk = small_kernel(sum_kernel, shape(chunk.shape, F32), [chunk, *came], ties)
    came = exchange(0, [chunk] * 3)
    beside = lax.ppermute(chunk, "gx", swap)
    ties = convolve(chunk)
    joined = small_kernel(join_kernel, shape((3 * chunk.shape[0], C), F32), came, [beside, *ties])
    others = lax.ppermute(joined, "gx", swap)
    full = write([(chunk, (0,)), (joined, (1, 3, 2))], True, None, joined)
    full = write([(beside, (0,)), (others, (1, 3, 2))], False, full, joined)
    return (made[0], made[1], full.reshape(3, 3, 3, C, C))


def solution(mesh):
    placed = (P("gx", "gy", "gz", None), P("gx", "gy", "gz"), P(), P("gx", "gy", "gz", None))
    return jax.shard_map(
        body,
        mesh=mesh,
        in_specs=placed,
        out_specs=(P("gx", "gy", "gz", None), P("gx", "gy", "gz", None), P()),
        check_vma=False,
    )
```
